32 devices in a mesh: groups: 2 (over x), expert: 8 (over z, y), context: 2 (over core).
Axes of the slice: x: 2, y: 2, z: 4, core: 2. Of those that a mesh axis runs over, the one named last changes fastest.
Arguments:
- query_heads: bfloat16 [16, 256, 2048], P(('groups', 'expert'), 'context'), parts along dimension 0, may hold values from -4.5 to 4.5
- key_heads: bfloat16 [16, 256, 2048], P(('groups', 'expert'), 'context'), parts along dimension 0, may hold values from -4.5 to 4.5
- value_heads: bfloat16 [16, 256, 2048], P(('groups', 'expert'), 'context'), parts along dimension 0, may hold values from -6 to 6
- latent: bfloat16 [16, 256, 1024], P(('groups', 'expert'), 'context'), parts along dimension 0, may hold values from -6 to 6
- router: bfloat16 [1024, 16], replicated, may hold values from -0.1875 to 0.1875
- expert_in: bfloat16 [16, 1024, 2048], P(('expert', 'context')), may hold values from -0.1875 to 0.1875
- expert_out: bfloat16 [16, 2048, 1024], P(('expert', 'context')), may hold values from -0.125 to 0.125
- routes: int32 [16, 256, 6], P(('groups', 'expert'), 'context'), parts along dimension 0, may hold values from 0 to 15, all different within a row; in each aligned block of 128 rows (0 to 127, 128 to 255, ..., all dimensions but the last counted through in order) at most 96 rows name the same one
- segments: int32 [16, 256], P(('groups', 'expert'), 'context'), parts along dimension 0, may hold values from 0 to 3, never falling along the last dimension, each value on 1 to 128 neighbouring positions
- offsets: int32 [16, 256], P(('groups', 'expert'), 'context'), parts along dimension 0, may hold values from 0 to 3
- capacity: int32 [16], replicated, may hold values from 512 to 1024, as said below
Outputs:
- attn_out: bfloat16 [16, 256, 2048], P(('groups', 'expert'), 'context'), parts along dimension 0
- moe_out: bfloat16 [16, 256, 1024], P(('groups', 'expert'), 'context'), parts along dimension 0
The draws below stay inside these ranges and needn't reach their ends.
There are 2 independent parts, one for each index of `groups`. The reference program is written for one: setup_inputs(seed, part) draws one part's arguments, and reference() takes and returns one part's arrays. A program takes and returns all parts, laid end to end along the dimension named above; an argument that names none is the same for every part. Nothing has to cross between parts.
Inputs may be any that keep to these rules, and one draw needn't show every extreme that they name: `routes`: each row names 6 different experts; among the rows of one device (aligned blocks of 128 tokens) no expert is named more than 96 times, a bound that some block reaches. Some expert's capacity is exactly 1024. `segments`: document numbers never fall along a window; each document spans 1 to 128 positions, one exactly that many.
All inputs are finite; a program needn't handle non-finite values.
Results may differ from the reference program's by a relative error of at most 0.008.
Values may be sent and summed in bfloat16 or wider, within the bound.
No kernel may reach another device: no remote copies, remote signals or barrier semaphores. Data moves between devices by JAX's collectives and lax.ppermute only.
A program may use at most 128 MiB of HBM per device.

```python
import math
import jax
import jax.numpy as jnp
import numpy as np
from jax import lax

HEADS = 16
HEAD_DIM = 128
LATENT = 1024
FFE = 2048
TOPK = 6
SEGS = 4
TOK_DEV = 128
SEQ = 256
SEQS = 8
EXPERTS = 16
CAPS = 96
CAPMAX = 1024


def draw_query_heads(key, part):
    key = jax.random.fold_in(key, 7)
    shape = (SEQS, SEQ, HEADS * HEAD_DIM)
    base = jnp.clip(jax.random.normal(key, shape, jnp.float32), -4.5, 4.5)
    return base.astype(jnp.bfloat16)


def draw_key_heads(key, part):
    key = jax.random.fold_in(key, 8)
    shape = (SEQS, SEQ, HEADS * HEAD_DIM)
    base = jnp.clip(jax.random.normal(key, shape, jnp.float32), -4.5, 4.5)
    return base.astype(jnp.bfloat16)


def draw_capacity(key, part):
    key = jax.random.fold_in(key, 9)
    first_key, second_key = jax.random.split(key)
    amounts = jax.random.randint(first_key, (EXPERTS,), CAPMAX // 2, CAPMAX + 1)
    fullest = jax.random.randint(second_key, (), 0, EXPERTS)
    return amounts.at[fullest].set(CAPMAX).astype(jnp.int32)


def with_ends(values, key, smallest, largest):
    longest = values.shape.index(max(values.shape))
    spots = []
    for shift in (0, 1):
        where = [jax.random.randint(jax.random.fold_in(key, axis), (), 0, length) for axis, length in enumerate(values.shape)]
        where[longest] = (where[longest] + shift) % values.shape[longest]
        spots.append(tuple(where))
    return values.at[spots[0]].set(smallest).at[spots[1]].set(largest)


def block_scale(own_key, extent, shards, low, high):
    gain, own = 1.0, jax.random.fold_in(own_key, 6)
    for position, blocks in shards:
        heights = jnp.exp(jax.random.uniform(jax.random.fold_in(own, position), (blocks,), jnp.float32, low / len(shards), high / len(shards)))
        gain = gain * jnp.repeat(heights, extent[position] // blocks).reshape([-1 if axis == position else 1 for axis in range(len(extent))])
    return gain


def length_profile(number_of, total, limit, lean):
    portions = [(1 << 20) // math.isqrt(standing ** lean) + 1 for standing in range(2, number_of + 1)]
    rest, holding = total - limit - (number_of - 1), [1] * (number_of - 1)
    while rest > 0:
        free = [i for i in range(number_of - 1) if holding[i] < limit]
        mass, remaining = sum([portions[i] for i in free]), rest
        for i in free:
            more = min(limit - holding[i], max(1, remaining * portions[i] // mass), rest)
            holding[i] = holding[i] + more
            rest = rest - more
    return np.array([limit] + holding)


def uneven_parts(own_key, number_of, total, limit, skew):
    if number_of == 2:
        one = jax.random.randint(own_key, (), max(1, total - limit), min(limit, total - 1) + 1)
        return jnp.stack([one, total - one])
    tallies = jnp.asarray(length_profile(number_of, total, limit, skew), jnp.int32)
    twos = (number_of - 1) // 2
    giver, receiver = tallies[1:1 + 2 * twos:2], tallies[2:2 + 2 * twos:2]
    margin = jnp.minimum(giver - 1, limit - receiver)
    passed = jax.random.randint(jax.random.fold_in(own_key, 1), (twos,), 0, 1 << 20) % (margin + 1)
    tallies = tallies.at[1:1 + 2 * twos:2].set(giver - passed).at[2:2 + 2 * twos:2].set(receiver + passed)
    return tallies[jax.random.permutation(jax.random.fold_in(own_key, 2), number_of)]


def routed_block(key, own, number, rows, count, top, bound, skew):
    sequence = jax.random.permutation(key, count)
    heavy_load, usual = load_shares(count, rows * top, bound, skew, True), load_shares(count, rows * top, bound, skew, False)
    places = jnp.arange(count)

    def named(lengths, turn):
        used = int((lengths > 0).sum())
        fixed = max(1, used // 4)
        passed = fixed + (places - fixed + turn * (used - fixed)) % max(1, count - fixed)
        return jnp.zeros((count,), jnp.int32).at[sequence[jnp.where(places < fixed, places, passed)]].set(jnp.asarray(lengths, jnp.int32))

    lengths = jnp.where(number % 4 == 0, named(heavy_load, number // 4), named(usual, number - number // 4 - 1))
    mixed = jax.random.permutation(jax.random.fold_in(own, 3), count)
    donor, taker = mixed[0:count // 2 * 2:2], mixed[1:count // 2 * 2:2]
    margin = jnp.minimum(lengths[donor] - 1, bound - lengths[taker]) // 2
    margin = jnp.where((donor == sequence[0]) | (taker == sequence[0]) | (lengths[taker] == 0), 0, jnp.maximum(margin, 0))
    passed = jax.random.randint(jax.random.fold_in(own, 4), (count // 2,), 0, 1 << 20) % (margin + 1)
    lengths = lengths.at[donor].add(-passed).at[taker].add(passed)
    members = jnp.searchsorted(jnp.cumsum(lengths), jnp.arange(rows * top), side="right").astype(jnp.int32)
    table = members.reshape(top, rows).T
    table = table[jax.random.permutation(jax.random.fold_in(own, 1), rows)]
    turn = jax.random.randint(jax.random.fold_in(own, 2), (rows, 1), 0, top)
    return jnp.take_along_axis(table, (jnp.arange(top)[None, :] + turn) % top, axis=1)


def load_shares(amount, total, most, slope, full):
    loads = [(1 << 20) // math.isqrt(standing ** slope) + 1 for standing in range(1, amount + 1)]
    largest = most if full else min(most, max(-(-total // amount), total * loads[0] // sum(loads)))
    least = 1 if total - largest >= amount - 1 else 0
    given, surplus = [largest] + [least] * (amount - 1), total - largest - least * (amount - 1)
    while surplus > 0:
        candidates = [i for i in range(1, amount) if given[i] < largest] or [i for i in range(1, amount) if given[i] < most]
        whole, remaining = sum([loads[i] for i in candidates]), surplus
        for i in candidates:
            more = min(most - given[i], max(1, remaining * loads[i] // whole), surplus)
            given[i] = given[i] + more
            surplus = surplus - more
    return np.array(given)


def bell_draw(stream_key, shape, scale, bound, pieces=(), kind=jnp.bfloat16):
    loudness = block_scale(stream_key, shape, pieces, -0.22, 0.18) if pieces else 1.0
    result = jax.random.normal(stream_key, shape, jnp.float32) * scale * loudness
    return jnp.minimum(jnp.maximum(result, -bound), bound).astype(kind)


def setup_inputs(seed: int = 0, part: int = 0) -> dict:
    key_of = jax.random.split(jax.random.key(seed), 12)
    part_splits = jax.random.split(jax.random.fold_in(key_of[11], part), 12)
    query_heads = draw_query_heads(jax.random.fold_in(jax.random.fold_in(key_of[11], part), 71), part)
    key_heads = draw_key_heads(jax.random.fold_in(jax.random.fold_in(key_of[11], part), 71), part)
    value_heads = bell_draw(part_splits[2], (SEQS, SEQ, HEADS * HEAD_DIM), 1.0, 6.0, ((0, 8), (1, 2)))
    latent = bell_draw(part_splits[3], (SEQS, SEQ, LATENT), 1.0, 6.0, ((0, 8), (1, 2)))
    router = bell_draw(key_of[4], (LATENT, EXPERTS), LATENT ** -0.5, 0.1875)
    expert_in = bell_draw(key_of[5], (EXPERTS, LATENT, FFE), LATENT ** -0.5, 0.1875, ((0, 16),))
    expert_out = bell_draw(key_of[6], (EXPERTS, FFE, LATENT), FFE ** -0.5, 0.125, ((0, 16),))
    routes_keys = jax.random.split(jax.random.fold_in(part_splits[7], 1), SEQS * SEQ // TOK_DEV)
    routes_turns = jax.random.permutation(jax.random.fold_in(part_splits[7], 3), SEQS * SEQ // TOK_DEV)
    routes = jax.vmap(lambda own, number: routed_block(jax.random.fold_in(part_splits[7], 2), own, number, TOK_DEV, EXPERTS, TOPK, CAPS, 2))(routes_keys, routes_turns).reshape((SEQS, SEQ, TOPK))
    segments = jax.vmap(lambda own: jnp.searchsorted(jnp.cumsum(uneven_parts(own, SEGS, SEQ, SEQ // 2, 2)), jnp.arange(SEQ), side="right"))(jax.random.split(part_splits[8], SEQS)).reshape((SEQS, SEQ)).astype(jnp.int32)
    offsets = with_ends(jax.random.randint(part_splits[9], (SEQS, SEQ), 0, 4), jax.random.fold_in(part_splits[9], 1), 0, 3).astype(jnp.int32)
    capacity = draw_capacity(jax.random.fold_in(key_of[11], 71), part)
    return dict(query_heads=query_heads, key_heads=key_heads, value_heads=value_heads, latent=latent, router=router, expert_in=expert_in, expert_out=expert_out, routes=routes, segments=segments, offsets=offsets, capacity=capacity)


def attend(window):
    queries, keys_in, values_in, doc_ids, look_ahead = window
    length = queries.shape[0]
    q_rows = queries.reshape(length, HEADS, HEAD_DIM).astype(jnp.float32)
    k_rows = keys_in.reshape(length, HEADS, HEAD_DIM).astype(jnp.float32)
    v_rows = values_in.reshape(length, HEADS, HEAD_DIM).astype(jnp.float32)
    scores = jnp.einsum("qhd,khd->hqk", q_rows, k_rows) * (HEAD_DIM ** -0.5)
    positions = jnp.arange(length, dtype=jnp.int32)
    visible = (doc_ids[None, :] == doc_ids[:, None]) & (positions[None, :] <= positions[:, None] + look_ahead[:, None])
    scores = jnp.where(visible[None, :, :], scores, -1e30)
    row_max = jnp.max(scores, axis=-1, keepdims=True)
    raw_weights = jnp.exp(scores - row_max)
    weights = (raw_weights / jnp.sum(raw_weights, axis=-1, keepdims=True)).astype(jnp.bfloat16)
    mixed_rows = jnp.einsum("hqk,khd->qhd", weights.astype(jnp.float32), v_rows)
    return mixed_rows.reshape(length, HEADS * HEAD_DIM).astype(jnp.bfloat16)


def expert_apply(operands):
    rows_in, w_first, w_second = operands
    hidden = jax.nn.relu(jnp.dot(rows_in, w_first, preferred_element_type=jnp.float32))
    hidden = (hidden * hidden).astype(jnp.bfloat16)
    return jnp.dot(hidden, w_second, preferred_element_type=jnp.float32).astype(jnp.bfloat16)


def reference(query_heads, key_heads, value_heads, latent, router, expert_in, expert_out, routes, segments, offsets, capacity):
    attn_out = lax.map(attend, (query_heads, key_heads, value_heads, segments, offsets))
    tokens = latent.reshape(SEQS * SEQ, LATENT)
    token_count = SEQS * SEQ
    logits = jnp.dot(tokens, router, preferred_element_type=jnp.float32)
    chosen_ids = routes.reshape(token_count, TOPK).astype(jnp.int32)
    picked = jnp.take_along_axis(logits, chosen_ids, axis=1)
    sigmas = jax.nn.sigmoid(picked)
    gates = sigmas / jnp.sum(sigmas, axis=1, keepdims=True)
    flat_ids = chosen_ids.reshape(-1)
    one_hot = (flat_ids[:, None] == jnp.arange(EXPERTS, dtype=jnp.int32)[None, :]).astype(jnp.int32)
    earlier = jnp.cumsum(one_hot, axis=0) - one_hot
    slots = jnp.sum(earlier * one_hot, axis=1).astype(jnp.int32)
    kept = slots < capacity[flat_ids]
    places = jnp.where(kept, flat_ids * CAPMAX + slots, EXPERTS * CAPMAX).astype(jnp.int32)
    owners = (jnp.arange(token_count * TOPK, dtype=jnp.int32) // TOPK).astype(jnp.int32)
    buffer_rows = jnp.zeros((EXPERTS * CAPMAX, LATENT), jnp.bfloat16).at[places].set(tokens[owners], mode="drop")
    results = lax.map(expert_apply, (buffer_rows.reshape(EXPERTS, CAPMAX, LATENT), expert_in, expert_out))
    results = results.reshape(EXPERTS * CAPMAX, LATENT)
    safe_places = jnp.minimum(places, EXPERTS * CAPMAX - 1).reshape(token_count, TOPK)
    gate_kept = jnp.where(kept.reshape(token_count, TOPK), gates, jnp.zeros_like(gates))
    total = jnp.zeros((token_count, LATENT), jnp.float32)
    for which in range(TOPK):
        total = total + gate_kept[:, which][:, None] * results[safe_places[:, which]].astype(jnp.float32)
    moe_out = total.astype(jnp.bfloat16).reshape(SEQS, SEQ, LATENT)
    return attn_out, moe_out
```

```python
import functools

import jax
import jax.numpy as jnp
from jax import lax
from jax.experimental import pallas as pl
from jax.experimental.pallas import tpu as pltpu
from jax.sharding import PartitionSpec as P

HEAD_DIM = 128
LATENT = 1024
TOPK = 6
DENSE_EXPERTS = 16
VMEM_LIMIT = 56 * 1024 * 1024


def run_expert(rows_in, w_first, w_second):
    hidden = jax.nn.relu(jnp.dot(rows_in, w_first, preferred_element_type=jnp.float32))
    hidden = (hidden * hidden).astype(jnp.bfloat16)
    return jnp.dot(hidden, w_second, preferred_element_type=jnp.float32).astype(jnp.bfloat16)


def column_of(row):
    n = row.shape[1]
    square = jnp.broadcast_to(row.astype(jnp.float32), (n, n)).T
    return square[:, :1].astype(jnp.int32)


def attend_kernel(
    place_ref, q_ref, k_own, k_far, v_own, v_far, doc_own, doc_far, ahead_ref, out_ref
):
    rows = q_ref.shape[0]
    heads = q_ref.shape[1] // HEAD_DIM
    here = place_ref[0] * rows
    there = (1 - place_ref[0]) * rows
    doc_query = column_of(doc_own[...])
    reach = here + lax.broadcasted_iota(jnp.int32, (rows, 1), 0) + column_of(ahead_ref[...])
    lane = lax.broadcasted_iota(jnp.int32, (1, rows), 1)
    see_own = (doc_own[...] == doc_query) & (here + lane <= reach)
    see_far = (doc_far[...] == doc_query) & (there + lane <= reach)
    scale = HEAD_DIM ** (-0.5)
    across = (((1,), (1,)), ((), ()))
    for head in range(heads):
        cols = slice(head * HEAD_DIM, (head + 1) * HEAD_DIM)
        q = q_ref[:, cols]
        near = lax.dot_general(q, k_own[:, cols], across, preferred_element_type=jnp.float32)
        far = lax.dot_general(q, k_far[:, cols], across, preferred_element_type=jnp.float32)
        near = jnp.where(see_own, near * scale, -1e30)
        far = jnp.where(see_far, far * scale, -1e30)
        top = jnp.max(jnp.maximum(near, far), axis=1, keepdims=True)
        near = jnp.exp(near - top)
        far = jnp.exp(far - top)
        share = 1.0 / jnp.sum(near + far, axis=1, keepdims=True)
        near = (near * share).astype(jnp.bfloat16)
        far = (far * share).astype(jnp.bfloat16)
        mixed = jnp.dot(near, v_own[:, cols], preferred_element_type=jnp.float32)
        mixed += jnp.dot(far, v_far[:, cols], preferred_element_type=jnp.float32)
        out_ref[:, cols] = mixed.astype(jnp.bfloat16)


def attend(place, q, k_own, k_far, v_own, v_far, doc_own, doc_far, ahead):
    vmem = pl.BlockSpec(memory_space=pltpu.VMEM)
    return pl.pallas_call(
        attend_kernel,
        out_shape=jax.ShapeDtypeStruct(q.shape, jnp.bfloat16),
        in_specs=[pl.BlockSpec(memory_space=pltpu.SMEM)] + [vmem] * 8,
        out_specs=vmem,
        compiler_params=pltpu.CompilerParams(vmem_limit_bytes=VMEM_LIMIT),
        cost_estimate=pl.CostEstimate(
            flops=4 * q.shape[0] * 2 * q.shape[0] * q.shape[1],
            bytes_accessed=6 * q.size * 2,
            transcendentals=2 * q.shape[0] * q.size // HEAD_DIM,
        ),
    )(place, q, k_own, k_far, v_own, v_far, doc_own, doc_far, ahead)


def gate_kernel(latent_ref, router_ref, routes_ref, out_ref):
    logits = jnp.dot(latent_ref[...], router_ref[...], preferred_element_type=jnp.float32)
    rows, experts = logits.shape
    lane = lax.broadcasted_iota(jnp.int32, (rows, experts), 1)
    named = lane == routes_ref[:, 0:1]
    for k in range(1, TOPK):
        named |= lane == routes_ref[:, k : k + 1]
    sigma = jnp.where(named, jax.nn.sigmoid(logits), 0.0)
    gates = sigma / jnp.sum(sigma, axis=1, keepdims=True)
    out_ref[...] = jnp.where(named, gates, -1.0).T


def gate_table(latent, router, routes):
    vmem = pl.BlockSpec(memory_space=pltpu.VMEM)
    return pl.pallas_call(
        gate_kernel,
        out_shape=jax.ShapeDtypeStruct((router.shape[1], latent.shape[0]), jnp.float32),
        in_specs=[vmem] * 3,
        out_specs=vmem,
    )(latent, router, routes)


def kept_gates(table, limit):
    sources, rows = table.shape
    named = table != -1.0
    flags = jnp.where(named, 1.0, 0.0)
    upto = lax.broadcasted_iota(jnp.int32, (rows, rows), 0) <= lax.broadcasted_iota(
        jnp.int32, (rows, rows), 1
    )
    running = jnp.dot(
        flags.astype(jnp.bfloat16),
        jnp.where(upto, 1.0, 0.0).astype(jnp.bfloat16),
        preferred_element_type=jnp.float32,
    )
    earlier = lax.broadcasted_iota(jnp.int32, (sources, sources), 1) < lax.broadcasted_iota(
        jnp.int32, (sources, sources), 0
    )
    totals = jnp.broadcast_to(running[:, rows - 1 :], (sources, rows))
    before = jnp.dot(
        jnp.where(earlier, 1.0, 0.0).astype(jnp.bfloat16),
        totals.astype(jnp.bfloat16),
        preferred_element_type=jnp.float32,
    )
    slots = before + running - flags
    return jnp.where(named & (slots < limit), table, 0.0).T


def expert_kernel(tile, own_ref, capacity_ref, table_ref, x_ref, w1_ref, w2_ref, out_ref, gates):
    step = pl.program_id(0)

    @pl.when(step == 0)
    def _():
        own = own_ref[0]
        limit = capacity_ref[own].astype(jnp.float32)
        gates[...] = kept_gates(table_ref[:, own, :], limit)

    rows = gates.shape[0]
    hidden = jnp.maximum(
        jnp.dot(x_ref[...], w1_ref[...], preferred_element_type=jnp.float32), 0.0
    )
    hidden = (hidden * hidden).astype(jnp.bfloat16)
    result = jnp.dot(hidden, w2_ref[...], preferred_element_type=jnp.float32)
    result = result.astype(jnp.bfloat16).astype(jnp.float32)
    lane = lax.broadcasted_iota(jnp.int32, gates.shape, 1)
    for part in range(tile // rows):
        source = step * (tile // rows) + part
        gate = jnp.sum(jnp.where(lane == source, gates[...], 0.0), axis=1, keepdims=True)
        place = slice(part * rows, (part + 1) * rows)
        out_ref[place, :] = (result[place, :] * gate).astype(jnp.bfloat16)


def expert_all(own, capacity, table, x, w_first, w_second):
    tile = 256
    total, width = x.shape
    sources, _, rows = table.shape
    smem = pl.BlockSpec(memory_space=pltpu.SMEM)

    def whole(shape):
        return pl.BlockSpec(shape, lambda i: (0,) * len(shape), pipeline_mode=pl.Buffered(1))

    return pl.pallas_call(
        functools.partial(expert_kernel, tile),
        grid=(total // tile,),
        out_shape=jax.ShapeDtypeStruct((total, width), jnp.bfloat16),
        in_specs=[
            smem,
            smem,
            whole(table.shape),
            pl.BlockSpec((tile, width), lambda i: (i, 0)),
            whole(w_first.shape),
            whole(w_second.shape),
        ],
        out_specs=pl.BlockSpec((tile, width), lambda i: (i, 0)),
        scratch_shapes=[pltpu.VMEM((rows, sources), jnp.float32)],
        compiler_params=pltpu.CompilerParams(vmem_limit_bytes=VMEM_LIMIT),
        cost_estimate=pl.CostEstimate(
            flops=4 * total * w_first.size,
            bytes_accessed=4 * total * width + 4 * w_first.size,
            transcendentals=0,
        ),
    )(own, capacity, table, x, w_first, w_second)


def dense_moe(latent, router, expert_in, expert_out, routes, capacity):
    axes = ("expert", "context")
    gates = gate_table(latent[0], router, routes[0])
    table = lax.all_gather(gates, axes, axis=0, tiled=False)
    everyone = lax.all_gather(latent[0], axes, axis=0, tiled=True)
    own = lax.axis_index(axes).astype(jnp.int32).reshape(1)
    partial = expert_all(own, capacity, table, everyone, expert_in[0], expert_out[0])
    return lax.psum_scatter(partial, axes, scatter_dimension=0, tiled=True)[None]


def routed_moe(latent, router, expert_in, expert_out, routes, capacity):
    tok_count = latent.shape[1]
    token_rows = latent[0]
    expert_count = router.shape[1]
    per_peer = max(2, 2 * tok_count * TOPK // expert_count)
    logits = jnp.dot(token_rows, router, preferred_element_type=jnp.float32)
    chosen_ids = routes[0]
    expert_ids = jnp.arange(expert_count, dtype=jnp.int32)
    one_hot = chosen_ids[:, :, None] == expert_ids[None, None, :]
    picked = jnp.sum(jnp.where(one_hot, logits[:, None, :], 0.0), axis=2)
    sigmas = jax.nn.sigmoid(picked)
    gates = sigmas / jnp.sum(sigmas, axis=1, keepdims=True)
    flat_hot = one_hot.reshape(tok_count * TOPK, expert_count).astype(jnp.int32)
    counts = jnp.sum(flat_hot, axis=0)
    ranks = jnp.sum((jnp.cumsum(flat_hot, axis=0) - flat_hot) * flat_hot, axis=1)
    count_rows = lax.all_gather(counts[None, :], ("expert", "context"), axis=0, tiled=True)
    own_index = lax.axis_index(("expert", "context"))
    lower_rows = jnp.arange(count_rows.shape[0], dtype=jnp.int32)[:, None] < own_index
    before = jnp.sum(jnp.where(lower_rows, count_rows, 0), axis=0)
    slots = jnp.sum(flat_hot * before[None, :], axis=1) + ranks
    limits = jnp.sum(flat_hot * capacity[None, :], axis=1)
    kept = slots < limits
    flat_ids = chosen_ids.reshape(-1)
    places = flat_ids * per_peer + ranks
    owners = jnp.arange(tok_count * TOPK, dtype=jnp.int32) // TOPK
    send_rows = (
        jnp.zeros((expert_count * per_peer, LATENT), jnp.bfloat16)
        .at[places]
        .set(token_rows[owners])
    )
    recv_rows = lax.all_to_all(
        send_rows.reshape(expert_count, per_peer, LATENT),
        ("expert", "context"),
        split_axis=0,
        concat_axis=0,
        tiled=True,
    ).reshape(expert_count * per_peer, LATENT)
    results = run_expert(recv_rows, expert_in[0], expert_out[0])
    returned = lax.all_to_all(
        results.reshape(expert_count, per_peer, LATENT),
        ("expert", "context"),
        split_axis=0,
        concat_axis=0,
        tiled=True,
    ).reshape(expert_count * per_peer, LATENT)
    gate_kept = jnp.where(kept, gates.reshape(-1), 0.0).reshape(tok_count, TOPK)
    back_rows = returned[places].reshape(tok_count, TOPK, LATENT).astype(jnp.float32)
    mixture = jnp.sum(gate_kept[:, :, None] * back_rows, axis=1)
    return mixture.astype(jnp.bfloat16).reshape(1, tok_count, LATENT)


def shards(
    query_heads,
    key_heads,
    value_heads,
    latent,
    router,
    expert_in,
    expert_out,
    routes,
    segments,
    offsets,
    capacity,
):
    swap = [(0, 1), (1, 0)]
    k_far = lax.ppermute(key_heads[0], "context", swap)
    v_far = lax.ppermute(value_heads[0], "context", swap)
    doc_far = lax.ppermute(segments, "context", swap)
    place = lax.axis_index("context").astype(jnp.int32).reshape(1)
    attn_out = attend(
        place, query_heads[0], key_heads[0], k_far, value_heads[0], v_far, segments, doc_far, offsets
    )[None]
    moe = dense_moe if router.shape[1] <= DENSE_EXPERTS else routed_moe
    moe_out = moe(latent, router, expert_in, expert_out, routes, capacity)
    return (attn_out, moe_out)


def solution(mesh):
    rows = P(("groups", "expert"), "context", None)
    placed = (
        rows,
        rows,
        rows,
        rows,
        P(),
        P(("expert", "context"), None, None),
        P(("expert", "context"), None, None),
        rows,
        P(("groups", "expert"), "context"),
        P(("groups", "expert"), "context"),
        P(),
    )
    return jax.shard_map(
        shards,
        mesh=mesh,
        in_specs=placed,
        out_specs=(rows, rows),
        check_vma=False,
    )
```

```python
import functools

import jax
import jax.numpy as jnp
from jax import lax
from jax.experimental import pallas as pl
from jax.experimental.pallas import tpu as pltpu
from jax.sharding import PartitionSpec as P

HEAD_DIM = 128
LATENT = 1024
TOPK = 6
DENSE_EXPERTS = 16
VMEM_LIMIT = 56 * 1024 * 1024
EXPERT_VMEM = 28 * 1024 * 1024


def run_expert(rows_in, w_first, w_second):
    hidden = jax.nn.relu(jnp.dot(rows_in, w_first, preferred_element_type=jnp.float32))
    hidden = (hidden * hidden).astype(jnp.bfloat16)
    return jnp.dot(hidden, w_second, preferred_element_type=jnp.float32).astype(jnp.bfloat16)


def column_of(row):
    n = row.shape[1]
    square = jnp.broadcast_to(row.astype(jnp.float32), (n, n)).T
    return square[:, :1].astype(jnp.int32)


def attend_kernel(
    place_ref, q_ref, k_own, k_far, v_own, v_far, doc_own, doc_far, ahead_ref, out_ref
):
    rows = q_ref.shape[0]
    heads = q_ref.shape[1] // HEAD_DIM
    here = place_ref[0] * rows
    there = (1 - place_ref[0]) * rows
    doc_query = column_of(doc_own[...])
    reach = here + lax.broadcasted_iota(jnp.int32, (rows, 1), 0) + column_of(ahead_ref[...])
    lane = lax.broadcasted_iota(jnp.int32, (1, rows), 1)
    see_own = (doc_own[...] == doc_query) & (here + lane <= reach)
    see_far = (doc_far[...] == doc_query) & (there + lane <= reach)
    scale = HEAD_DIM ** (-0.5)
    across = (((1,), (1,)), ((), ()))
    for head in range(heads):
        cols = slice(head * HEAD_DIM, (head + 1) * HEAD_DIM)
        q = q_ref[:, cols]
        near = lax.dot_general(q, k_own[:, cols], across, preferred_element_type=jnp.float32)
        far = lax.dot_general(q, k_far[:, cols], across, preferred_element_type=jnp.float32)
        near = jnp.where(see_own, near * scale, -1e30)
        far = jnp.where(see_far, far * scale, -1e30)
        top = jnp.max(jnp.maximum(near, far), axis=1, keepdims=True)
        near = jnp.exp(near - top)
        far = jnp.exp(far - top)
        share = 1.0 / jnp.sum(near + far, axis=1, keepdims=True)
        near = (near * share).astype(jnp.bfloat16)
        far = (far * share).astype(jnp.bfloat16)
        mixed = jnp.dot(near, v_own[:, cols], preferred_element_type=jnp.float32)
        mixed += jnp.dot(far, v_far[:, cols], preferred_element_type=jnp.float32)
        out_ref[:, cols] = mixed.astype(jnp.bfloat16)


def attend(place, q, k_own, k_far, v_own, v_far, doc_own, doc_far, ahead):
    vmem = pl.BlockSpec(memory_space=pltpu.VMEM)
    return pl.pallas_call(
        attend_kernel,
        out_shape=jax.ShapeDtypeStruct(q.shape, jnp.bfloat16),
        in_specs=[pl.BlockSpec(memory_space=pltpu.SMEM)] + [vmem] * 8,
        out_specs=vmem,
        compiler_params=pltpu.CompilerParams(vmem_limit_bytes=VMEM_LIMIT),
        cost_estimate=pl.CostEstimate(
            flops=4 * q.shape[0] * 2 * q.shape[0] * q.shape[1],
            bytes_accessed=6 * q.size * 2,
            transcendentals=2 * q.shape[0] * q.size // HEAD_DIM,
        ),
    )(place, q, k_own, k_far, v_own, v_far, doc_own, doc_far, ahead)


def gate_kernel(latent_ref, router_ref, routes_ref, out_ref):
    logits = lax.dot_general(
        router_ref[...], latent_ref[...], (((1,), (1,)), ((), ())), preferred_element_type=jnp.float32
    )
    number = lax.broadcasted_iota(jnp.int32, logits.shape, 0)
    named = number == routes_ref[0]
    for k in range(1, TOPK):
        named |= number == routes_ref[k]
    sigma = jnp.where(named, jax.nn.sigmoid(logits), 0.0)
    gates = sigma / jnp.sum(sigma, axis=0, keepdims=True)
    out_ref[...] = jnp.where(named, gates, -1.0)


def gate_table(latent, router, routes):
    vmem = pl.BlockSpec(memory_space=pltpu.VMEM)
    return pl.pallas_call(
        gate_kernel,
        out_shape=jax.ShapeDtypeStruct((router.shape[1], latent.shape[0]), jnp.float32),
        in_specs=[vmem] * 3,
        out_specs=vmem,
    )(latent, router.T, routes.transpose(2, 0, 1))


def kept_kernel(own_ref, order_ref, capacity_ref, table_ref, out_ref):
    own = own_ref[0]
    table = table_ref[:, own, :]
    sources, rows = table.shape
    named = table != -1.0
    flags = jnp.where(named, 1.0, 0.0)
    upto = lax.broadcasted_iota(jnp.int32, (rows, rows), 0) <= lax.broadcasted_iota(
        jnp.int32, (rows, rows), 1
    )
    running = jnp.dot(
        flags.astype(jnp.bfloat16),
        jnp.where(upto, 1.0, 0.0).astype(jnp.bfloat16),
        preferred_element_type=jnp.float32,
    )
    device = lax.broadcasted_iota(jnp.int32, (sources, sources), 0) ^ own
    other = lax.broadcasted_iota(jnp.int32, (sources, sources), 1) ^ own
    totals = jnp.broadcast_to(running[:, rows - 1 :], (sources, rows))
    before = jnp.dot(
        jnp.where(other < device, 1.0, 0.0).astype(jnp.bfloat16),
        totals.astype(jnp.bfloat16),
        preferred_element_type=jnp.float32,
    )
    slots = before + running - flags
    limit = capacity_ref[own].astype(jnp.float32)
    kept = jnp.where(named & (slots < limit), table, 0.0)
    entry = lax.broadcasted_iota(jnp.int32, table.shape, 0)
    ordered = [
        jnp.sum(jnp.where(entry == order_ref[place], kept, 0.0), axis=0, keepdims=True)
        for place in range(sources)
    ]
    out_ref[...] = jnp.concatenate(ordered, axis=0).T


def kept_gates(own, order, capacity, table):
    smem = pl.BlockSpec(memory_space=pltpu.SMEM)
    vmem = pl.BlockSpec(memory_space=pltpu.VMEM)
    return pl.pallas_call(
        kept_kernel,
        out_shape=jax.ShapeDtypeStruct((table.shape[2], table.shape[0]), jnp.float32),
        in_specs=[smem, smem, smem, vmem],
        out_specs=vmem,
    )(own, order, capacity, table)


def expert_kernel(columns, gates_ref, *refs):
    count = len(columns)
    blocks, (w1_ref, w2_ref, keep_ref, give_ref, hidden_ref) = refs[:count], refs[count:]
    rows = blocks[0].shape[0]
    x = jnp.concatenate([block[...] for block in blocks], axis=0)
    step = 512
    for first in range(0, w1_ref.shape[1], step):
        cols = slice(first, first + step)
        hidden = jnp.maximum(jnp.dot(x, w1_ref[:, cols], preferred_element_type=jnp.float32), 0.0)
        hidden_ref[:, cols] = (hidden * hidden).astype(jnp.bfloat16)
    for first in range(0, w2_ref.shape[1], step):
        cols = slice(first, first + step)
        result = jnp.dot(hidden_ref[...], w2_ref[:, cols], preferred_element_type=jnp.float32)
        for index, column in enumerate(columns):
            gate = gates_ref[:, column : column + 1]
            part = result[index * rows : (index + 1) * rows]
            out = give_ref if index % 2 else keep_ref
            out[index // 2, :, cols] = (part * gate).astype(jnp.bfloat16)


def run_pieces(gates, pieces, w_first, w_second):
    columns, blocks = [], []
    for place, mine, theirs in pieces:
        columns += [2 * place, 2 * place + 1]
        blocks += [mine, theirs]
    rows, width = blocks[0].shape
    vmem = pl.BlockSpec(memory_space=pltpu.VMEM)
    half = jax.ShapeDtypeStruct((len(pieces), rows, width), jnp.bfloat16)
    return pl.pallas_call(
        functools.partial(expert_kernel, tuple(columns)),
        out_shape=(half, half),
        in_specs=[vmem] * (3 + len(blocks)),
        out_specs=(vmem, vmem),
        scratch_shapes=[pltpu.VMEM((rows * len(blocks), w_first.shape[1]), jnp.bfloat16)],
        compiler_params=pltpu.CompilerParams(vmem_limit_bytes=EXPERT_VMEM),
        cost_estimate=pl.CostEstimate(
            flops=4 * rows * len(blocks) * w_first.size,
            bytes_accessed=4 * rows * len(blocks) * width + 4 * w_first.size,
            transcendentals=0,
        ),
    )(gates, *blocks, w_first, w_second)


def dense_moe(latent, router, expert_in, expert_out, routes, capacity):
    f32 = jnp.float32
    line = router.shape[1] // 4
    spots = [(z, y) for z in range(line) for y in range(2)]
    sibling = [(0, 1), (1, 0)]
    across = [(2 * z + y, 2 * z + 1 - y) for z, y in spots]

    def toward(step):
        return [(2 * z + y, 2 * ((z + step) % line) + y) for z, y in spots]

    def swap_core(x):
        return lax.ppermute(x, "context", sibling)

    def swap_side(x):
        return lax.ppermute(x, "expert", across)

    def along(x, step):
        return lax.ppermute(x, "expert", toward(step))

    own = lax.axis_index(("expert", "context")).astype(jnp.int32)
    z = own // 4
    order = jnp.stack(
        [4 * (z ^ ((z - step) % line)) + rest for step in range(line) for rest in range(4)]
    )

    table = gate_table(latent[0], router, routes)[None]
    table = jnp.concatenate([table, swap_core(table)], axis=0)
    table = jnp.concatenate([table, swap_side(table)], axis=0)
    span = 1
    while span < line:
        flip = [(2 * z + y, 2 * (z ^ span) + y) for z, y in spots]
        table = jnp.concatenate([table, lax.ppermute(table, "expert", flip)], axis=0)
        span *= 2
    gates = kept_gates(own.reshape(1), order, capacity, table)

    chunk = latent[0]
    ahead, side = [], []
    for step in range(line):
        if step:
            chunk = along(chunk, 1)
        beside = swap_side(chunk)
        ahead.append((2 * step, chunk, swap_core(chunk)))
        side.append((2 * step + 1, beside, swap_core(beside)))

    total = None
    waiting = None
    for step in range(line + 1):
        pieces = ([side[step - 1]] if step else []) + ([ahead[step]] if step < line else [])
        keep, give = run_pieces(gates, pieces, expert_in[0], expert_out[0])
        got = swap_core(give)
        if step:
            crossing = (keep[0].astype(f32) + got[0].astype(f32)).astype(jnp.bfloat16)
            arrived = swap_side(crossing)
            column = waiting[0].astype(f32) + waiting[1].astype(f32) + arrived.astype(f32)
            if step == 1:
                total = column
            else:
                sent = along(column.astype(jnp.bfloat16), line - (step - 1))
                total = total + sent.astype(f32)
        waiting = (keep[-1], got[-1])
    return total.astype(jnp.bfloat16)[None]


def routed_moe(latent, router, expert_in, expert_out, routes, capacity):
    tok_count = latent.shape[1]
    token_rows = latent[0]
    expert_count = router.shape[1]
    per_peer = max(2, 2 * tok_count * TOPK // expert_count)
    logits = jnp.dot(token_rows, router, preferred_element_type=jnp.float32)
    chosen_ids = routes[0]
    expert_ids = jnp.arange(expert_count, dtype=jnp.int32)
    one_hot = chosen_ids[:, :, None] == expert_ids[None, None, :]
    picked = jnp.sum(jnp.where(one_hot, logits[:, None, :], 0.0), axis=2)
    sigmas = jax.nn.sigmoid(picked)
    gates = sigmas / jnp.sum(sigmas, axis=1, keepdims=True)
    flat_hot = one_hot.reshape(tok_count * TOPK, expert_count).astype(jnp.int32)
    counts = jnp.sum(flat_hot, axis=0)
    ranks = jnp.sum((jnp.cumsum(flat_hot, axis=0) - flat_hot) * flat_hot, axis=1)
    count_rows = lax.all_gather(counts[None, :], ("expert", "context"), axis=0, tiled=True)
    own_index = lax.axis_index(("expert", "context"))
    lower_rows = jnp.arange(count_rows.shape[0], dtype=jnp.int32)[:, None] < own_index
    before = jnp.sum(jnp.where(lower_rows, count_rows, 0), axis=0)
    slots = jnp.sum(flat_hot * before[None, :], axis=1) + ranks
    limits = jnp.sum(flat_hot * capacity[None, :], axis=1)
    kept = slots < limits
    flat_ids = chosen_ids.reshape(-1)
    places = flat_ids * per_peer + ranks
    owners = jnp.arange(tok_count * TOPK, dtype=jnp.int32) // TOPK
    send_rows = (
        jnp.zeros((expert_count * per_peer, LATENT), jnp.bfloat16)
        .at[places]
        .set(token_rows[owners])
    )
    recv_rows = lax.all_to_all(
        send_rows.reshape(expert_count, per_peer, LATENT),
        ("expert", "context"),
        split_axis=0,
        concat_axis=0,
        tiled=True,
    ).reshape(expert_count * per_peer, LATENT)
    results = run_expert(recv_rows, expert_in[0], expert_out[0])
    returned = lax.all_to_all(
        results.reshape(expert_count, per_peer, LATENT),
        ("expert", "context"),
        split_axis=0,
        concat_axis=0,
        tiled=True,
    ).reshape(expert_count * per_peer, LATENT)
    gate_kept = jnp.where(kept, gates.reshape(-1), 0.0).reshape(tok_count, TOPK)
    back_rows = returned[places].reshape(tok_count, TOPK, LATENT).astype(jnp.float32)
    mixture = jnp.sum(gate_kept[:, :, None] * back_rows, axis=1)
    return mixture.astype(jnp.bfloat16).reshape(1, tok_count, LATENT)


def shards(
    query_heads,
    key_heads,
    value_heads,
    latent,
    router,
    expert_in,
    expert_out,
    routes,
    segments,
    offsets,
    capacity,
):
    swap = [(0, 1), (1, 0)]
    k_far = lax.ppermute(key_heads[0], "context", swap)
    v_far = lax.ppermute(value_heads[0], "context", swap)
    doc_far = lax.ppermute(segments, "context", swap)
    place = lax.axis_index("context").astype(jnp.int32).reshape(1)
    attn_out = attend(
        place, query_heads[0], key_heads[0], k_far, value_heads[0], v_far, segments, doc_far, offsets
    )[None]
    moe = dense_moe if router.shape[1] <= DENSE_EXPERTS else routed_moe
    moe_out = moe(latent, router, expert_in, expert_out, routes, capacity)
    return (attn_out, moe_out)


def solution(mesh):
    rows = P(("groups", "expert"), "context", None)
    placed = (
        rows,
        rows,
        rows,
        rows,
        P(),
        P(("expert", "context"), None, None),
        P(("expert", "context"), None, None),
        rows,
        P(("groups", "expert"), "context"),
        P(("groups", "expert"), "context"),
        P(),
    )
    return jax.shard_map(
        shards,
        mesh=mesh,
        in_specs=placed,
        out_specs=(rows, rows),
        check_vma=False,
    )
```

```python
import functools

import jax
import jax.numpy as jnp
from jax import lax
from jax.experimental import pallas as pl
from jax.experimental.pallas import tpu as pltpu
from jax.sharding import PartitionSpec as P

HEAD_DIM = 128
LATENT = 1024
TOPK = 6
DENSE_EXPERTS = 16
VMEM_LIMIT = 56 * 1024 * 1024
EXPERT_VMEM = 28 * 1024 * 1024


def run_expert(rows_in, w_first, w_second):
    hidden = jax.nn.relu(jnp.dot(rows_in, w_first, preferred_element_type=jnp.float32))
    hidden = (hidden * hidden).astype(jnp.bfloat16)
    return jnp.dot(hidden, w_second, preferred_element_type=jnp.float32).astype(jnp.bfloat16)


def column_of(row):
    n = row.shape[1]
    square = jnp.broadcast_to(row.astype(jnp.float32), (n, n)).T
    return square[:, :1].astype(jnp.int32)


def attend_kernel(
    place_ref, q_ref, k_own, k_far, v_own, v_far, doc_own, doc_far, ahead_ref, out_ref
):
    rows = q_ref.shape[0]
    heads = q_ref.shape[1] // HEAD_DIM
    here = place_ref[0] * rows
    there = (1 - place_ref[0]) * rows
    doc_query = column_of(doc_own[...])
    reach = here + lax.broadcasted_iota(jnp.int32, (rows, 1), 0) + column_of(ahead_ref[...])
    lane = lax.broadcasted_iota(jnp.int32, (1, rows), 1)
    see_own = (doc_own[...] == doc_query) & (here + lane <= reach)
    see_far = (doc_far[...] == doc_query) & (there + lane <= reach)
    scale = HEAD_DIM ** (-0.5)
    across = (((1,), (1,)), ((), ()))
    for head in range(heads):
        cols = slice(head * HEAD_DIM, (head + 1) * HEAD_DIM)
        q = q_ref[:, cols]
        near = lax.dot_general(q, k_own[:, cols], across, preferred_element_type=jnp.float32)
        far = lax.dot_general(q, k_far[:, cols], across, preferred_element_type=jnp.float32)
        near = jnp.where(see_own, near * scale, -1e30)
        far = jnp.where(see_far, far * scale, -1e30)
        top = jnp.max(jnp.maximum(near, far), axis=1, keepdims=True)
        near = jnp.exp(near - top)
        far = jnp.exp(far - top)
        share = 1.0 / jnp.sum(near + far, axis=1, keepdims=True)
        near = (near * share).astype(jnp.bfloat16)
        far = (far * share).astype(jnp.bfloat16)
        mixed = jnp.dot(near, v_own[:, cols], preferred_element_type=jnp.float32)
        mixed += jnp.dot(far, v_far[:, cols], preferred_element_type=jnp.float32)
        out_ref[:, cols] = mixed.astype(jnp.bfloat16)


def attend(place, q, k_own, k_far, v_own, v_far, doc_own, doc_far, ahead):
    vmem = pl.BlockSpec(memory_space=pltpu.VMEM)
    return pl.pallas_call(
        attend_kernel,
        out_shape=jax.ShapeDtypeStruct(q.shape, jnp.bfloat16),
        in_specs=[pl.BlockSpec(memory_space=pltpu.SMEM)] + [vmem] * 8,
        out_specs=vmem,
        compiler_params=pltpu.CompilerParams(vmem_limit_bytes=VMEM_LIMIT),
        cost_estimate=pl.CostEstimate(
            flops=4 * q.shape[0] * 2 * q.shape[0] * q.shape[1],
            bytes_accessed=6 * q.size * 2,
            transcendentals=2 * q.shape[0] * q.size // HEAD_DIM,
        ),
    )(place, q, k_own, k_far, v_own, v_far, doc_own, doc_far, ahead)


def gate_kernel(latent_ref, router_ref, routes_ref, out_ref):
    logits = lax.dot_general(
        router_ref[...], latent_ref[...], (((1,), (1,)), ((), ())), preferred_element_type=jnp.float32
    )
    number = lax.broadcasted_iota(jnp.int32, logits.shape, 0)
    named = number == routes_ref[0]
    for k in range(1, TOPK):
        named |= number == routes_ref[k]
    sigma = jnp.where(named, jax.nn.sigmoid(logits), 0.0)
    gates = sigma / jnp.sum(sigma, axis=0, keepdims=True)
    out_ref[...] = jnp.where(named, gates, -1.0)


def gate_table(latent, router, routes):
    vmem = pl.BlockSpec(memory_space=pltpu.VMEM)
    return pl.pallas_call(
        gate_kernel,
        out_shape=jax.ShapeDtypeStruct((router.shape[1], latent.shape[0]), jnp.float32),
        in_specs=[vmem] * 3,
        out_specs=vmem,
    )(latent, router.T, routes.transpose(2, 0, 1))


def kept_kernel(line, own_ref, capacity_ref, *refs):
    tables, out_ref = refs[:-1], refs[-1]
    own = own_ref[0]
    z = own // 4
    rows = tables[0].shape[2]
    sources = 4 * line
    upto = lax.broadcasted_iota(jnp.int32, (rows, rows), 0) <= lax.broadcasted_iota(
        jnp.int32, (rows, rows), 1
    )
    upto = jnp.where(upto, 1.0, 0.0).astype(jnp.bfloat16)
    device = lax.broadcasted_iota(jnp.int32, (sources, sources), 0) ^ own
    other = lax.broadcasted_iota(jnp.int32, (sources, sources), 1) ^ own
    lower = jnp.where(other < device, 1.0, 0.0).astype(jnp.bfloat16)
    entry = lax.broadcasted_iota(jnp.int32, (sources, rows), 0)
    gates = []
    for which in range(2):
        expert = own ^ which
        table = jnp.concatenate([part[:, expert, :] for part in tables], axis=0)
        named = table != -1.0
        flags = jnp.where(named, 1.0, 0.0)
        running = jnp.dot(flags.astype(jnp.bfloat16), upto, preferred_element_type=jnp.float32)
        totals = jnp.broadcast_to(running[:, rows - 1 :], (sources, rows)).astype(jnp.bfloat16)
        before = jnp.dot(lower, totals, preferred_element_type=jnp.float32)
        slots = before + running - flags
        limit = capacity_ref[expert].astype(jnp.float32)
        gates.append(jnp.where(named & (slots < limit), table, 0.0))
    ordered = []
    for step in range(line):
        home = 4 * (z ^ lax.rem(z + line - step, line))
        for side in range(2):
            for kept in gates:
                here = jnp.where(entry == home + 2 * side, kept, 0.0)
                ordered.append(jnp.sum(here, axis=0, keepdims=True))
    out_ref[...] = jnp.concatenate(ordered, axis=0).T


def kept_gates(own, capacity, tables):
    smem = pl.BlockSpec(memory_space=pltpu.SMEM)
    vmem = pl.BlockSpec(memory_space=pltpu.VMEM)
    line, rows = len(tables), tables[0].shape[2]
    return pl.pallas_call(
        functools.partial(kept_kernel, line),
        out_shape=jax.ShapeDtypeStruct((rows, 4 * line), jnp.float32),
        in_specs=[smem, smem] + [vmem] * line,
        out_specs=vmem,
    )(own, capacity, *tables)


def expert_kernel(place, gates_ref, xz_ref, xy_ref, w1a, w2a, w1b, w2b, z_ref, y_ref, hidden_ref):
    rows = xz_ref.shape[0]
    x = jnp.concatenate([xz_ref[...], xy_ref[...]], axis=0)
    step = 512
    for which, w1_ref in enumerate((w1a, w1b)):
        for first in range(0, w1_ref.shape[1], step):
            cols = slice(first, first + step)
            hidden = jnp.dot(x, w1_ref[:, cols], preferred_element_type=jnp.float32)
            hidden = jnp.maximum(hidden, 0.0)
            hidden_ref[which, :, cols] = (hidden * hidden).astype(jnp.bfloat16)
    for first in range(0, w2a.shape[1], step):
        cols = slice(first, first + step)
        results = [
            jnp.dot(hidden_ref[which], w2_ref[:, cols], preferred_element_type=jnp.float32)
            for which, w2_ref in enumerate((w2a, w2b))
        ]
        for side, out_ref in enumerate((z_ref, y_ref)):
            column = 4 * place + 2 * side
            part = slice(side * rows, (side + 1) * rows)
            mixed = results[0][part] * gates_ref[:, column : column + 1]
            mixed += results[1][part] * gates_ref[:, column + 1 : column + 2]
            out_ref[:, cols] = mixed.astype(jnp.bfloat16)


def run_piece(place, gates, from_line, from_side, weights):
    rows, width = from_line.shape
    hidden = weights[0].shape[1]
    vmem = pl.BlockSpec(memory_space=pltpu.VMEM)
    piece = jax.ShapeDtypeStruct((rows, width), jnp.bfloat16)
    return pl.pallas_call(
        functools.partial(expert_kernel, place),
        out_shape=(piece, piece),
        in_specs=[vmem] * 7,
        out_specs=(vmem, vmem),
        scratch_shapes=[pltpu.VMEM((2, 2 * rows, hidden), jnp.bfloat16)],
        compiler_params=pltpu.CompilerParams(vmem_limit_bytes=EXPERT_VMEM),
        cost_estimate=pl.CostEstimate(
            flops=16 * rows * width * hidden,
            bytes_accessed=8 * rows * width + 8 * width * hidden,
            transcendentals=0,
        ),
    )(gates, from_line, from_side, *weights)


def dense_moe(latent, router, expert_in, expert_out, routes, capacity):
    f32 = jnp.float32
    axes = ("expert", "context")
    line = router.shape[1] // 4
    spots = [(z, y) for z in range(line) for y in range(2)]
    sibling = [(0, 1), (1, 0)]
    across = [(2 * z + y, 2 * z + 1 - y) for z, y in spots]
    diagonal = [(4 * z + k, 4 * z + 3 - k) for z in range(line) for k in range(4)]

    def swap_core(x):
        return lax.ppermute(x, "context", sibling)

    def swap_side(x):
        return lax.ppermute(x, "expert", across)

    def along(x, step):
        return lax.ppermute(x, "expert", [(2 * z + y, 2 * ((z + step) % line) + y) for z, y in spots])

    def flipped(x, span):
        return lax.ppermute(x, "expert", [(2 * z + y, 2 * (z ^ span) + y) for z, y in spots])

    own = lax.axis_index(axes).astype(jnp.int32).reshape(1)
    rows = latent[0]
    from_line = [rows] + [along(rows, step) for step in range(1, line)]
    from_side = [swap_side(x) for x in from_line]
    w_first, w_second = expert_in[0], expert_out[0]
    weights = (w_first, w_second, swap_core(w_first), swap_core(w_second))

    table = gate_table(rows, router, routes)[None]
    table = jnp.concatenate(
        [table, swap_core(table), swap_side(table), lax.ppermute(table, axes, diagonal)], axis=0
    )
    tables = [table] + [flipped(table, span) for span in range(1, line)]
    gates = kept_gates(own, capacity, tables)

    total = None
    for step in list(range(1, line)) + [0]:
        mine, theirs = run_piece(step, gates, from_line[step], from_side[step], weights)
        column = mine.astype(f32) + swap_side(theirs).astype(f32)
        if step:
            column = along(column.astype(jnp.bfloat16), line - step).astype(f32)
        total = column if total is None else total + column
    return total.astype(jnp.bfloat16)[None]


def routed_moe(latent, router, expert_in, expert_out, routes, capacity):
    tok_count = latent.shape[1]
    token_rows = latent[0]
    expert_count = router.shape[1]
    per_peer = max(2, 2 * tok_count * TOPK // expert_count)
    logits = jnp.dot(token_rows, router, preferred_element_type=jnp.float32)
    chosen_ids = routes[0]
    expert_ids = jnp.arange(expert_count, dtype=jnp.int32)
    one_hot = chosen_ids[:, :, None] == expert_ids[None, None, :]
    picked = jnp.sum(jnp.where(one_hot, logits[:, None, :], 0.0), axis=2)
    sigmas = jax.nn.sigmoid(picked)
    gates = sigmas / jnp.sum(sigmas, axis=1, keepdims=True)
    flat_hot = one_hot.reshape(tok_count * TOPK, expert_count).astype(jnp.int32)
    counts = jnp.sum(flat_hot, axis=0)
    ranks = jnp.sum((jnp.cumsum(flat_hot, axis=0) - flat_hot) * flat_hot, axis=1)
    count_rows = lax.all_gather(counts[None, :], ("expert", "context"), axis=0, tiled=True)
    own_index = lax.axis_index(("expert", "context"))
    lower_rows = jnp.arange(count_rows.shape[0], dtype=jnp.int32)[:, None] < own_index
    before = jnp.sum(jnp.where(lower_rows, count_rows, 0), axis=0)
    slots = jnp.sum(flat_hot * before[None, :], axis=1) + ranks
    limits = jnp.sum(flat_hot * capacity[None, :], axis=1)
    kept = slots < limits
    flat_ids = chosen_ids.reshape(-1)
    places = flat_ids * per_peer + ranks
    owners = jnp.arange(tok_count * TOPK, dtype=jnp.int32) // TOPK
    send_rows = (
        jnp.zeros((expert_count * per_peer, LATENT), jnp.bfloat16)
        .at[places]
        .set(token_rows[owners])
    )
    recv_rows = lax.all_to_all(
        send_rows.reshape(expert_count, per_peer, LATENT),
        ("expert", "context"),
        split_axis=0,
        concat_axis=0,
        tiled=True,
    ).reshape(expert_count * per_peer, LATENT)
    results = run_expert(recv_rows, expert_in[0], expert_out[0])
    returned = lax.all_to_all(
        results.reshape(expert_count, per_peer, LATENT),
        ("expert", "context"),
        split_axis=0,
        concat_axis=0,
        tiled=True,
    ).reshape(expert_count * per_peer, LATENT)
    gate_kept = jnp.where(kept, gates.reshape(-1), 0.0).reshape(tok_count, TOPK)
    back_rows = returned[places].reshape(tok_count, TOPK, LATENT).astype(jnp.float32)
    mixture = jnp.sum(gate_kept[:, :, None] * back_rows, axis=1)
    return mixture.astype(jnp.bfloat16).reshape(1, tok_count, LATENT)


def shards(
    query_heads,
    key_heads,
    value_heads,
    latent,
    router,
    expert_in,
    expert_out,
    routes,
    segments,
    offsets,
    capacity,
):
    swap = [(0, 1), (1, 0)]
    k_far = lax.ppermute(key_heads[0], "context", swap)
    v_far = lax.ppermute(value_heads[0], "context", swap)
    doc_far = lax.ppermute(segments, "context", swap)
    place = lax.axis_index("context").astype(jnp.int32).reshape(1)
    attn_out = attend(
        place, query_heads[0], key_heads[0], k_far, value_heads[0], v_far, segments, doc_far, offsets
    )[None]
    moe = dense_moe if router.shape[1] <= DENSE_EXPERTS else routed_moe
    moe_out = moe(latent, router, expert_in, expert_out, routes, capacity)
    return (attn_out, moe_out)


def solution(mesh):
    rows = P(("groups", "expert"), "context", None)
    placed = (
        rows,
        rows,
        rows,
        rows,
        P(),
        P(("expert", "context"), None, None),
        P(("expert", "context"), None, None),
        rows,
        P(("groups", "expert"), "context"),
        P(("groups", "expert"), "context"),
        P(),
    )
    return jax.shard_map(
        shards,
        mesh=mesh,
        in_specs=placed,
        out_specs=(rows, rows),
        check_vma=False,
    )
```

```python
import functools
import math

import jax
import jax.numpy as jnp
from jax import lax
from jax.experimental import pallas as pl
from jax.experimental.pallas import tpu as pltpu
from jax.sharding import PartitionSpec as P

HEAD_DIM = 128
LATENT = 1024
TOPK = 6
DENSE_EXPERTS = 16
EXPERT_VMEM = 28 * 1024 * 1024
ATTEND_VMEM = 16 * 1024 * 1024
EXPERT_COST = 1024
ATTEND_COST = 1024


def run_expert(rows_in, w_first, w_second):
    hidden = jax.nn.relu(jnp.dot(rows_in, w_first, preferred_element_type=jnp.float32))
    hidden = (hidden * hidden).astype(jnp.bfloat16)
    return jnp.dot(hidden, w_second, preferred_element_type=jnp.float32).astype(jnp.bfloat16)


def column_of(row):
    n = row.shape[1]
    square = jnp.broadcast_to(row.astype(jnp.float32), (n, n)).T
    return square[:, :1].astype(jnp.int32)


def attend_kernel(place_ref, q_ref, k_own, k_far, v_own, v_far, doc_own, doc_far, ahead_ref, *rest):
    out_ref = rest[-1]
    rows = q_ref.shape[0]
    heads = q_ref.shape[1] // HEAD_DIM
    here = place_ref[0] * rows
    there = (1 - place_ref[0]) * rows
    doc_query = column_of(doc_own[...])
    reach = here + lax.broadcasted_iota(jnp.int32, (rows, 1), 0) + column_of(ahead_ref[...])
    lane = lax.broadcasted_iota(jnp.int32, (1, rows), 1)
    doc_key = jnp.concatenate([doc_own[...], doc_far[...]], axis=1)
    spot = jnp.concatenate([here + lane, there + lane], axis=1)
    visible = (doc_key == doc_query) & (spot <= reach)
    scale = HEAD_DIM ** (-0.5) * math.log2(math.e)
    across = (((1,), (1,)), ((), ()))
    for head in range(heads):
        cols = slice(head * HEAD_DIM, (head + 1) * HEAD_DIM)
        keys = jnp.concatenate([k_own[:, cols], k_far[:, cols]], axis=0)
        values = jnp.concatenate([v_own[:, cols], v_far[:, cols]], axis=0)
        scores = lax.dot_general(q_ref[:, cols], keys, across, preferred_element_type=jnp.float32)
        scores = jnp.where(visible, scores * scale, -1e30)
        raw = jnp.exp2(scores - jnp.max(scores, axis=1, keepdims=True))
        share = 1.0 / jnp.sum(raw, axis=1, keepdims=True)
        mixed = jnp.dot(raw.astype(jnp.bfloat16), values, preferred_element_type=jnp.float32)
        out_ref[:, cols] = (mixed * share).astype(jnp.bfloat16)


def attend(half, place, q, k_own, k_far, v_own, v_far, doc_own, doc_far, ahead, before=None, after=()):
    rows, width = q.shape
    smem = pl.BlockSpec(memory_space=pltpu.SMEM)
    heads = pl.BlockSpec((rows, width // 2), lambda i: (0, half))
    line = pl.BlockSpec((1, rows), lambda i: (0, 0))
    extra = list(after) + ([] if before is None else [before])
    return pl.pallas_call(
        attend_kernel,
        grid=(1,),
        out_shape=jax.ShapeDtypeStruct(q.shape, jnp.bfloat16),
        in_specs=[smem] + [heads] * 5 + [line] * 3 + [pl.BlockSpec(memory_space=pl.ANY)] * len(extra),
        out_specs=heads,
        input_output_aliases={} if before is None else {8 + len(extra): 0},
        compiler_params=pltpu.CompilerParams(vmem_limit_bytes=ATTEND_VMEM),
        cost_estimate=pl.CostEstimate(flops=ATTEND_COST, bytes_accessed=ATTEND_COST, transcendentals=0),
    )(place, q, k_own, k_far, v_own, v_far, doc_own, doc_far, ahead, *extra)


def prep_kernel(latent_ref, *refs):
    parts, rows_ref, table_ref = refs[:-2], refs[-2], refs[-1]
    rows_ref[...] = latent_ref[...]
    for index, part in enumerate(parts):
        for k in range(TOPK):
            table_ref[index, k : k + 1, :] = part[k]
        table_ref[index, TOPK:, :] = jnp.full((8 - TOPK, part.shape[2]), -1, jnp.int32)


def prepare(latent, parts):
    vmem = pl.BlockSpec(memory_space=pltpu.VMEM)
    return pl.pallas_call(
        prep_kernel,
        out_shape=(
            jax.ShapeDtypeStruct(latent.shape, latent.dtype),
            jax.ShapeDtypeStruct((len(parts), 8, latent.shape[0]), jnp.int32),
        ),
        in_specs=[vmem] * (1 + len(parts)),
        out_specs=(vmem, vmem),
        cost_estimate=pl.CostEstimate(flops=1024, bytes_accessed=1024, transcendentals=0),
    )(latent, *parts)


def kept_kernel(line, own_ref, capacity_ref, *refs):
    tables, out_ref = refs[:-1], refs[-1]
    own = own_ref[0]
    z = own // 4
    rows = tables[0].shape[2]
    sources = 4 * line
    upto = lax.broadcasted_iota(jnp.int32, (rows, rows), 0) <= lax.broadcasted_iota(
        jnp.int32, (rows, rows), 1
    )
    upto = jnp.where(upto, 1.0, 0.0).astype(jnp.bfloat16)
    device = lax.broadcasted_iota(jnp.int32, (sources, sources), 0) ^ own
    other = lax.broadcasted_iota(jnp.int32, (sources, sources), 1) ^ own
    lower = jnp.where(other < device, 1.0, 0.0).astype(jnp.bfloat16)
    entry = lax.broadcasted_iota(jnp.int32, (sources, rows), 0)
    named = []
    for k in range(TOPK):
        named.append(jnp.concatenate([part[:, k, :] for part in tables], axis=0))
    kept = []
    for which in range(2):
        expert = own ^ which
        mine = named[0] == expert
        for k in range(1, TOPK):
            mine |= named[k] == expert
        flags = jnp.where(mine, 1.0, 0.0)
        running = jnp.dot(flags.astype(jnp.bfloat16), upto, preferred_element_type=jnp.float32)
        totals = jnp.broadcast_to(running[:, rows - 1 :], (sources, rows)).astype(jnp.bfloat16)
        before = jnp.dot(lower, totals, preferred_element_type=jnp.float32)
        slots = before + running - flags
        limit = capacity_ref[expert].astype(jnp.float32)
        kept.append(jnp.where(mine & (slots < limit), 1, 0))
    for step in range(line):
        home = 4 * (z ^ lax.rem(z + line - step, line))
        for side in range(2):
            here = entry == home + 2 * side
            for k, part in enumerate(named + kept):
                picked = jnp.sum(jnp.where(here, part, 0), axis=0, keepdims=True)
                out_ref[2 * step + side, k : k + 1, :] = picked


def kept_rows(own, capacity, tables):
    smem = pl.BlockSpec(memory_space=pltpu.SMEM)
    vmem = pl.BlockSpec(memory_space=pltpu.VMEM)
    line, rows = len(tables), tables[0].shape[2]
    return pl.pallas_call(
        functools.partial(kept_kernel, line),
        out_shape=jax.ShapeDtypeStruct((2 * line, 8, rows), jnp.int32),
        in_specs=[smem, smem] + [vmem] * line,
        out_specs=vmem,
        cost_estimate=pl.CostEstimate(flops=1024, bytes_accessed=1024, transcendentals=0),
    )(own, capacity, *tables)


def gate_columns(own, router_ref, x, kept):
    logits = lax.dot_general(
        router_ref[...], x, (((1,), (1,)), ((), ())), preferred_element_type=jnp.float32
    )
    number = lax.broadcasted_iota(jnp.int32, logits.shape, 0)
    named = number == kept[0:1]
    for k in range(1, TOPK):
        named |= number == kept[k : k + 1]
    sigma = jnp.where(named, jax.nn.sigmoid(logits), 0.0)
    gates = sigma / jnp.sum(sigma, axis=0, keepdims=True)
    lines = []
    for which in range(2):
        gate = jnp.sum(jnp.where(number == own ^ which, gates, 0.0), axis=0, keepdims=True)
        lines.append(jnp.where(kept[TOPK + which : TOPK + which + 1] > 0, gate, 0.0))
    square = jnp.concatenate(lines + [jnp.zeros((x.shape[0] - 2, x.shape[0]), jnp.float32)], axis=0)
    return square.T


def expert_kernel(
    place, own_ref, kept_ref, router_ref, xz_ref, xy_ref, w1a, w2a, w1b_any, w2b_any, *rest
):
    z_ref, y_ref, hidden_ref, w1b, w2b, sems = rest[-6:]
    loads = [
        pltpu.make_async_copy(w1b_any, w1b, sems.at[0]),
        pltpu.make_async_copy(w2b_any, w2b, sems.at[1]),
    ]
    for load in loads:
        load.start()
    own = own_ref[0]
    rows = xz_ref.shape[0]
    x = jnp.concatenate([xz_ref[...], xy_ref[...]], axis=0)
    step = 512

    def enter(which, w1_ref):
        for first in range(0, w1_ref.shape[1], step):
            cols = slice(first, first + step)
            hidden = jnp.dot(x, w1_ref[:, cols], preferred_element_type=jnp.float32)
            hidden = jnp.maximum(hidden, 0.0)
            hidden_ref[which, :, cols] = (hidden * hidden).astype(jnp.bfloat16)

    enter(0, w1a)
    gates = [
        gate_columns(own, router_ref, x_ref[...], kept_ref[2 * place + side])
        for side, x_ref in enumerate((xz_ref, xy_ref))
    ]
    loads[0].wait()
    enter(1, w1b)
    loads[1].wait()
    for first in range(0, w2a.shape[1], step):
        cols = slice(first, first + step)
        results = [
            jnp.dot(hidden_ref[which], w2_ref[:, cols], preferred_element_type=jnp.float32)
            for which, w2_ref in enumerate((w2a, w2b))
        ]
        for side, out_ref in enumerate((z_ref, y_ref)):
            part = slice(side * rows, (side + 1) * rows)
            mixed = results[0][part] * gates[side][:, 0:1] + results[1][part] * gates[side][:, 1:2]
            out_ref[:, cols] = mixed.astype(jnp.bfloat16)


def run_piece(place, own, kept, router, from_line, from_side, weights, after):
    rows, width = from_line.shape
    hidden = weights[0].shape[1]
    smem = pl.BlockSpec(memory_space=pltpu.SMEM)
    vmem = pl.BlockSpec(memory_space=pltpu.VMEM)
    anywhere = pl.BlockSpec(memory_space=pl.ANY)
    piece = jax.ShapeDtypeStruct((rows, width), jnp.bfloat16)
    return pl.pallas_call(
        functools.partial(expert_kernel, place),
        out_shape=(piece, piece),
        in_specs=[smem] + [vmem] * 6 + [anywhere] * (2 + len(after)),
        out_specs=(vmem, vmem),
        scratch_shapes=[
            pltpu.VMEM((2, 2 * rows, hidden), jnp.bfloat16),
            pltpu.VMEM(weights[2].shape, jnp.bfloat16),
            pltpu.VMEM(weights[3].shape, jnp.bfloat16),
            pltpu.SemaphoreType.DMA((2,)),
        ],
        compiler_params=pltpu.CompilerParams(vmem_limit_bytes=EXPERT_VMEM),
        cost_estimate=pl.CostEstimate(flops=EXPERT_COST, bytes_accessed=EXPERT_COST, transcendentals=0),
    )(own, kept, router, from_line, from_side, *weights, *after)


def dense_moe(latent, router, expert_in, expert_out, routes, capacity, attention):
    f32 = jnp.float32
    axes = ("expert", "context")
    line = router.shape[1] // 4
    spots = [(z, y) for z in range(line) for y in range(2)]
    sibling = [(0, 1), (1, 0)]
    across = [(2 * z + y, 2 * z + 1 - y) for z, y in spots]
    diagonal = [(4 * z + k, 4 * z + 3 - k) for z in range(line) for k in range(4)]

    def swap_core(x):
        return lax.ppermute(x, "context", sibling)

    def swap_side(x):
        return lax.ppermute(x, "expert", across)

    def along(x, step):
        return lax.ppermute(x, "expert", [(2 * z + y, 2 * ((z + step) % line) + y) for z, y in spots])

    def flipped(x, span):
        return lax.ppermute(x, "expert", [(2 * z + y, 2 * (z ^ span) + y) for z, y in spots])

    own = lax.axis_index(axes).astype(jnp.int32).reshape(1)
    named = routes[0].T[:, None, :]
    parts = [named, swap_core(named), swap_side(named), lax.ppermute(named, axes, diagonal)]
    rows, table = prepare(latent[0], parts)
    tables = [table] + [flipped(table, span) for span in range(1, line)]
    kept = kept_rows(own, capacity, tables)

    w_first, w_second = expert_in[0], expert_out[0]
    weights = (w_first, w_second, swap_core(w_first), swap_core(w_second))
    from_line = [rows] + [along(rows, step) for step in range(1, line)]
    from_side = [swap_side(x) for x in from_line]

    half = attention(0, after=(kept,))
    total = None
    after = ()
    for step in range(line):
        mine, theirs = run_piece(
            step, own, kept, router.T, from_line[step], from_side[step], weights, after
        )
        after = (mine,)
        column = mine.astype(f32) + swap_side(theirs).astype(f32)
        if step:
            column = along(column.astype(jnp.bfloat16), line - step).astype(f32)
        total = column if total is None else total + column
    return attention(1, before=half, after=after), total.astype(jnp.bfloat16)[None]


def routed_moe(latent, router, expert_in, expert_out, routes, capacity):
    tok_count = latent.shape[1]
    token_rows = latent[0]
    expert_count = router.shape[1]
    per_peer = max(2, 2 * tok_count * TOPK // expert_count)
    logits = jnp.dot(token_rows, router, preferred_element_type=jnp.float32)
    chosen_ids = routes[0]
    expert_ids = jnp.arange(expert_count, dtype=jnp.int32)
    one_hot = chosen_ids[:, :, None] == expert_ids[None, None, :]
    picked = jnp.sum(jnp.where(one_hot, logits[:, None, :], 0.0), axis=2)
    sigmas = jax.nn.sigmoid(picked)
    gates = sigmas / jnp.sum(sigmas, axis=1, keepdims=True)
    flat_hot = one_hot.reshape(tok_count * TOPK, expert_count).astype(jnp.int32)
    counts = jnp.sum(flat_hot, axis=0)
    ranks = jnp.sum((jnp.cumsum(flat_hot, axis=0) - flat_hot) * flat_hot, axis=1)
    count_rows = lax.all_gather(counts[None, :], ("expert", "context"), axis=0, tiled=True)
    own_index = lax.axis_index(("expert", "context"))
    lower_rows = jnp.arange(count_rows.shape[0], dtype=jnp.int32)[:, None] < own_index
    before = jnp.sum(jnp.where(lower_rows, count_rows, 0), axis=0)
    slots = jnp.sum(flat_hot * before[None, :], axis=1) + ranks
    limits = jnp.sum(flat_hot * capacity[None, :], axis=1)
    kept = slots < limits
    flat_ids = chosen_ids.reshape(-1)
    places = flat_ids * per_peer + ranks
    owners = jnp.arange(tok_count * TOPK, dtype=jnp.int32) // TOPK
    send_rows = (
        jnp.zeros((expert_count * per_peer, LATENT), jnp.bfloat16)
        .at[places]
        .set(token_rows[owners])
    )
    recv_rows = lax.all_to_all(
        send_rows.reshape(expert_count, per_peer, LATENT),
        ("expert", "context"),
        split_axis=0,
        concat_axis=0,
        tiled=True,
    ).reshape(expert_count * per_peer, LATENT)
    results = run_expert(recv_rows, expert_in[0], expert_out[0])
    returned = lax.all_to_all(
        results.reshape(expert_count, per_peer, LATENT),
        ("expert", "context"),
        split_axis=0,
        concat_axis=0,
        tiled=True,
    ).reshape(expert_count * per_peer, LATENT)
    gate_kept = jnp.where(kept, gates.reshape(-1), 0.0).reshape(tok_count, TOPK)
    back_rows = returned[places].reshape(tok_count, TOPK, LATENT).astype(jnp.float32)
    mixture = jnp.sum(gate_kept[:, :, None] * back_rows, axis=1)
    return mixture.astype(jnp.bfloat16).reshape(1, tok_count, LATENT)


def shards(
    query_heads,
    key_heads,
    value_heads,
    latent,
    router,
    expert_in,
    expert_out,
    routes,
    segments,
    offsets,
    capacity,
):
    swap = [(0, 1), (1, 0)]
    k_far = lax.ppermute(key_heads[0], "context", swap)
    v_far = lax.ppermute(value_heads[0], "context", swap)
    doc_far = lax.ppermute(segments, "context", swap)
    place = lax.axis_index("context").astype(jnp.int32).reshape(1)

    def attention(half, **order):
        return attend(
            half,
            place,
            query_heads[0],
            key_heads[0],
            k_far,
            value_heads[0],
            v_far,
            segments,
            doc_far,
            offsets,
            **order,
        )

    if router.shape[1] <= DENSE_EXPERTS:
        attn_out, moe_out = dense_moe(
            latent, router, expert_in, expert_out, routes, capacity, attention
        )
    else:
        attn_out = attention(1, before=attention(0))
        moe_out = routed_moe(latent, router, expert_in, expert_out, routes, capacity)
    return (attn_out[None], moe_out)


def solution(mesh):
    rows = P(("groups", "expert"), "context", None)
    placed = (
        rows,
        rows,
        rows,
        rows,
        P(),
        P(("expert", "context"), None, None),
        P(("expert", "context"), None, None),
        rows,
        P(("groups", "expert"), "context"),
        P(("groups", "expert"), "context"),
        P(),
    )
    return jax.shard_map(
        shards,
        mesh=mesh,
        in_specs=placed,
        out_specs=(rows, rows),
        check_vma=False,
    )
```

```python
import functools
import math

import jax
import jax.numpy as jnp
from jax import lax
from jax.experimental import pallas as pl
from jax.experimental.pallas import tpu as pltpu
from jax.sharding import PartitionSpec as P

HEAD_DIM = 128
LATENT = 1024
TOPK = 6
DENSE_EXPERTS = 16
EXPERT_VMEM = 16 * 1024 * 1024
ATTEND_VMEM = 10 * 1024 * 1024
SMALL_VMEM = 4 * 1024 * 1024
LOAD_VMEM = 44 * 1024 * 1024


def run_expert(rows_in, w_first, w_second):
    hidden = jax.nn.relu(jnp.dot(rows_in, w_first, preferred_element_type=jnp.float32))
    hidden = (hidden * hidden).astype(jnp.bfloat16)
    return jnp.dot(hidden, w_second, preferred_element_type=jnp.float32).astype(jnp.bfloat16)


def column_of(row):
    n = row.shape[1]
    square = jnp.broadcast_to(row.astype(jnp.float32), (n, n)).T
    return square[:, :1].astype(jnp.int32)


def attend_kernel(place_ref, q_ref, k_own, k_far, v_own, v_far, doc_own, doc_far, ahead_ref, *rest):
    out_ref = rest[-1]
    rows = q_ref.shape[0]
    heads = q_ref.shape[1] // HEAD_DIM
    here = place_ref[0] * rows
    there = (1 - place_ref[0]) * rows
    doc_query = column_of(doc_own[...])
    reach = here + lax.broadcasted_iota(jnp.int32, (rows, 1), 0) + column_of(ahead_ref[...])
    lane = lax.broadcasted_iota(jnp.int32, (1, rows), 1)
    doc_key = jnp.concatenate([doc_own[...], doc_far[...]], axis=1)
    spot = jnp.concatenate([here + lane, there + lane], axis=1)
    visible = (doc_key == doc_query) & (spot <= reach)
    scale = HEAD_DIM ** (-0.5) * math.log2(math.e)
    across = (((1,), (1,)), ((), ()))
    for head in range(heads):
        cols = slice(head * HEAD_DIM, (head + 1) * HEAD_DIM)
        keys = jnp.concatenate([k_own[:, cols], k_far[:, cols]], axis=0)
        values = jnp.concatenate([v_own[:, cols], v_far[:, cols]], axis=0)
        scores = lax.dot_general(q_ref[:, cols], keys, across, preferred_element_type=jnp.float32)
        scores = jnp.where(visible, scores * scale, -1e30)
        raw = jnp.exp2(scores - jnp.max(scores, axis=1, keepdims=True))
        share = 1.0 / jnp.sum(raw, axis=1, keepdims=True)
        mixed = jnp.dot(raw.astype(jnp.bfloat16), values, preferred_element_type=jnp.float32)
        out_ref[:, cols] = (mixed * share).astype(jnp.bfloat16)


def attend(half, place, q, k_own, k_far, v_own, v_far, doc_own, doc_far, ahead, before=None, after=()):
    rows, width = q.shape
    smem = pl.BlockSpec(memory_space=pltpu.SMEM)
    heads = pl.BlockSpec((rows, width // 2), lambda i: (0, half))
    line = pl.BlockSpec((1, rows), lambda i: (0, 0))
    extra = list(after) + ([] if before is None else [before])
    return pl.pallas_call(
        attend_kernel,
        grid=(1,),
        out_shape=jax.ShapeDtypeStruct(q.shape, jnp.bfloat16),
        in_specs=[smem] + [heads] * 5 + [line] * 3 + [pl.BlockSpec(memory_space=pl.ANY)] * len(extra),
        out_specs=heads,
        input_output_aliases={} if before is None else {8 + len(extra): 0},
        compiler_params=pltpu.CompilerParams(vmem_limit_bytes=ATTEND_VMEM),
        cost_estimate=pl.CostEstimate(
            flops=4 * rows * rows * width, bytes_accessed=6 * rows * width, transcendentals=0
        ),
    )(place, q, k_own, k_far, v_own, v_far, doc_own, doc_far, ahead, *extra)


def pack_kernel(latent_ref, named_ref, doc_ref, rows_ref, table_ref):
    rows_ref[...] = latent_ref[...]
    for k in range(TOPK):
        table_ref[0, k : k + 1, :] = named_ref[k]
    table_ref[0, TOPK : TOPK + 1, :] = doc_ref[...]
    table_ref[0, TOPK + 1 :, :] = doc_ref[...]


def pack(latent, named, doc):
    vmem = pl.BlockSpec(memory_space=pltpu.VMEM)
    return pl.pallas_call(
        pack_kernel,
        out_shape=(
            jax.ShapeDtypeStruct(latent.shape, latent.dtype),
            jax.ShapeDtypeStruct((1, 8, latent.shape[0]), jnp.int32),
        ),
        in_specs=[vmem] * 3,
        out_specs=(vmem, vmem),
        compiler_params=pltpu.CompilerParams(vmem_limit_bytes=SMALL_VMEM),
    )(latent, named, doc)


def join_kernel(first_ref, second_ref, *refs):
    count = first_ref.shape[0]
    refs[-1][:count] = first_ref[...]
    refs[-1][count:] = second_ref[...]


def join(first, second, passed=None, after=()):
    vmem = pl.BlockSpec(memory_space=pltpu.VMEM)
    anywhere = pl.BlockSpec(memory_space=pl.ANY)
    table = jax.ShapeDtypeStruct((2 * first.shape[0],) + first.shape[1:], first.dtype)
    through = [] if passed is None else [passed]
    out = pl.pallas_call(
        join_kernel,
        out_shape=[jax.ShapeDtypeStruct(x.shape, x.dtype) for x in through] + [table],
        in_specs=[vmem] * 2 + [anywhere] * (len(through) + len(after)),
        out_specs=[anywhere] * len(through) + [vmem],
        input_output_aliases={2: 0} if through else {},
        compiler_params=pltpu.CompilerParams(vmem_limit_bytes=SMALL_VMEM),
    )(first, second, *through, *after)
    return out if through else out[0]


def load_kernel(w1_any, w2_any, *refs):
    w1_ref, w2_ref, sems = refs[-3:]
    loads = [
        pltpu.make_async_copy(w1_any, w1_ref, sems.at[0]),
        pltpu.make_async_copy(w2_any, w2_ref, sems.at[1]),
    ]
    for load in loads:
        load.start()
    for load in loads:
        load.wait()


def load_weights(w_first, w_second, after):
    anywhere = pl.BlockSpec(memory_space=pl.ANY)
    vmem = pl.BlockSpec(memory_space=pltpu.VMEM)
    return pl.pallas_call(
        load_kernel,
        out_shape=(
            pltpu.VMEM(w_first.shape, w_first.dtype),
            pltpu.VMEM(w_second.shape, w_second.dtype),
        ),
        in_specs=[anywhere] * (2 + len(after)),
        out_specs=(vmem, vmem),
        scratch_shapes=[pltpu.SemaphoreType.DMA((2,))],
        compiler_params=pltpu.CompilerParams(vmem_limit_bytes=LOAD_VMEM),
    )(w_first, w_second, *after)


def kept_kernel(own_ref, capacity_ref, low_ref, high_ref, *refs):
    out_ref = refs[-1]
    tables = (low_ref, high_ref)
    own = own_ref[0]
    z = own // 4
    rows = low_ref.shape[2]
    sources = 2 * low_ref.shape[0]
    line = sources // 4
    upto = lax.broadcasted_iota(jnp.int32, (rows, rows), 0) <= lax.broadcasted_iota(
        jnp.int32, (rows, rows), 1
    )
    upto = jnp.where(upto, 1.0, 0.0).astype(jnp.bfloat16)
    device = lax.broadcasted_iota(jnp.int32, (sources, sources), 0) ^ own
    other = lax.broadcasted_iota(jnp.int32, (sources, sources), 1) ^ own
    lower = jnp.where(other < device, 1.0, 0.0).astype(jnp.bfloat16)
    entry = lax.broadcasted_iota(jnp.int32, (sources, rows), 0)
    named = []
    for k in range(TOPK):
        named.append(jnp.concatenate([part[:, k, :] for part in tables], axis=0))
    kept = []
    for which in range(2):
        expert = own ^ which
        mine = named[0] == expert
        for k in range(1, TOPK):
            mine |= named[k] == expert
        flags = jnp.where(mine, 1.0, 0.0)
        running = jnp.dot(flags.astype(jnp.bfloat16), upto, preferred_element_type=jnp.float32)
        totals = jnp.broadcast_to(running[:, rows - 1 :], (sources, rows)).astype(jnp.bfloat16)
        before = jnp.dot(lower, totals, preferred_element_type=jnp.float32)
        slots = before + running - flags
        limit = capacity_ref[expert].astype(jnp.float32)
        kept.append(jnp.where(mine & (slots < limit), 1, 0))
    for step in range(line):
        home = 4 * (z ^ lax.rem(z + line - step, line))
        for side in range(2):
            here = entry == home + 2 * side
            for k, part in enumerate(named + kept):
                picked = jnp.sum(jnp.where(here, part, 0), axis=0, keepdims=True)
                out_ref[2 * step + side, k : k + 1, :] = picked


def kept_rows(own, capacity, low, high, after):
    smem = pl.BlockSpec(memory_space=pltpu.SMEM)
    vmem = pl.BlockSpec(memory_space=pltpu.VMEM)
    anywhere = pl.BlockSpec(memory_space=pl.ANY)
    return pl.pallas_call(
        kept_kernel,
        out_shape=jax.ShapeDtypeStruct(low.shape, jnp.int32),
        in_specs=[smem, smem, vmem, vmem] + [anywhere] * len(after),
        out_specs=vmem,
        compiler_params=pltpu.CompilerParams(vmem_limit_bytes=SMALL_VMEM),
    )(own, capacity, low, high, *after)


def gate_columns(own, router_ref, x, kept):
    logits = lax.dot_general(
        router_ref[...], x, (((1,), (1,)), ((), ())), preferred_element_type=jnp.float32
    )
    number = lax.broadcasted_iota(jnp.int32, logits.shape, 0)
    named = number == kept[0:1]
    for k in range(1, TOPK):
        named |= number == kept[k : k + 1]
    sigma = jnp.where(named, jax.nn.sigmoid(logits), 0.0)
    gates = sigma / jnp.sum(sigma, axis=0, keepdims=True)
    lines = []
    for which in range(2):
        gate = jnp.sum(jnp.where(number == own ^ which, gates, 0.0), axis=0, keepdims=True)
        lines.append(jnp.where(kept[TOPK + which : TOPK + which + 1] > 0, gate, 0.0))
    square = jnp.concatenate(lines + [jnp.zeros((x.shape[0] - 2, x.shape[0]), jnp.float32)], axis=0)
    return square.T


def expert_kernel(place, own_ref, kept_ref, router_ref, xz_ref, xy_ref, w1a, w2a, w1b, w2b, *rest):
    z_ref, y_ref, hidden_ref = rest[-3:]
    own = own_ref[0]
    rows = xz_ref.shape[0]
    x = jnp.concatenate([xz_ref[...], xy_ref[...]], axis=0)
    step = 512
    for which, w1_ref in enumerate((w1a, w1b)):
        for first in range(0, w1_ref.shape[1], step):
            cols = slice(first, first + step)
            hidden = jnp.dot(x, w1_ref[:, cols], preferred_element_type=jnp.float32)
            hidden = jnp.maximum(hidden, 0.0)
            hidden_ref[which, :, cols] = (hidden * hidden).astype(jnp.bfloat16)
    gates = [
        gate_columns(own, router_ref, x_ref[...], kept_ref[2 * place + side])
        for side, x_ref in enumerate((xz_ref, xy_ref))
    ]
    for first in range(0, w2a.shape[1], step):
        cols = slice(first, first + step)
        results = [
            jnp.dot(hidden_ref[which], w2_ref[:, cols], preferred_element_type=jnp.float32)
            for which, w2_ref in enumerate((w2a, w2b))
        ]
        for side, out_ref in enumerate((z_ref, y_ref)):
            part = slice(side * rows, (side + 1) * rows)
            mixed = results[0][part] * gates[side][:, 0:1] + results[1][part] * gates[side][:, 1:2]
            out_ref[:, cols] = mixed.astype(jnp.bfloat16)


def run_piece(place, own, kept, router, from_line, from_side, weights, after):
    rows, width = from_line.shape
    hidden = weights[0].shape[1]
    smem = pl.BlockSpec(memory_space=pltpu.SMEM)
    vmem = pl.BlockSpec(memory_space=pltpu.VMEM)
    anywhere = pl.BlockSpec(memory_space=pl.ANY)
    piece = jax.ShapeDtypeStruct((rows, width), jnp.bfloat16)
    weights = [pltpu.with_memory_space_constraint(w, pltpu.VMEM) for w in weights]
    return pl.pallas_call(
        functools.partial(expert_kernel, place),
        out_shape=(piece, piece),
        in_specs=[smem] + [vmem] * 8 + [anywhere] * len(after),
        out_specs=(vmem, vmem),
        scratch_shapes=[pltpu.VMEM((2, 2 * rows, hidden), jnp.bfloat16)],
        compiler_params=pltpu.CompilerParams(vmem_limit_bytes=EXPERT_VMEM),
        cost_estimate=pl.CostEstimate(
            flops=16 * rows * width * hidden,
            bytes_accessed=8 * rows * width,
            transcendentals=0,
        ),
    )(own, kept, router, from_line, from_side, *weights, *after)


def add_kernel(count, first_ref, second_ref, *refs):
    total = first_ref[...].astype(jnp.float32) + second_ref[...].astype(jnp.float32)
    outs = refs[len(refs) - count - 1 :]
    outs[-1][...] = total.astype(jnp.bfloat16)
    for index in range(count):
        outs[index][...] = refs[index][...]


def add(first, second, after=(), staged=()):
    vmem = pl.BlockSpec(memory_space=pltpu.VMEM)
    anywhere = pl.BlockSpec(memory_space=pl.ANY)
    out = pl.pallas_call(
        functools.partial(add_kernel, len(staged)),
        out_shape=[jax.ShapeDtypeStruct(x.shape, x.dtype) for x in staged]
        + [jax.ShapeDtypeStruct(first.shape, first.dtype)],
        in_specs=[vmem] * (2 + len(staged)) + [anywhere] * len(after),
        out_specs=[vmem] * (1 + len(staged)),
        compiler_params=pltpu.CompilerParams(vmem_limit_bytes=SMALL_VMEM),
        cost_estimate=pl.CostEstimate(flops=first.size, bytes_accessed=first.size, transcendentals=0),
    )(first, second, *staged, *after)
    return out if staged else out[0]


def dense_moe(latent, router, expert_in, expert_out, routes, segments, capacity, k_near, v_near, attention):
    f32 = jnp.float32
    line = router.shape[1] // 4
    spots = [(z, y) for z in range(line) for y in range(2)]
    sibling = [(0, 1), (1, 0)]
    across = [(2 * z + y, 2 * z + 1 - y) for z, y in spots]

    def swap_core(x):
        return lax.ppermute(x, "context", sibling)

    def swap_side(x):
        return lax.ppermute(x, "expert", across)

    def along(x, step):
        return lax.ppermute(x, "expert", [(2 * z + y, 2 * ((z + step) % line) + y) for z, y in spots])

    def flipped(x, span):
        return lax.ppermute(x, "expert", [(2 * z + y, 2 * (z ^ span) + y) for z, y in spots])

    own = lax.axis_index(("expert", "context")).astype(jnp.int32).reshape(1)
    w_first, w_second = expert_in[0], expert_out[0]
    far_weights = (swap_core(w_first), swap_core(w_second))

    rows, tile = pack(latent[0], routes.transpose(2, 0, 1), segments)
    arriving = along(latent[0], 1)
    beside = swap_core(tile)
    doc_far = beside[0, TOPK : TOPK + 1, :]
    rows, table = join(tile, beside, passed=rows)
    from_line = [rows, arriving]
    from_side = [swap_side(rows)]
    weights = tuple(load_weights(w_first, w_second, (table,))) + far_weights
    from_line[1], table = join(table, swap_side(table), passed=arriving, after=weights[:2])
    for step in range(2, line):
        from_line.append(along(from_line[-1], 1))
    from_side += [swap_side(x) for x in from_line[1:]]
    span = 1
    while 2 * span < line:
        table = join(table, flipped(table, span), after=(from_line[1],))
        span *= 2
    kept = kept_rows(own, capacity, table, flipped(table, span), (from_line[2], from_side[0]))

    def piece(step, *after):
        return run_piece(step, own, kept, router.T, from_line[step], from_side[step], weights, after)

    one, theirs = piece(1)
    one_far = swap_side(theirs)
    two, theirs = piece(2, one, from_line[3])
    two_far = swap_side(theirs)
    k_near, v_near, first = add(one, one_far, after=(two,), staged=(k_near, v_near))
    home = [along(first, line - 1)]
    three, theirs = piece(3, two, first)
    three_far = swap_side(theirs)
    second = add(two, two_far, after=(three,))
    home.append(along(second, line - 2))
    near, theirs = piece(0, three, second)
    near_far = swap_side(theirs)
    third = add(three, three_far, after=(near,))
    home.append(along(third, line - 3))
    swapped = (k_near, swap_core(k_near), v_near, swap_core(v_near))
    half = attention(0, doc_far, *swapped, after=(third,))
    attn_out = attention(1, doc_far, *swapped, before=half)
    total = near.astype(f32) + near_far.astype(f32)
    for part in home:
        total += part.astype(f32)
    return attn_out, total.astype(jnp.bfloat16)[None]


def routed_moe(latent, router, expert_in, expert_out, routes, capacity):
    tok_count = latent.shape[1]
    token_rows = latent[0]
    expert_count = router.shape[1]
    per_peer = max(2, 2 * tok_count * TOPK // expert_count)
    logits = jnp.dot(token_rows, router, preferred_element_type=jnp.float32)
    chosen_ids = routes[0]
    expert_ids = jnp.arange(expert_count, dtype=jnp.int32)
    one_hot = chosen_ids[:, :, None] == expert_ids[None, None, :]
    picked = jnp.sum(jnp.where(one_hot, logits[:, None, :], 0.0), axis=2)
    sigmas = jax.nn.sigmoid(picked)
    gates = sigmas / jnp.sum(sigmas, axis=1, keepdims=True)
    flat_hot = one_hot.reshape(tok_count * TOPK, expert_count).astype(jnp.int32)
    counts = jnp.sum(flat_hot, axis=0)
    ranks = jnp.sum((jnp.cumsum(flat_hot, axis=0) - flat_hot) * flat_hot, axis=1)
    count_rows = lax.all_gather(counts[None, :], ("expert", "context"), axis=0, tiled=True)
    own_index = lax.axis_index(("expert", "context"))
    lower_rows = jnp.arange(count_rows.shape[0], dtype=jnp.int32)[:, None] < own_index
    before = jnp.sum(jnp.where(lower_rows, count_rows, 0), axis=0)
    slots = jnp.sum(flat_hot * before[None, :], axis=1) + ranks
    limits = jnp.sum(flat_hot * capacity[None, :], axis=1)
    kept = slots < limits
    flat_ids = chosen_ids.reshape(-1)
    places = flat_ids * per_peer + ranks
    owners = jnp.arange(tok_count * TOPK, dtype=jnp.int32) // TOPK
    send_rows = (
        jnp.zeros((expert_count * per_peer, LATENT), jnp.bfloat16)
        .at[places]
        .set(token_rows[owners])
    )
    recv_rows = lax.all_to_all(
        send_rows.reshape(expert_count, per_peer, LATENT),
        ("expert", "context"),
        split_axis=0,
        concat_axis=0,
        tiled=True,
    ).reshape(expert_count * per_peer, LATENT)
    results = run_expert(recv_rows, expert_in[0], expert_out[0])
    returned = lax.all_to_all(
        results.reshape(expert_count, per_peer, LATENT),
        ("expert", "context"),
        split_axis=0,
        concat_axis=0,
        tiled=True,
    ).reshape(expert_count * per_peer, LATENT)
    gate_kept = jnp.where(kept, gates.reshape(-1), 0.0).reshape(tok_count, TOPK)
    back_rows = returned[places].reshape(tok_count, TOPK, LATENT).astype(jnp.float32)
    mixture = jnp.sum(gate_kept[:, :, None] * back_rows, axis=1)
    return mixture.astype(jnp.bfloat16).reshape(1, tok_count, LATENT)


def shards(
    query_heads,
    key_heads,
    value_heads,
    latent,
    router,
    expert_in,
    expert_out,
    routes,
    segments,
    offsets,
    capacity,
):
    swap = [(0, 1), (1, 0)]
    place = lax.axis_index("context").astype(jnp.int32).reshape(1)

    def attention(half, doc_far, *keys_and_values, **order):
        return attend(
            half, place, query_heads[0], *keys_and_values, segments, doc_far, offsets, **order
        )

    if router.shape[1] <= DENSE_EXPERTS:
        attn_out, moe_out = dense_moe(
            latent,
            router,
            expert_in,
            expert_out,
            routes,
            segments,
            capacity,
            key_heads[0],
            value_heads[0],
            attention,
        )
    else:
        doc_far = lax.ppermute(segments, "context", swap)
        k_far = lax.ppermute(key_heads[0], "context", swap)
        v_far = lax.ppermute(value_heads[0], "context", swap)
        swapped = (key_heads[0], k_far, value_heads[0], v_far)
        attn_out = attention(1, doc_far, *swapped, before=attention(0, doc_far, *swapped))
        moe_out = routed_moe(latent, router, expert_in, expert_out, routes, capacity)
    return (attn_out[None], moe_out)


def solution(mesh):
    rows = P(("groups", "expert"), "context", None)
    placed = (
        rows,
        rows,
        rows,
        rows,
        P(),
        P(("expert", "context"), None, None),
        P(("expert", "context"), None, None),
        rows,
        P(("groups", "expert"), "context"),
        P(("groups", "expert"), "context"),
        P(),
    )
    return jax.shard_map(
        shards,
        mesh=mesh,
        in_specs=placed,
        out_specs=(rows, rows),
        check_vma=False,
    )
```

```python
import functools
import math

import jax
import jax.numpy as jnp
from jax import lax
from jax.experimental import pallas as pl
from jax.experimental.pallas import tpu as pltpu
from jax.sharding import PartitionSpec as P

HEAD_DIM = 128
LATENT = 1024
TOPK = 6
DENSE_EXPERTS = 16
EXPERT_VMEM = 20 * 1024 * 1024
ATTEND_VMEM = 8 * 1024 * 1024
SMALL_VMEM = 4 * 1024 * 1024


def run_expert(rows_in, w_first, w_second):
    hidden = jax.nn.relu(jnp.dot(rows_in, w_first, preferred_element_type=jnp.float32))
    hidden = (hidden * hidden).astype(jnp.bfloat16)
    return jnp.dot(hidden, w_second, preferred_element_type=jnp.float32).astype(jnp.bfloat16)


def column_of(row):
    n = row.shape[1]
    square = jnp.broadcast_to(row.astype(jnp.float32), (n, n)).T
    return square[:, :1].astype(jnp.int32)


def attend_kernel(place_ref, q_ref, k_own, k_far, v_own, v_far, doc_own, doc_far, ahead_ref, *rest):
    out_ref = rest[-1]
    rows = q_ref.shape[0]
    heads = q_ref.shape[1] // HEAD_DIM
    here = place_ref[0] * rows
    there = (1 - place_ref[0]) * rows
    doc_query = column_of(doc_own[...])
    reach = here + lax.broadcasted_iota(jnp.int32, (rows, 1), 0) + column_of(ahead_ref[...])
    lane = lax.broadcasted_iota(jnp.int32, (1, rows), 1)
    doc_key = jnp.concatenate([doc_own[...], doc_far[...]], axis=1)
    spot = jnp.concatenate([here + lane, there + lane], axis=1)
    visible = (doc_key == doc_query) & (spot <= reach)
    scale = HEAD_DIM ** (-0.5) * math.log2(math.e)
    across = (((1,), (1,)), ((), ()))
    for head in range(heads):
        cols = slice(head * HEAD_DIM, (head + 1) * HEAD_DIM)
        keys = jnp.concatenate([k_own[:, cols], k_far[:, cols]], axis=0)
        values = jnp.concatenate([v_own[:, cols], v_far[:, cols]], axis=0)
        scores = lax.dot_general(q_ref[:, cols], keys, across, preferred_element_type=jnp.float32)
        scores = jnp.where(visible, scores * scale, -1e30)
        raw = jnp.exp2(scores - jnp.max(scores, axis=1, keepdims=True))
        share = 1.0 / jnp.sum(raw, axis=1, keepdims=True)
        mixed = jnp.dot(raw.astype(jnp.bfloat16), values, preferred_element_type=jnp.float32)
        out_ref[:, cols] = (mixed * share).astype(jnp.bfloat16)


def attend(half, place, q, k_own, k_far, v_own, v_far, doc_own, doc_far, ahead, before=None, after=()):
    rows, width = q.shape
    smem = pl.BlockSpec(memory_space=pltpu.SMEM)
    heads = pl.BlockSpec((rows, width // 2), lambda i: (0, half))
    line = pl.BlockSpec((1, rows), lambda i: (0, 0))
    extra = list(after) + ([] if before is None else [before])
    return pl.pallas_call(
        attend_kernel,
        grid=(1,),
        out_shape=jax.ShapeDtypeStruct(q.shape, jnp.bfloat16),
        in_specs=[smem] + [heads] * 5 + [line] * 3 + [pl.BlockSpec(memory_space=pl.ANY)] * len(extra),
        out_specs=heads,
        input_output_aliases={} if before is None else {8 + len(extra): 0},
        compiler_params=pltpu.CompilerParams(vmem_limit_bytes=ATTEND_VMEM),
        cost_estimate=pl.CostEstimate(
            flops=4 * rows * rows * width, bytes_accessed=6 * rows * width, transcendentals=0
        ),
    )(place, q, k_own, k_far, v_own, v_far, doc_own, doc_far, ahead, *extra)


def pack_kernel(named_any, doc_any, table_ref, named_ref, doc_ref, sems):
    loads = [
        pltpu.make_async_copy(named_any, named_ref, sems.at[0]),
        pltpu.make_async_copy(doc_any, doc_ref, sems.at[1]),
    ]
    for load in loads:
        load.start()
    for load in loads:
        load.wait()
    for k in range(TOPK):
        table_ref[0, k : k + 1, :] = named_ref[k]
    table_ref[0, TOPK : TOPK + 1, :] = doc_ref[...]
    table_ref[0, TOPK + 1 :, :] = doc_ref[...]


def pack(named, doc):
    anywhere = pl.BlockSpec(memory_space=pl.ANY)
    return pl.pallas_call(
        pack_kernel,
        out_shape=jax.ShapeDtypeStruct((1, 8, doc.shape[1]), jnp.int32),
        in_specs=[anywhere] * 2,
        out_specs=pl.BlockSpec(memory_space=pltpu.VMEM),
        scratch_shapes=[
            pltpu.VMEM(named.shape, jnp.int32),
            pltpu.VMEM(doc.shape, jnp.int32),
            pltpu.SemaphoreType.DMA((2,)),
        ],
        compiler_params=pltpu.CompilerParams(vmem_limit_bytes=SMALL_VMEM),
    )(named, doc)


def join_kernel(first_ref, second_ref, *refs):
    count = first_ref.shape[0]
    refs[-1][:count] = first_ref[...]
    refs[-1][count:] = second_ref[...]


def join(first, second, passed=None, after=()):
    vmem = pl.BlockSpec(memory_space=pltpu.VMEM)
    anywhere = pl.BlockSpec(memory_space=pl.ANY)
    table = jax.ShapeDtypeStruct((2 * first.shape[0],) + first.shape[1:], first.dtype)
    through = [] if passed is None else [passed]
    out = pl.pallas_call(
        join_kernel,
        out_shape=[jax.ShapeDtypeStruct(x.shape, x.dtype) for x in through] + [table],
        in_specs=[vmem] * 2 + [anywhere] * (len(through) + len(after)),
        out_specs=[anywhere] * len(through) + [vmem],
        input_output_aliases={2: 0} if through else {},
        compiler_params=pltpu.CompilerParams(vmem_limit_bytes=SMALL_VMEM),
    )(first, second, *through, *after)
    return out if through else out[0]


def hold_kernel(*refs):
    refs[-1][...] = jnp.zeros_like(refs[-1])


def hold(resident, after):
    vmem = pl.BlockSpec(memory_space=pltpu.VMEM)
    anywhere = pl.BlockSpec(memory_space=pl.ANY)
    return pl.pallas_call(
        hold_kernel,
        out_shape=jax.ShapeDtypeStruct((8, 128), jnp.int32),
        in_specs=[vmem] * len(resident) + [anywhere] * len(after),
        out_specs=vmem,
        compiler_params=pltpu.CompilerParams(vmem_limit_bytes=EXPERT_VMEM),
    )(*resident, *after)


def behind_kernel(*refs):
    pass


def behind(x, after):
    anywhere = pl.BlockSpec(memory_space=pl.ANY)
    return pl.pallas_call(
        behind_kernel,
        out_shape=jax.ShapeDtypeStruct(x.shape, x.dtype),
        in_specs=[anywhere] * (1 + len(after)),
        out_specs=anywhere,
        input_output_aliases={0: 0},
        compiler_params=pltpu.CompilerParams(vmem_limit_bytes=SMALL_VMEM),
    )(x, *after)


def kept_kernel(own_ref, capacity_ref, low_ref, high_ref, *refs):
    out_ref = refs[-1]
    tables = (low_ref, high_ref)
    own = own_ref[0]
    z = own // 4
    rows = low_ref.shape[2]
    sources = 2 * low_ref.shape[0]
    line = sources // 4
    upto = lax.broadcasted_iota(jnp.int32, (rows, rows), 0) <= lax.broadcasted_iota(
        jnp.int32, (rows, rows), 1
    )
    upto = jnp.where(upto, 1.0, 0.0).astype(jnp.bfloat16)
    device = lax.broadcasted_iota(jnp.int32, (sources, sources), 0) ^ own
    other = lax.broadcasted_iota(jnp.int32, (sources, sources), 1) ^ own
    lower = jnp.where(other < device, 1.0, 0.0).astype(jnp.bfloat16)
    entry = lax.broadcasted_iota(jnp.int32, (sources, rows), 0)
    named = []
    for k in range(TOPK):
        named.append(jnp.concatenate([part[:, k, :] for part in tables], axis=0))
    kept = []
    for which in range(2):
        expert = own ^ which
        mine = named[0] == expert
        for k in range(1, TOPK):
            mine |= named[k] == expert
        flags = jnp.where(mine, 1.0, 0.0)
        running = jnp.dot(flags.astype(jnp.bfloat16), upto, preferred_element_type=jnp.float32)
        totals = jnp.broadcast_to(running[:, rows - 1 :], (sources, rows)).astype(jnp.bfloat16)
        before = jnp.dot(lower, totals, preferred_element_type=jnp.float32)
        slots = before + running - flags
        limit = capacity_ref[expert].astype(jnp.float32)
        kept.append(jnp.where(mine & (slots < limit), 1, 0))
    for step in range(line):
        home = 4 * (z ^ lax.rem(z + line - step, line))
        for side in range(2):
            here = entry == home + 2 * side
            for k, part in enumerate(named + kept):
                picked = jnp.sum(jnp.where(here, part, 0), axis=0, keepdims=True)
                out_ref[2 * step + side, k : k + 1, :] = picked


def kept_rows(own, capacity, low, high, after):
    smem = pl.BlockSpec(memory_space=pltpu.SMEM)
    vmem = pl.BlockSpec(memory_space=pltpu.VMEM)
    anywhere = pl.BlockSpec(memory_space=pl.ANY)
    return pl.pallas_call(
        kept_kernel,
        out_shape=jax.ShapeDtypeStruct(low.shape, jnp.int32),
        in_specs=[smem, smem, vmem, vmem] + [anywhere] * len(after),
        out_specs=vmem,
        compiler_params=pltpu.CompilerParams(vmem_limit_bytes=SMALL_VMEM),
    )(own, capacity, low, high, *after)


def gate_columns(own, router_ref, x, kept):
    logits = lax.dot_general(
        router_ref[...], x, (((1,), (1,)), ((), ())), preferred_element_type=jnp.float32
    )
    number = lax.broadcasted_iota(jnp.int32, logits.shape, 0)
    named = number == kept[0:1]
    for k in range(1, TOPK):
        named |= number == kept[k : k + 1]
    sigma = jnp.where(named, jax.nn.sigmoid(logits), 0.0)
    gates = sigma / jnp.sum(sigma, axis=0, keepdims=True)
    lines = []
    for which in range(2):
        gate = jnp.sum(jnp.where(number == own ^ which, gates, 0.0), axis=0, keepdims=True)
        lines.append(jnp.where(kept[TOPK + which : TOPK + which + 1] > 0, gate, 0.0))
    square = jnp.concatenate(lines + [jnp.zeros((x.shape[0] - 2, x.shape[0]), jnp.float32)], axis=0)
    return square.T


def expert_kernel(
    place, own_ref, kept_ref, router_ref, xz_ref, xy_ref, w1a, w2a, w1b_any, w2b_any, *rest
):
    z_ref, y_ref, hidden_ref, mixed_ref, w1b, w2b, sems = rest[-7:]
    loads = [
        pltpu.make_async_copy(w1b_any, w1b, sems.at[0]),
        pltpu.make_async_copy(w2b_any, w2b, sems.at[1]),
    ]
    for load in loads:
        load.start()
    own = own_ref[0]
    rows = xz_ref.shape[0]
    x = jnp.concatenate([xz_ref[...], xy_ref[...]], axis=0)
    step = 512

    def enter(w1_ref):
        for first in range(0, w1_ref.shape[1], step):
            cols = slice(first, first + step)
            hidden = jnp.dot(x, w1_ref[:, cols], preferred_element_type=jnp.float32)
            hidden = jnp.maximum(hidden, 0.0)
            hidden_ref[:, cols] = (hidden * hidden).astype(jnp.bfloat16)

    enter(w1a)
    gates = [
        gate_columns(own, router_ref, x_ref[...], kept_ref[2 * place + side])
        for side, x_ref in enumerate((xz_ref, xy_ref))
    ]
    gates = [jnp.concatenate([g[:, which : which + 1] for g in gates], axis=0) for which in range(2)]
    for first in range(0, w2a.shape[1], step):
        cols = slice(first, first + step)
        result = jnp.dot(hidden_ref[...], w2a[:, cols], preferred_element_type=jnp.float32)
        mixed_ref[:, cols] = result * gates[0]
    loads[0].wait()
    enter(w1b)
    loads[1].wait()
    for first in range(0, w2b.shape[1], step):
        cols = slice(first, first + step)
        result = jnp.dot(hidden_ref[...], w2b[:, cols], preferred_element_type=jnp.float32)
        mixed = (mixed_ref[:, cols] + result * gates[1]).astype(jnp.bfloat16)
        z_ref[:, cols] = mixed[:rows]
        y_ref[:, cols] = mixed[rows:]


def run_piece(place, own, kept, router, from_line, from_side, weights, after):
    rows, width = from_line.shape
    hidden = weights[0].shape[1]
    smem = pl.BlockSpec(memory_space=pltpu.SMEM)
    vmem = pl.BlockSpec(memory_space=pltpu.VMEM)
    anywhere = pl.BlockSpec(memory_space=pl.ANY)
    piece = jax.ShapeDtypeStruct((rows, width), jnp.bfloat16)
    return pl.pallas_call(
        functools.partial(expert_kernel, place),
        out_shape=(piece, piece),
        in_specs=[smem] + [vmem] * 6 + [anywhere] * (2 + len(after)),
        out_specs=(vmem, vmem),
        scratch_shapes=[
            pltpu.VMEM((2 * rows, hidden), jnp.bfloat16),
            pltpu.VMEM((2 * rows, width), jnp.float32),
            pltpu.VMEM(weights[2].shape, jnp.bfloat16),
            pltpu.VMEM(weights[3].shape, jnp.bfloat16),
            pltpu.SemaphoreType.DMA((2,)),
        ],
        compiler_params=pltpu.CompilerParams(vmem_limit_bytes=EXPERT_VMEM),
        cost_estimate=pl.CostEstimate(
            flops=16 * rows * width * hidden,
            bytes_accessed=8 * rows * width,
            transcendentals=0,
        ),
    )(own, kept, router, from_line, from_side, *weights, *after)


def add_kernel(count, first_ref, second_ref, *refs):
    total = first_ref[...].astype(jnp.float32) + second_ref[...].astype(jnp.float32)
    outs = refs[len(refs) - count - 1 :]
    outs[-1][...] = total.astype(jnp.bfloat16)
    for index in range(count):
        outs[index][...] = refs[index][...]


def add(first, second, after=(), staged=()):
    vmem = pl.BlockSpec(memory_space=pltpu.VMEM)
    anywhere = pl.BlockSpec(memory_space=pl.ANY)
    out = pl.pallas_call(
        functools.partial(add_kernel, len(staged)),
        out_shape=[jax.ShapeDtypeStruct(x.shape, x.dtype) for x in staged]
        + [jax.ShapeDtypeStruct(first.shape, first.dtype)],
        in_specs=[vmem] * (2 + len(staged)) + [anywhere] * len(after),
        out_specs=[vmem] * (1 + len(staged)),
        compiler_params=pltpu.CompilerParams(vmem_limit_bytes=SMALL_VMEM),
        cost_estimate=pl.CostEstimate(flops=first.size, bytes_accessed=first.size, transcendentals=0),
    )(first, second, *staged, *after)
    return out if staged else out[0]


def dense_moe(latent, router, expert_in, expert_out, routes, segments, capacity, k_near, v_near, attention):
    f32 = jnp.float32
    line = router.shape[1] // 4
    spots = [(z, y) for z in range(line) for y in range(2)]
    sibling = [(0, 1), (1, 0)]
    across = [(2 * z + y, 2 * z + 1 - y) for z, y in spots]

    def swap_core(x):
        return lax.ppermute(x, "context", sibling)

    def swap_side(x):
        return lax.ppermute(x, "expert", across)

    def along(x, step):
        return lax.ppermute(x, "expert", [(2 * z + y, 2 * ((z + step) % line) + y) for z, y in spots])

    def flipped(x, span):
        return lax.ppermute(x, "expert", [(2 * z + y, 2 * (z ^ span) + y) for z, y in spots])

    own = lax.axis_index(("expert", "context")).astype(jnp.int32).reshape(1)
    own_weights = (expert_in[0], expert_out[0])
    weights = own_weights + (swap_core(own_weights[0]), swap_core(own_weights[1]))

    arriving, beside_own = along(latent[0], 1), swap_side(latent[0])
    tile = pack(routes.transpose(2, 0, 1), segments)
    beside = swap_core(tile)
    doc_far = beside[0, TOPK : TOPK + 1, :]
    table = join(tile, beside)
    arriving, table = join(table, swap_side(table), passed=arriving, after=(beside_own,))
    flip = flipped(table, 1)
    from_line = [latent[0], arriving, along(arriving, 1)]
    from_side = [beside_own, swap_side(arriving)]
    table = join(table, flip, after=(hold(own_weights, (table,)),))
    flip = flipped(table, 2)
    from_line[2] = behind(from_line[2], (table,))
    for step in range(3, line):
        from_line.append(along(from_line[-1], 1))
    from_side += [swap_side(x) for x in from_line[2:]]
    kept = kept_rows(own, capacity, table, flip, (from_line[2], from_side[1]))

    def piece(step, *after):
        return run_piece(step, own, kept, router.T, from_line[step], from_side[step], weights, after)

    one, theirs = piece(1)
    one_far = swap_side(theirs)
    two, theirs = piece(2, one, from_line[3])
    two_far = swap_side(theirs)
    k_near, v_near, first = add(one, one_far, after=(two,), staged=(k_near, v_near))
    home = [along(first, line - 1)]
    three, theirs = piece(3, two, first)
    three_far = swap_side(theirs)
    second = add(two, two_far, after=(three,))
    home.append(along(second, line - 2))
    near, theirs = piece(0, three, second)
    near_far = swap_side(theirs)
    third = add(three, three_far, after=(near,))
    home.append(along(third, line - 3))
    swapped = (k_near, swap_core(k_near), v_near, swap_core(v_near))
    half = attention(0, doc_far, *swapped, after=(third,))
    attn_out = attention(1, doc_far, *swapped, before=half)
    total = near.astype(f32) + near_far.astype(f32)
    for part in home:
        total += part.astype(f32)
    return attn_out, total.astype(jnp.bfloat16)[None]


def routed_moe(latent, router, expert_in, expert_out, routes, capacity):
    tok_count = latent.shape[1]
    token_rows = latent[0]
    expert_count = router.shape[1]
    per_peer = max(2, 2 * tok_count * TOPK // expert_count)
    logits = jnp.dot(token_rows, router, preferred_element_type=jnp.float32)
    chosen_ids = routes[0]
    expert_ids = jnp.arange(expert_count, dtype=jnp.int32)
    one_hot = chosen_ids[:, :, None] == expert_ids[None, None, :]
    picked = jnp.sum(jnp.where(one_hot, logits[:, None, :], 0.0), axis=2)
    sigmas = jax.nn.sigmoid(picked)
    gates = sigmas / jnp.sum(sigmas, axis=1, keepdims=True)
    flat_hot = one_hot.reshape(tok_count * TOPK, expert_count).astype(jnp.int32)
    counts = jnp.sum(flat_hot, axis=0)
    ranks = jnp.sum((jnp.cumsum(flat_hot, axis=0) - flat_hot) * flat_hot, axis=1)
    count_rows = lax.all_gather(counts[None, :], ("expert", "context"), axis=0, tiled=True)
    own_index = lax.axis_index(("expert", "context"))
    lower_rows = jnp.arange(count_rows.shape[0], dtype=jnp.int32)[:, None] < own_index
    before = jnp.sum(jnp.where(lower_rows, count_rows, 0), axis=0)
    slots = jnp.sum(flat_hot * before[None, :], axis=1) + ranks
    limits = jnp.sum(flat_hot * capacity[None, :], axis=1)
    kept = slots < limits
    flat_ids = chosen_ids.reshape(-1)
    places = flat_ids * per_peer + ranks
    owners = jnp.arange(tok_count * TOPK, dtype=jnp.int32) // TOPK
    send_rows = (
        jnp.zeros((expert_count * per_peer, LATENT), jnp.bfloat16)
        .at[places]
        .set(token_rows[owners])
    )
    recv_rows = lax.all_to_all(
        send_rows.reshape(expert_count, per_peer, LATENT),
        ("expert", "context"),
        split_axis=0,
        concat_axis=0,
        tiled=True,
    ).reshape(expert_count * per_peer, LATENT)
    results = run_expert(recv_rows, expert_in[0], expert_out[0])
    returned = lax.all_to_all(
        results.reshape(expert_count, per_peer, LATENT),
        ("expert", "context"),
        split_axis=0,
        concat_axis=0,
        tiled=True,
    ).reshape(expert_count * per_peer, LATENT)
    gate_kept = jnp.where(kept, gates.reshape(-1), 0.0).reshape(tok_count, TOPK)
    back_rows = returned[places].reshape(tok_count, TOPK, LATENT).astype(jnp.float32)
    mixture = jnp.sum(gate_kept[:, :, None] * back_rows, axis=1)
    return mixture.astype(jnp.bfloat16).reshape(1, tok_count, LATENT)


def shards(
    query_heads,
    key_heads,
    value_heads,
    latent,
    router,
    expert_in,
    expert_out,
    routes,
    segments,
    offsets,
    capacity,
):
    swap = [(0, 1), (1, 0)]
    place = lax.axis_index("context").astype(jnp.int32).reshape(1)

    def attention(half, doc_far, *keys_and_values, **order):
        return attend(
            half, place, query_heads[0], *keys_and_values, segments, doc_far, offsets, **order
        )

    if router.shape[1] <= DENSE_EXPERTS:
        attn_out, moe_out = dense_moe(
            latent,
            router,
            expert_in,
            expert_out,
            routes,
            segments,
            capacity,
            key_heads[0],
            value_heads[0],
            attention,
        )
    else:
        doc_far = lax.ppermute(segments, "context", swap)
        k_far = lax.ppermute(key_heads[0], "context", swap)
        v_far = lax.ppermute(value_heads[0], "context", swap)
        swapped = (key_heads[0], k_far, value_heads[0], v_far)
        attn_out = attention(1, doc_far, *swapped, before=attention(0, doc_far, *swapped))
        moe_out = routed_moe(latent, router, expert_in, expert_out, routes, capacity)
    return (attn_out[None], moe_out)


def solution(mesh):
    rows = P(("groups", "expert"), "context", None)
    placed = (
        rows,
        rows,
        rows,
        rows,
        P(),
        P(("expert", "context"), None, None),
        P(("expert", "context"), None, None),
        rows,
        P(("groups", "expert"), "context"),
        P(("groups", "expert"), "context"),
        P(),
    )
    return jax.shard_map(
        shards,
        mesh=mesh,
        in_specs=placed,
        out_specs=(rows, rows),
        check_vma=False,
    )
```

```python
import functools
import math

import jax
import jax.numpy as jnp
from jax import lax
from jax.experimental import pallas as pl
from jax.experimental.pallas import tpu as pltpu
from jax.sharding import PartitionSpec as P

HEAD_DIM = 128
LATENT = 1024
TOPK = 6
DENSE_EXPERTS = 16
EXPERT_VMEM = 26 * 1024 * 1024
FIRST_VMEM = 40 * 1024 * 1024
ATTEND_VMEM = 8 * 1024 * 1024
SMALL_VMEM = 4 * 1024 * 1024
WINDOW = 4


def run_expert(rows_in, w_first, w_second):
    hidden = jax.nn.relu(jnp.dot(rows_in, w_first, preferred_element_type=jnp.float32))
    hidden = (hidden * hidden).astype(jnp.bfloat16)
    return jnp.dot(hidden, w_second, preferred_element_type=jnp.float32).astype(jnp.bfloat16)


def column_of(row):
    n = row.shape[1]
    square = jnp.broadcast_to(row.astype(jnp.float32), (n, n)).T
    return square[:, :1].astype(jnp.int32)


def attend_kernel(place_ref, q_ref, k_own, k_far, v_own, v_far, doc_own, doc_far, ahead_ref, *rest):
    out_ref = rest[-1]
    rows = q_ref.shape[0]
    heads = q_ref.shape[1] // HEAD_DIM
    here = place_ref[0] * rows
    there = (1 - place_ref[0]) * rows
    doc_query = column_of(doc_own[...])
    reach = here + lax.broadcasted_iota(jnp.int32, (rows, 1), 0) + column_of(ahead_ref[...])
    lane = lax.broadcasted_iota(jnp.int32, (1, rows), 1)
    doc_key = jnp.concatenate([doc_own[...], doc_far[...]], axis=1)
    spot = jnp.concatenate([here + lane, there + lane], axis=1)
    visible = (doc_key == doc_query) & (spot <= reach)
    scale = HEAD_DIM ** (-0.5) * math.log2(math.e)
    across = (((1,), (1,)), ((), ()))
    for head in range(heads):
        cols = slice(head * HEAD_DIM, (head + 1) * HEAD_DIM)
        keys = jnp.concatenate([k_own[:, cols], k_far[:, cols]], axis=0)
        values = jnp.concatenate([v_own[:, cols], v_far[:, cols]], axis=0)
        scores = lax.dot_general(q_ref[:, cols], keys, across, preferred_element_type=jnp.float32)
        scores = jnp.where(visible, scores * scale, -1e30)
        raw = jnp.exp2(scores - jnp.max(scores, axis=1, keepdims=True))
        share = 1.0 / jnp.sum(raw, axis=1, keepdims=True)
        mixed = jnp.dot(raw.astype(jnp.bfloat16), values, preferred_element_type=jnp.float32)
        out_ref[:, cols] = (mixed * share).astype(jnp.bfloat16)


def attend(half, place, q, k_own, k_far, v_own, v_far, doc_own, doc_far, ahead, before=None, after=()):
    rows, width = q.shape
    smem = pl.BlockSpec(memory_space=pltpu.SMEM)
    heads = pl.BlockSpec((rows, width // 2), lambda i: (0, half))
    line = pl.BlockSpec((1, rows), lambda i: (0, 0))
    extra = list(after) + ([] if before is None else [before])
    return pl.pallas_call(
        attend_kernel,
        grid=(1,),
        out_shape=jax.ShapeDtypeStruct(q.shape, jnp.bfloat16),
        in_specs=[smem] + [heads] * 5 + [line] * 3 + [pl.BlockSpec(memory_space=pl.ANY)] * len(extra),
        out_specs=heads,
        input_output_aliases={} if before is None else {8 + len(extra): 0},
        compiler_params=pltpu.CompilerParams(vmem_limit_bytes=ATTEND_VMEM),
        cost_estimate=pl.CostEstimate(
            flops=4 * rows * rows * width, bytes_accessed=6 * rows * width, transcendentals=0
        ),
    )(place, q, k_own, k_far, v_own, v_far, doc_own, doc_far, ahead, *extra)


def pack_kernel(named_any, doc_any, table_ref, named_ref, doc_ref, sems):
    loads = [
        pltpu.make_async_copy(named_any, named_ref, sems.at[0]),
        pltpu.make_async_copy(doc_any, doc_ref, sems.at[1]),
    ]
    for load in loads:
        load.start()
    for load in loads:
        load.wait()
    for k in range(TOPK):
        table_ref[0, k : k + 1, :] = named_ref[k]
    table_ref[0, TOPK : TOPK + 1, :] = doc_ref[...]
    table_ref[0, TOPK + 1 :, :] = doc_ref[...]


def pack(named, doc):
    anywhere = pl.BlockSpec(memory_space=pl.ANY)
    return pl.pallas_call(
        pack_kernel,
        out_shape=jax.ShapeDtypeStruct((1, 8, doc.shape[1]), jnp.int32),
        in_specs=[anywhere] * 2,
        out_specs=pl.BlockSpec(memory_space=pltpu.VMEM),
        scratch_shapes=[
            pltpu.VMEM(named.shape, jnp.int32),
            pltpu.VMEM(doc.shape, jnp.int32),
            pltpu.SemaphoreType.DMA((2,)),
        ],
        compiler_params=pltpu.CompilerParams(vmem_limit_bytes=SMALL_VMEM),
    )(named, doc)


def join_kernel(first_ref, second_ref, *refs):
    count = first_ref.shape[0]
    refs[-1][:count] = first_ref[...]
    refs[-1][count:] = second_ref[...]


def copy_join_kernel(first_ref, second_ref, rows_ref, copy_ref, out_ref):
    join_kernel(first_ref, second_ref, out_ref)
    copy_ref[...] = rows_ref[...]


def join(first, second, passed=None, after=(), copy=False):
    vmem = pl.BlockSpec(memory_space=pltpu.VMEM)
    anywhere = pl.BlockSpec(memory_space=pl.ANY)
    table = jax.ShapeDtypeStruct((2 * first.shape[0],) + first.shape[1:], first.dtype)
    through = [] if passed is None else [passed]
    place = vmem if copy else anywhere
    out = pl.pallas_call(
        copy_join_kernel if copy else join_kernel,
        out_shape=[jax.ShapeDtypeStruct(x.shape, x.dtype) for x in through] + [table],
        in_specs=[vmem] * 2 + [place] * len(through) + [anywhere] * len(after),
        out_specs=[place] * len(through) + [vmem],
        input_output_aliases={2: 0} if through and not copy else {},
        compiler_params=pltpu.CompilerParams(vmem_limit_bytes=SMALL_VMEM),
    )(first, second, *through, *after)
    return out if through else out[0]


def behind_kernel(*refs):
    pass


def behind(x, after):
    anywhere = pl.BlockSpec(memory_space=pl.ANY)
    return pl.pallas_call(
        behind_kernel,
        out_shape=jax.ShapeDtypeStruct(x.shape, x.dtype),
        in_specs=[anywhere] * (1 + len(after)),
        out_specs=anywhere,
        input_output_aliases={0: 0},
        compiler_params=pltpu.CompilerParams(vmem_limit_bytes=SMALL_VMEM),
    )(x, *after)


def kept_kernel(own_ref, capacity_ref, low_ref, high_ref, *refs):
    out_ref = refs[-2]
    tables = (low_ref, high_ref)
    own = own_ref[0]
    z = own // 4
    rows = low_ref.shape[2]
    sources = 2 * low_ref.shape[0]
    line = sources // 4
    upto = lax.broadcasted_iota(jnp.int32, (rows, rows), 0) <= lax.broadcasted_iota(
        jnp.int32, (rows, rows), 1
    )
    upto = jnp.where(upto, 1.0, 0.0).astype(jnp.bfloat16)
    device = lax.broadcasted_iota(jnp.int32, (sources, sources), 0) ^ own
    other = lax.broadcasted_iota(jnp.int32, (sources, sources), 1) ^ own
    lower = jnp.where(other < device, 1.0, 0.0).astype(jnp.bfloat16)
    entry = lax.broadcasted_iota(jnp.int32, (sources, rows), 0)
    named = []
    for k in range(TOPK):
        named.append(jnp.concatenate([part[:, k, :] for part in tables], axis=0))
    kept = []
    for which in range(2):
        expert = own ^ which
        mine = named[0] == expert
        for k in range(1, TOPK):
            mine |= named[k] == expert
        flags = jnp.where(mine, 1.0, 0.0)
        running = jnp.dot(flags.astype(jnp.bfloat16), upto, preferred_element_type=jnp.float32)
        totals = jnp.broadcast_to(running[:, rows - 1 :], (sources, rows)).astype(jnp.bfloat16)
        before = jnp.dot(lower, totals, preferred_element_type=jnp.float32)
        slots = before + running - flags
        limit = capacity_ref[expert].astype(jnp.float32)
        kept.append(jnp.where(mine & (slots < limit), 1, 0))
    for step in range(line):
        home = 4 * (z ^ lax.rem(z + line - step, line))
        for side in range(2):
            here = entry == home + 2 * side
            for k, part in enumerate(named + kept):
                picked = jnp.sum(jnp.where(here, part, 0), axis=0, keepdims=True)
                out_ref[2 * step + side, k : k + 1, :] = picked


def kept_rows(own, capacity, low, high, passed, after):
    smem = pl.BlockSpec(memory_space=pltpu.SMEM)
    vmem = pl.BlockSpec(memory_space=pltpu.VMEM)
    anywhere = pl.BlockSpec(memory_space=pl.ANY)
    return pl.pallas_call(
        kept_kernel,
        out_shape=(
            jax.ShapeDtypeStruct(low.shape, jnp.int32),
            jax.ShapeDtypeStruct(passed.shape, passed.dtype),
        ),
        in_specs=[smem, smem, vmem, vmem] + [anywhere] * (1 + len(after)),
        out_specs=(vmem, anywhere),
        input_output_aliases={4: 1},
        compiler_params=pltpu.CompilerParams(vmem_limit_bytes=SMALL_VMEM),
    )(own, capacity, low, high, passed, *after)


def gate_columns(own, router_ref, x, kept):
    logits = lax.dot_general(
        router_ref[...], x, (((1,), (1,)), ((), ())), preferred_element_type=jnp.float32
    )
    number = lax.broadcasted_iota(jnp.int32, logits.shape, 0)
    named = number == kept[0:1]
    for k in range(1, TOPK):
        named |= number == kept[k : k + 1]
    sigma = jnp.where(named, jax.nn.sigmoid(logits), 0.0)
    gates = sigma / jnp.sum(sigma, axis=0, keepdims=True)
    lines = []
    for which in range(2):
        gate = jnp.sum(jnp.where(number == own ^ which, gates, 0.0), axis=0, keepdims=True)
        lines.append(jnp.where(kept[TOPK + which : TOPK + which + 1] > 0, gate, 0.0))
    square = jnp.concatenate(lines + [jnp.zeros((x.shape[0] - 2, x.shape[0]), jnp.float32)], axis=0)
    return square.T


def expert_kernel(place, first, own_ref, kept_ref, router_ref, xz_ref, xy_ref, *refs):
    step = 512
    if first:
        sources = refs[:4]
        z_ref, y_ref, *weights, hidden_ref, mixed_ref, sems = refs[-9:]
    else:
        weights = refs[:4]
        z_ref, y_ref, hidden_ref, mixed_ref = refs[-4:]
    chunks = [(w, c) for w in range(4) for c in range(0, weights[w].shape[1], step)]

    def load(index):
        which, column = chunks[index]
        cols = pl.ds(column, step)
        return pltpu.make_async_copy(
            sources[which].at[:, cols], weights[which].at[:, cols], sems.at[index]
        )

    def ready(which, column):
        if first:
            index = chunks.index((which, column))
            load(index).wait()
            if index + WINDOW < len(chunks):
                load(index + WINDOW).start()

    if first:
        for index in range(WINDOW):
            load(index).start()
    own = own_ref[0]
    rows = xz_ref.shape[0]
    x = jnp.concatenate([xz_ref[...], xy_ref[...]], axis=0)
    gates = [
        gate_columns(own, router_ref, x_ref[...], kept_ref[2 * place + side])
        for side, x_ref in enumerate((xz_ref, xy_ref))
    ]
    for which in range(2):
        gate = jnp.concatenate([g[:, which : which + 1] for g in gates], axis=0)
        w1_ref, w2_ref = weights[2 * which], weights[2 * which + 1]
        for column in range(0, w1_ref.shape[1], step):
            cols = slice(column, column + step)
            ready(2 * which, column)
            hidden = jnp.dot(x, w1_ref[:, cols], preferred_element_type=jnp.float32)
            hidden = jnp.maximum(hidden, 0.0)
            hidden_ref[which, :, cols] = (hidden * hidden).astype(jnp.bfloat16)
        for column in range(0, w2_ref.shape[1], step):
            cols = slice(column, column + step)
            ready(2 * which + 1, column)
            result = jnp.dot(hidden_ref[which], w2_ref[:, cols], preferred_element_type=jnp.float32)
            if which == 0:
                mixed_ref[:, cols] = result * gate
            else:
                mixed = (mixed_ref[:, cols] + result * gate).astype(jnp.bfloat16)
                z_ref[:, cols] = mixed[:rows]
                y_ref[:, cols] = mixed[rows:]


def run_piece(place, first, own, kept, router, from_line, from_side, weights, after):
    rows, width = from_line.shape
    hidden = weights[0].shape[1]
    smem = pl.BlockSpec(memory_space=pltpu.SMEM)
    vmem = pl.BlockSpec(memory_space=pltpu.VMEM)
    hbm = pl.BlockSpec(memory_space=pltpu.HBM)
    anywhere = pl.BlockSpec(memory_space=pl.ANY)
    piece = jax.ShapeDtypeStruct((rows, width), jnp.bfloat16)
    staged = [pltpu.VMEM(w.shape, w.dtype) for w in weights] if first else []
    scratch = [
        pltpu.VMEM((2, 2 * rows, hidden), jnp.bfloat16),
        pltpu.VMEM((2 * rows, width), jnp.float32),
    ]
    if first:
        scratch.append(pltpu.SemaphoreType.DMA((4 * (hidden + width) // 1024,)))
    return pl.pallas_call(
        functools.partial(expert_kernel, place, first),
        out_shape=[piece, piece] + staged,
        in_specs=[smem] + [vmem] * 4 + [hbm if first else vmem] * 4 + [anywhere] * len(after),
        out_specs=[vmem] * (2 + len(staged)),
        scratch_shapes=scratch,
        compiler_params=pltpu.CompilerParams(vmem_limit_bytes=FIRST_VMEM if first else EXPERT_VMEM),
        cost_estimate=pl.CostEstimate(
            flops=16 * rows * width * hidden,
            bytes_accessed=8 * rows * width,
            transcendentals=0,
        ),
    )(own, kept, router, from_line, from_side, *weights, *after)


def add_kernel(count, first_ref, second_ref, *refs):
    total = first_ref[...].astype(jnp.float32) + second_ref[...].astype(jnp.float32)
    outs = refs[len(refs) - count - 1 :]
    outs[-1][...] = total.astype(jnp.bfloat16)
    for index in range(count):
        outs[index][...] = refs[index][...]


def add(first, second, after=(), staged=()):
    vmem = pl.BlockSpec(memory_space=pltpu.VMEM)
    anywhere = pl.BlockSpec(memory_space=pl.ANY)
    out = pl.pallas_call(
        functools.partial(add_kernel, len(staged)),
        out_shape=[jax.ShapeDtypeStruct(x.shape, x.dtype) for x in staged]
        + [jax.ShapeDtypeStruct(first.shape, first.dtype)],
        in_specs=[vmem] * (2 + len(staged)) + [anywhere] * len(after),
        out_specs=[vmem] * (1 + len(staged)),
        compiler_params=pltpu.CompilerParams(vmem_limit_bytes=SMALL_VMEM),
        cost_estimate=pl.CostEstimate(flops=first.size, bytes_accessed=first.size, transcendentals=0),
    )(first, second, *staged, *after)
    return out if staged else out[0]


def dense_moe(latent, router, expert_in, expert_out, routes, segments, capacity, k_near, v_near, attention):
    f32 = jnp.float32
    line = router.shape[1] // 4
    spots = [(z, y) for z in range(line) for y in range(2)]
    sibling = [(0, 1), (1, 0)]
    across = [(2 * z + y, 2 * z + 1 - y) for z, y in spots]

    def swap_core(x):
        return lax.ppermute(x, "context", sibling)

    def swap_side(x):
        return lax.ppermute(x, "expert", across)

    def along(x, step):
        return lax.ppermute(x, "expert", [(2 * z + y, 2 * ((z + step) % line) + y) for z, y in spots])

    def flipped(x, span):
        return lax.ppermute(x, "expert", [(2 * z + y, 2 * (z ^ span) + y) for z, y in spots])

    own = lax.axis_index(("expert", "context")).astype(jnp.int32).reshape(1)
    own_weights = (expert_in[0], expert_out[0])
    weights = own_weights + (swap_core(own_weights[0]), swap_core(own_weights[1]))

    arriving, beside_own = along(latent[0], 1), swap_side(latent[0])
    tile = pack(routes.transpose(2, 0, 1), segments)
    beside = swap_core(tile)
    doc_far = beside[0, TOPK : TOPK + 1, :]
    table = join(tile, beside)
    arriving, table = join(table, swap_side(table), passed=arriving, after=(beside_own,))
    from_side = [beside_own, swap_side(arriving)]
    passed, table = join(table, flipped(table, 1), passed=arriving, copy=True)
    flip = flipped(table, 2)
    kept, passed = kept_rows(own, capacity, table, flip, along(passed, 1), (from_side[1],))
    from_line = [latent[0], arriving, passed]
    from_side.append(swap_side(passed))
    last = along(passed, 1)

    def piece(step, weights, *after):
        return run_piece(
            step, step == 1, own, kept, router.T, from_line[step], from_side[step], weights, after
        )

    one, theirs, *weights = piece(1, weights)
    one_far = swap_side(theirs)
    last = behind(last, (one,))
    from_line.append(last)
    from_side.append(swap_side(last))
    two, theirs = piece(2, weights, one, from_line[3])
    two_far = swap_side(theirs)
    k_near, v_near, first = add(one, one_far, after=(two,), staged=(k_near, v_near))
    home = [along(first, line - 1)]
    three, theirs = piece(3, weights, two, first)
    three_far = swap_side(theirs)
    second = add(two, two_far, after=(three,))
    home.append(along(second, line - 2))
    near, theirs = piece(0, weights, three, second)
    near_far = swap_side(theirs)
    third = add(three, three_far, after=(near,))
    home.append(along(third, line - 3))
    swapped = (k_near, swap_core(k_near), v_near, swap_core(v_near))
    half = attention(0, doc_far, *swapped, after=(third,))
    attn_out = attention(1, doc_far, *swapped, before=half)
    total = near.astype(f32) + near_far.astype(f32)
    for part in home:
        total += part.astype(f32)
    return attn_out, total.astype(jnp.bfloat16)[None]


def routed_moe(latent, router, expert_in, expert_out, routes, capacity):
    tok_count = latent.shape[1]
    token_rows = latent[0]
    expert_count = router.shape[1]
    per_peer = max(2, 2 * tok_count * TOPK // expert_count)
    logits = jnp.dot(token_rows, router, preferred_element_type=jnp.float32)
    chosen_ids = routes[0]
    expert_ids = jnp.arange(expert_count, dtype=jnp.int32)
    one_hot = chosen_ids[:, :, None] == expert_ids[None, None, :]
    picked = jnp.sum(jnp.where(one_hot, logits[:, None, :], 0.0), axis=2)
    sigmas = jax.nn.sigmoid(picked)
    gates = sigmas / jnp.sum(sigmas, axis=1, keepdims=True)
    flat_hot = one_hot.reshape(tok_count * TOPK, expert_count).astype(jnp.int32)
    counts = jnp.sum(flat_hot, axis=0)
    ranks = jnp.sum((jnp.cumsum(flat_hot, axis=0) - flat_hot) * flat_hot, axis=1)
    count_rows = lax.all_gather(counts[None, :], ("expert", "context"), axis=0, tiled=True)
    own_index = lax.axis_index(("expert", "context"))
    lower_rows = jnp.arange(count_rows.shape[0], dtype=jnp.int32)[:, None] < own_index
    before = jnp.sum(jnp.where(lower_rows, count_rows, 0), axis=0)
    slots = jnp.sum(flat_hot * before[None, :], axis=1) + ranks
    limits = jnp.sum(flat_hot * capacity[None, :], axis=1)
    kept = slots < limits
    flat_ids = chosen_ids.reshape(-1)
    places = flat_ids * per_peer + ranks
    owners = jnp.arange(tok_count * TOPK, dtype=jnp.int32) // TOPK
    send_rows = (
        jnp.zeros((expert_count * per_peer, LATENT), jnp.bfloat16)
        .at[places]
        .set(token_rows[owners])
    )
    recv_rows = lax.all_to_all(
        send_rows.reshape(expert_count, per_peer, LATENT),
        ("expert", "context"),
        split_axis=0,
        concat_axis=0,
        tiled=True,
    ).reshape(expert_count * per_peer, LATENT)
    results = run_expert(recv_rows, expert_in[0], expert_out[0])
    returned = lax.all_to_all(
        results.reshape(expert_count, per_peer, LATENT),
        ("expert", "context"),
        split_axis=0,
        concat_axis=0,
        tiled=True,
    ).reshape(expert_count * per_peer, LATENT)
    gate_kept = jnp.where(kept, gates.reshape(-1), 0.0).reshape(tok_count, TOPK)
    back_rows = returned[places].reshape(tok_count, TOPK, LATENT).astype(jnp.float32)
    mixture = jnp.sum(gate_kept[:, :, None] * back_rows, axis=1)
    return mixture.astype(jnp.bfloat16).reshape(1, tok_count, LATENT)


def shards(
    query_heads,
    key_heads,
    value_heads,
    latent,
    router,
    expert_in,
    expert_out,
    routes,
    segments,
    offsets,
    capacity,
):
    swap = [(0, 1), (1, 0)]
    place = lax.axis_index("context").astype(jnp.int32).reshape(1)

    def attention(half, doc_far, *keys_and_values, **order):
        return attend(
            half, place, query_heads[0], *keys_and_values, segments, doc_far, offsets, **order
        )

    if router.shape[1] <= DENSE_EXPERTS:
        attn_out, moe_out = dense_moe(
            latent,
            router,
            expert_in,
            expert_out,
            routes,
            segments,
            capacity,
            key_heads[0],
            value_heads[0],
            attention,
        )
    else:
        doc_far = lax.ppermute(segments, "context", swap)
        k_far = lax.ppermute(key_heads[0], "context", swap)
        v_far = lax.ppermute(value_heads[0], "context", swap)
        swapped = (key_heads[0], k_far, value_heads[0], v_far)
        attn_out = attention(1, doc_far, *swapped, before=attention(0, doc_far, *swapped))
        moe_out = routed_moe(latent, router, expert_in, expert_out, routes, capacity)
    return (attn_out[None], moe_out)


def solution(mesh):
    rows = P(("groups", "expert"), "context", None)
    placed = (
        rows,
        rows,
        rows,
        rows,
        P(),
        P(("expert", "context"), None, None),
        P(("expert", "context"), None, None),
        rows,
        P(("groups", "expert"), "context"),
        P(("groups", "expert"), "context"),
        P(),
    )
    return jax.shard_map(
        shards,
        mesh=mesh,
        in_specs=placed,
        out_specs=(rows, rows),
        check_vma=False,
    )
```

```python
import functools
import math

import jax
import jax.numpy as jnp
from jax import lax
from jax.experimental import pallas as pl
from jax.experimental.pallas import tpu as pltpu
from jax.sharding import PartitionSpec as P

HEAD_DIM = 128
LATENT = 1024
TOPK = 6
DENSE_EXPERTS = 16
EXPERT_VMEM = 26 * 1024 * 1024
FIRST_VMEM = 26 * 1024 * 1024
LOAD_VMEM = 44 * 1024 * 1024
ATTEND_VMEM = 8 * 1024 * 1024
SMALL_VMEM = 4 * 1024 * 1024
WINDOW = 4


def run_expert(rows_in, w_first, w_second):
    hidden = jax.nn.relu(jnp.dot(rows_in, w_first, preferred_element_type=jnp.float32))
    hidden = (hidden * hidden).astype(jnp.bfloat16)
    return jnp.dot(hidden, w_second, preferred_element_type=jnp.float32).astype(jnp.bfloat16)


def column_of(row):
    n = row.shape[1]
    square = jnp.broadcast_to(row.astype(jnp.float32), (n, n)).T
    return square[:, :1].astype(jnp.int32)


def attend_kernel(place_ref, q_ref, k_own, k_far, v_own, v_far, doc_own, doc_far, ahead_ref, *rest):
    out_ref = rest[-1]
    rows = q_ref.shape[0]
    heads = q_ref.shape[1] // HEAD_DIM
    here = place_ref[0] * rows
    there = (1 - place_ref[0]) * rows
    doc_query = column_of(doc_own[...])
    reach = here + lax.broadcasted_iota(jnp.int32, (rows, 1), 0) + column_of(ahead_ref[...])
    lane = lax.broadcasted_iota(jnp.int32, (1, rows), 1)
    doc_key = jnp.concatenate([doc_own[...], doc_far[...]], axis=1)
    spot = jnp.concatenate([here + lane, there + lane], axis=1)
    visible = (doc_key == doc_query) & (spot <= reach)
    scale = HEAD_DIM ** (-0.5) * math.log2(math.e)
    across = (((1,), (1,)), ((), ()))
    for head in range(heads):
        cols = slice(head * HEAD_DIM, (head + 1) * HEAD_DIM)
        keys = jnp.concatenate([k_own[:, cols], k_far[:, cols]], axis=0)
        values = jnp.concatenate([v_own[:, cols], v_far[:, cols]], axis=0)
        scores = lax.dot_general(q_ref[:, cols], keys, across, preferred_element_type=jnp.float32)
        scores = jnp.where(visible, scores * scale, -1e30)
        raw = jnp.exp2(scores - jnp.max(scores, axis=1, keepdims=True))
        share = 1.0 / jnp.sum(raw, axis=1, keepdims=True)
        mixed = jnp.dot(raw.astype(jnp.bfloat16), values, preferred_element_type=jnp.float32)
        out_ref[:, cols] = (mixed * share).astype(jnp.bfloat16)


def attend(half, place, q, k_own, k_far, v_own, v_far, doc_own, doc_far, ahead, before=None, after=()):
    rows, width = q.shape
    smem = pl.BlockSpec(memory_space=pltpu.SMEM)
    heads = pl.BlockSpec((rows, width // 2), lambda i: (0, half))
    line = pl.BlockSpec((1, rows), lambda i: (0, 0))
    extra = list(after) + ([] if before is None else [before])
    return pl.pallas_call(
        attend_kernel,
        grid=(1,),
        out_shape=jax.ShapeDtypeStruct(q.shape, jnp.bfloat16),
        in_specs=[smem] + [heads] * 5 + [line] * 3 + [pl.BlockSpec(memory_space=pl.ANY)] * len(extra),
        out_specs=heads,
        input_output_aliases={} if before is None else {8 + len(extra): 0},
        compiler_params=pltpu.CompilerParams(vmem_limit_bytes=ATTEND_VMEM),
        cost_estimate=pl.CostEstimate(
            flops=4 * rows * rows * width, bytes_accessed=6 * rows * width, transcendentals=0
        ),
    )(place, q, k_own, k_far, v_own, v_far, doc_own, doc_far, ahead, *extra)


def pack_kernel(named_any, doc_any, table_ref, named_ref, doc_ref, sems):
    loads = [
        pltpu.make_async_copy(named_any, named_ref, sems.at[0]),
        pltpu.make_async_copy(doc_any, doc_ref, sems.at[1]),
    ]
    for load in loads:
        load.start()
    for load in loads:
        load.wait()
    for k in range(TOPK):
        table_ref[0, k : k + 1, :] = named_ref[k]
    table_ref[0, TOPK : TOPK + 1, :] = doc_ref[...]
    table_ref[0, TOPK + 1 :, :] = doc_ref[...]


def pack(named, doc):
    anywhere = pl.BlockSpec(memory_space=pl.ANY)
    return pl.pallas_call(
        pack_kernel,
        out_shape=jax.ShapeDtypeStruct((1, 8, doc.shape[1]), jnp.int32),
        in_specs=[anywhere] * 2,
        out_specs=pl.BlockSpec(memory_space=pltpu.VMEM),
        scratch_shapes=[
            pltpu.VMEM(named.shape, jnp.int32),
            pltpu.VMEM(doc.shape, jnp.int32),
            pltpu.SemaphoreType.DMA((2,)),
        ],
        compiler_params=pltpu.CompilerParams(vmem_limit_bytes=SMALL_VMEM),
    )(named, doc)


def join_kernel(first_ref, second_ref, *refs):
    count = first_ref.shape[0]
    refs[-1][:count] = first_ref[...]
    refs[-1][count:] = second_ref[...]


def copy_join_kernel(first_ref, second_ref, rows_ref, copy_ref, out_ref):
    join_kernel(first_ref, second_ref, out_ref)
    copy_ref[...] = rows_ref[...]


def join(first, second, passed=None, after=(), copy=False):
    vmem = pl.BlockSpec(memory_space=pltpu.VMEM)
    anywhere = pl.BlockSpec(memory_space=pl.ANY)
    table = jax.ShapeDtypeStruct((2 * first.shape[0],) + first.shape[1:], first.dtype)
    through = [] if passed is None else [passed]
    place = vmem if copy else anywhere
    out = pl.pallas_call(
        copy_join_kernel if copy else join_kernel,
        out_shape=[jax.ShapeDtypeStruct(x.shape, x.dtype) for x in through] + [table],
        in_specs=[vmem] * 2 + [place] * len(through) + [anywhere] * len(after),
        out_specs=[place] * len(through) + [vmem],
        input_output_aliases={2: 0} if through and not copy else {},
        compiler_params=pltpu.CompilerParams(vmem_limit_bytes=SMALL_VMEM),
    )(first, second, *through, *after)
    return out if through else out[0]


def load_kernel(w1_any, w2_any, *refs):
    w1_ref, w2_ref, sems = refs[-3:]
    loads = []
    for index, (source, target) in enumerate(((w1_any, w1_ref), (w2_any, w2_ref))):
        rows = source.shape[0] // 2
        for half in range(2):
            part = pl.ds(half * rows, rows)
            loads.append(
                pltpu.make_async_copy(source.at[part], target.at[part], sems.at[2 * index + half])
            )
    for load in loads:
        load.start()
    for load in loads:
        load.wait()


def load_weights(w_first, w_second, after):
    hbm = pl.BlockSpec(memory_space=pltpu.HBM)
    anywhere = pl.BlockSpec(memory_space=pl.ANY)
    vmem = pl.BlockSpec(memory_space=pltpu.VMEM)
    return pl.pallas_call(
        load_kernel,
        out_shape=[pltpu.VMEM(w.shape, w.dtype) for w in (w_first, w_second)],
        in_specs=[hbm] * 2 + [anywhere] * len(after),
        out_specs=[vmem] * 2,
        scratch_shapes=[pltpu.SemaphoreType.DMA((4,))],
        compiler_params=pltpu.CompilerParams(vmem_limit_bytes=LOAD_VMEM),
    )(w_first, w_second, *after)


def behind_kernel(*refs):
    pass


def behind(x, after):
    anywhere = pl.BlockSpec(memory_space=pl.ANY)
    return pl.pallas_call(
        behind_kernel,
        out_shape=jax.ShapeDtypeStruct(x.shape, x.dtype),
        in_specs=[anywhere] * (1 + len(after)),
        out_specs=anywhere,
        input_output_aliases={0: 0},
        compiler_params=pltpu.CompilerParams(vmem_limit_bytes=SMALL_VMEM),
    )(x, *after)


def kept_kernel(own_ref, capacity_ref, low_ref, high_ref, *refs):
    out_ref = refs[-2]
    tables = (low_ref, high_ref)
    own = own_ref[0]
    z = own // 4
    rows = low_ref.shape[2]
    sources = 2 * low_ref.shape[0]
    line = sources // 4
    upto = lax.broadcasted_iota(jnp.int32, (rows, rows), 0) <= lax.broadcasted_iota(
        jnp.int32, (rows, rows), 1
    )
    upto = jnp.where(upto, 1.0, 0.0).astype(jnp.bfloat16)

    def device_of(entry):
        flips = 4 * lax.rem(entry, line) + 2 * lax.rem(lax.div(entry, line), 2)
        return own ^ (flips + lax.div(entry, 2 * line))

    device = device_of(lax.broadcasted_iota(jnp.int32, (sources, sources), 0))
    other = device_of(lax.broadcasted_iota(jnp.int32, (sources, sources), 1))
    lower = jnp.where(other < device, 1.0, 0.0).astype(jnp.bfloat16)
    entry = lax.broadcasted_iota(jnp.int32, (sources, rows), 0)
    named = []
    for k in range(TOPK):
        named.append(jnp.concatenate([part[:, k, :] for part in tables], axis=0))
    kept = []
    for which in range(2):
        expert = own ^ which
        mine = named[0] == expert
        for k in range(1, TOPK):
            mine |= named[k] == expert
        flags = jnp.where(mine, 1.0, 0.0)
        running = jnp.dot(flags.astype(jnp.bfloat16), upto, preferred_element_type=jnp.float32)
        totals = jnp.broadcast_to(running[:, rows - 1 :], (sources, rows)).astype(jnp.bfloat16)
        before = jnp.dot(lower, totals, preferred_element_type=jnp.float32)
        slots = before + running - flags
        limit = capacity_ref[expert].astype(jnp.float32)
        kept.append(jnp.where(mine & (slots < limit), 1, 0))
    for step in range(line):
        home = z ^ lax.rem(z + line - step, line)
        for side in range(2):
            here = entry == home + line * side
            for k, part in enumerate(named + kept):
                picked = jnp.sum(jnp.where(here, part, 0), axis=0, keepdims=True)
                out_ref[2 * step + side, k : k + 1, :] = picked


def kept_rows(own, capacity, low, high, passed, after):
    smem = pl.BlockSpec(memory_space=pltpu.SMEM)
    vmem = pl.BlockSpec(memory_space=pltpu.VMEM)
    anywhere = pl.BlockSpec(memory_space=pl.ANY)
    return pl.pallas_call(
        kept_kernel,
        out_shape=(
            jax.ShapeDtypeStruct(low.shape, jnp.int32),
            jax.ShapeDtypeStruct(passed.shape, passed.dtype),
        ),
        in_specs=[smem, smem, vmem, vmem] + [anywhere] * (1 + len(after)),
        out_specs=(vmem, anywhere),
        input_output_aliases={4: 1},
        compiler_params=pltpu.CompilerParams(vmem_limit_bytes=SMALL_VMEM),
    )(own, capacity, low, high, passed, *after)


def gate_columns(own, router_ref, x, kept):
    logits = lax.dot_general(
        router_ref[...], x, (((1,), (1,)), ((), ())), preferred_element_type=jnp.float32
    )
    number = lax.broadcasted_iota(jnp.int32, logits.shape, 0)
    named = number == kept[0:1]
    for k in range(1, TOPK):
        named |= number == kept[k : k + 1]
    sigma = jnp.where(named, jax.nn.sigmoid(logits), 0.0)
    gates = sigma / jnp.sum(sigma, axis=0, keepdims=True)
    lines = []
    for which in range(2):
        gate = jnp.sum(jnp.where(number == own ^ which, gates, 0.0), axis=0, keepdims=True)
        lines.append(jnp.where(kept[TOPK + which : TOPK + which + 1] > 0, gate, 0.0))
    square = jnp.concatenate(lines + [jnp.zeros((x.shape[0] - 2, x.shape[0]), jnp.float32)], axis=0)
    return square.T


def expert_kernel(place, first, own_ref, kept_ref, router_ref, xz_ref, xy_ref, *refs):
    step = 512
    if first:
        sources = refs[:4]
        z_ref, y_ref, *staged, hidden_ref, mixed_ref, sems = refs[-7:]
        weights = list(refs[:2]) + staged
    else:
        weights = refs[:4]
        z_ref, y_ref, hidden_ref, mixed_ref = refs[-4:]
    chunks = [(w, c) for w in (2, 3) for c in range(0, weights[w].shape[1], step)]

    def load(index):
        which, column = chunks[index]
        cols = pl.ds(column, step)
        return pltpu.make_async_copy(
            sources[which].at[:, cols], weights[which].at[:, cols], sems.at[index]
        )

    def ready(which, column):
        if first and which > 1:
            index = chunks.index((which, column))
            load(index).wait()
            if index + WINDOW < len(chunks):
                load(index + WINDOW).start()

    if first:
        for index in range(WINDOW):
            load(index).start()
    own = own_ref[0]
    rows = xz_ref.shape[0]
    x = jnp.concatenate([xz_ref[...], xy_ref[...]], axis=0)
    gates = [
        gate_columns(own, router_ref, x_ref[...], kept_ref[2 * place + side])
        for side, x_ref in enumerate((xz_ref, xy_ref))
    ]
    for which in range(2):
        gate = jnp.concatenate([g[:, which : which + 1] for g in gates], axis=0)
        w1_ref, w2_ref = weights[2 * which], weights[2 * which + 1]
        for column in range(0, w1_ref.shape[1], step):
            cols = slice(column, column + step)
            ready(2 * which, column)
            hidden = jnp.dot(x, w1_ref[:, cols], preferred_element_type=jnp.float32)
            hidden = jnp.maximum(hidden, 0.0)
            hidden_ref[which, :, cols] = (hidden * hidden).astype(jnp.bfloat16)
        for column in range(0, w2_ref.shape[1], step):
            cols = slice(column, column + step)
            ready(2 * which + 1, column)
            result = jnp.dot(hidden_ref[which], w2_ref[:, cols], preferred_element_type=jnp.float32)
            if which == 0:
                mixed_ref[:, cols] = result * gate
            else:
                mixed = (mixed_ref[:, cols] + result * gate).astype(jnp.bfloat16)
                z_ref[:, cols] = mixed[:rows]
                y_ref[:, cols] = mixed[rows:]


def run_piece(place, first, own, kept, router, from_line, from_side, weights, after):
    rows, width = from_line.shape
    hidden = weights[0].shape[1]
    smem = pl.BlockSpec(memory_space=pltpu.SMEM)
    vmem = pl.BlockSpec(memory_space=pltpu.VMEM)
    hbm = pl.BlockSpec(memory_space=pltpu.HBM)
    anywhere = pl.BlockSpec(memory_space=pl.ANY)
    piece = jax.ShapeDtypeStruct((rows, width), jnp.bfloat16)
    staged = [pltpu.VMEM(w.shape, w.dtype) for w in weights[2:]] if first else []
    scratch = [
        pltpu.VMEM((2, 2 * rows, hidden), jnp.bfloat16),
        pltpu.VMEM((2 * rows, width), jnp.float32),
    ]
    if first:
        scratch.append(pltpu.SemaphoreType.DMA(((hidden + width) // 512,)))
    return pl.pallas_call(
        functools.partial(expert_kernel, place, first),
        out_shape=[piece, piece] + staged,
        in_specs=[smem] + [vmem] * 6 + [hbm if first else vmem] * 2 + [anywhere] * len(after),
        out_specs=[vmem] * (2 + len(staged)),
        scratch_shapes=scratch,
        compiler_params=pltpu.CompilerParams(vmem_limit_bytes=FIRST_VMEM if first else EXPERT_VMEM),
        cost_estimate=pl.CostEstimate(
            flops=16 * rows * width * hidden,
            bytes_accessed=8 * rows * width,
            transcendentals=0,
        ),
    )(own, kept, router, from_line, from_side, *weights, *after)


def add_kernel(count, first_ref, second_ref, *refs):
    total = first_ref[...].astype(jnp.float32) + second_ref[...].astype(jnp.float32)
    outs = refs[len(refs) - count - 1 :]
    outs[-1][...] = total.astype(jnp.bfloat16)
    for index in range(count):
        outs[index][...] = refs[index][...]


def add(first, second, after=(), staged=()):
    vmem = pl.BlockSpec(memory_space=pltpu.VMEM)
    anywhere = pl.BlockSpec(memory_space=pl.ANY)
    out = pl.pallas_call(
        functools.partial(add_kernel, len(staged)),
        out_shape=[jax.ShapeDtypeStruct(x.shape, x.dtype) for x in staged]
        + [jax.ShapeDtypeStruct(first.shape, first.dtype)],
        in_specs=[vmem] * (2 + len(staged)) + [anywhere] * len(after),
        out_specs=[vmem] * (1 + len(staged)),
        compiler_params=pltpu.CompilerParams(vmem_limit_bytes=SMALL_VMEM),
        cost_estimate=pl.CostEstimate(flops=first.size, bytes_accessed=first.size, transcendentals=0),
    )(first, second, *staged, *after)
    return out if staged else out[0]


def dense_moe(latent, router, expert_in, expert_out, routes, segments, capacity, k_near, v_near, attention):
    f32 = jnp.float32
    line = router.shape[1] // 4
    spots = [(z, y) for z in range(line) for y in range(2)]
    sibling = [(0, 1), (1, 0)]
    across = [(2 * z + y, 2 * z + 1 - y) for z, y in spots]

    def swap_core(x):
        return lax.ppermute(x, "context", sibling)

    def swap_side(x):
        return lax.ppermute(x, "expert", across)

    def along(x, step):
        return lax.ppermute(x, "expert", [(2 * z + y, 2 * ((z + step) % line) + y) for z, y in spots])

    def flipped(x, span):
        return lax.ppermute(x, "expert", [(2 * z + y, 2 * (z ^ span) + y) for z, y in spots])

    own = lax.axis_index(("expert", "context")).astype(jnp.int32).reshape(1)
    far_weights = [swap_core(expert_in[0]), swap_core(expert_out[0])]

    arriving, beside_own = along(latent[0], 1), swap_side(latent[0])
    table = pack(routes.transpose(2, 0, 1), segments)
    span = 1
    while 2 * span < line:
        table = join(table, flipped(table, span))
        span *= 2
    arriving, table = join(table, flipped(table, span), passed=arriving, after=(beside_own,))
    across_table = swap_side(table)
    chained = along(arriving, 1)
    passed, table = join(table, across_table, passed=arriving, copy=True)
    far_table = swap_core(table)
    from_side = [beside_own, swap_side(passed)]
    kept, passed = kept_rows(own, capacity, table, far_table, chained, ())
    doc_far = far_table[0, TOPK : TOPK + 1, :]
    from_line = [latent[0], arriving, passed]
    last = along(passed, 1)
    from_side.append(swap_side(passed))
    weights = list(load_weights(expert_in[0], expert_out[0], (kept,))) + far_weights

    def piece(step, weights, *after):
        return run_piece(
            step, step == 1, own, kept, router.T, from_line[step], from_side[step], weights, after
        )

    one, theirs, *weights[2:] = piece(1, weights)
    one_far = swap_side(theirs)
    last = behind(last, (one,))
    from_line.append(last)
    from_side.append(swap_side(last))
    two, theirs = piece(2, weights, one, from_line[3])
    two_far = swap_side(theirs)
    k_near, v_near, first = add(one, one_far, after=(two,), staged=(k_near, v_near))
    home = [along(first, line - 1)]
    three, theirs = piece(3, weights, two, first)
    three_far = swap_side(theirs)
    second = add(two, two_far, after=(three,))
    home.append(along(second, line - 2))
    near, theirs = piece(0, weights, three, second)
    near_far = swap_side(theirs)
    third = add(three, three_far, after=(near,))
    home.append(along(third, line - 3))
    swapped = (k_near, swap_core(k_near), v_near, swap_core(v_near))
    half = attention(0, doc_far, *swapped, after=(third,))
    attn_out = attention(1, doc_far, *swapped, before=half)
    total = near.astype(f32) + near_far.astype(f32)
    for part in home:
        total += part.astype(f32)
    return attn_out, total.astype(jnp.bfloat16)[None]


def routed_moe(latent, router, expert_in, expert_out, routes, capacity):
    tok_count = latent.shape[1]
    token_rows = latent[0]
    expert_count = router.shape[1]
    per_peer = max(2, 2 * tok_count * TOPK // expert_count)
    logits = jnp.dot(token_rows, router, preferred_element_type=jnp.float32)
    chosen_ids = routes[0]
    expert_ids = jnp.arange(expert_count, dtype=jnp.int32)
    one_hot = chosen_ids[:, :, None] == expert_ids[None, None, :]
    picked = jnp.sum(jnp.where(one_hot, logits[:, None, :], 0.0), axis=2)
    sigmas = jax.nn.sigmoid(picked)
    gates = sigmas / jnp.sum(sigmas, axis=1, keepdims=True)
    flat_hot = one_hot.reshape(tok_count * TOPK, expert_count).astype(jnp.int32)
    counts = jnp.sum(flat_hot, axis=0)
    ranks = jnp.sum((jnp.cumsum(flat_hot, axis=0) - flat_hot) * flat_hot, axis=1)
    count_rows = lax.all_gather(counts[None, :], ("expert", "context"), axis=0, tiled=True)
    own_index = lax.axis_index(("expert", "context"))
    lower_rows = jnp.arange(count_rows.shape[0], dtype=jnp.int32)[:, None] < own_index
    before = jnp.sum(jnp.where(lower_rows, count_rows, 0), axis=0)
    slots = jnp.sum(flat_hot * before[None, :], axis=1) + ranks
    limits = jnp.sum(flat_hot * capacity[None, :], axis=1)
    kept = slots < limits
    flat_ids = chosen_ids.reshape(-1)
    places = flat_ids * per_peer + ranks
    owners = jnp.arange(tok_count * TOPK, dtype=jnp.int32) // TOPK
    send_rows = (
        jnp.zeros((expert_count * per_peer, LATENT), jnp.bfloat16)
        .at[places]
        .set(token_rows[owners])
    )
    recv_rows = lax.all_to_all(
        send_rows.reshape(expert_count, per_peer, LATENT),
        ("expert", "context"),
        split_axis=0,
        concat_axis=0,
        tiled=True,
    ).reshape(expert_count * per_peer, LATENT)
    results = run_expert(recv_rows, expert_in[0], expert_out[0])
    returned = lax.all_to_all(
        results.reshape(expert_count, per_peer, LATENT),
        ("expert", "context"),
        split_axis=0,
        concat_axis=0,
        tiled=True,
    ).reshape(expert_count * per_peer, LATENT)
    gate_kept = jnp.where(kept, gates.reshape(-1), 0.0).reshape(tok_count, TOPK)
    back_rows = returned[places].reshape(tok_count, TOPK, LATENT).astype(jnp.float32)
    mixture = jnp.sum(gate_kept[:, :, None] * back_rows, axis=1)
    return mixture.astype(jnp.bfloat16).reshape(1, tok_count, LATENT)


def shards(
    query_heads,
    key_heads,
    value_heads,
    latent,
    router,
    expert_in,
    expert_out,
    routes,
    segments,
    offsets,
    capacity,
):
    swap = [(0, 1), (1, 0)]
    place = lax.axis_index("context").astype(jnp.int32).reshape(1)

    def attention(half, doc_far, *keys_and_values, **order):
        return attend(
            half, place, query_heads[0], *keys_and_values, segments, doc_far, offsets, **order
        )

    if router.shape[1] <= DENSE_EXPERTS:
        attn_out, moe_out = dense_moe(
            latent,
            router,
            expert_in,
            expert_out,
            routes,
            segments,
            capacity,
            key_heads[0],
            value_heads[0],
            attention,
        )
    else:
        doc_far = lax.ppermute(segments, "context", swap)
        k_far = lax.ppermute(key_heads[0], "context", swap)
        v_far = lax.ppermute(value_heads[0], "context", swap)
        swapped = (key_heads[0], k_far, value_heads[0], v_far)
        attn_out = attention(1, doc_far, *swapped, before=attention(0, doc_far, *swapped))
        moe_out = routed_moe(latent, router, expert_in, expert_out, routes, capacity)
    return (attn_out[None], moe_out)


def solution(mesh):
    rows = P(("groups", "expert"), "context", None)
    placed = (
        rows,
        rows,
        rows,
        rows,
        P(),
        P(("expert", "context"), None, None),
        P(("expert", "context"), None, None),
        rows,
        P(("groups", "expert"), "context"),
        P(("groups", "expert"), "context"),
        P(),
    )
    return jax.shard_map(
        shards,
        mesh=mesh,
        in_specs=placed,
        out_specs=(rows, rows),
        check_vma=False,
    )
```

```python
import functools
import math

import jax
import jax.numpy as jnp
from jax import lax
from jax.experimental import pallas as pl
from jax.experimental.pallas import tpu as pltpu
from jax.sharding import PartitionSpec as P

HEAD_DIM = 128
LATENT = 1024
TOPK = 6
DENSE_EXPERTS = 16
EXPERT_VMEM = 26 * 1024 * 1024
FIRST_VMEM = 26 * 1024 * 1024
LOAD_VMEM = 44 * 1024 * 1024
ATTEND_VMEM = 8 * 1024 * 1024
SMALL_VMEM = 4 * 1024 * 1024
WINDOW = 4


def run_expert(rows_in, w_first, w_second):
    hidden = jax.nn.relu(jnp.dot(rows_in, w_first, preferred_element_type=jnp.float32))
    hidden = (hidden * hidden).astype(jnp.bfloat16)
    return jnp.dot(hidden, w_second, preferred_element_type=jnp.float32).astype(jnp.bfloat16)


def column_of(row):
    n = row.shape[1]
    square = jnp.broadcast_to(row.astype(jnp.float32), (n, n)).T
    return square[:, :1].astype(jnp.int32)


def attend_kernel(place_ref, q_ref, k_own, k_far, v_own, v_far, doc_own, doc_far, ahead_ref, *rest):
    out_ref = rest[-1]
    rows = q_ref.shape[0]
    heads = q_ref.shape[1] // HEAD_DIM
    here = place_ref[0] * rows
    there = (1 - place_ref[0]) * rows
    doc_query = column_of(doc_own[...])
    reach = here + lax.broadcasted_iota(jnp.int32, (rows, 1), 0) + column_of(ahead_ref[...])
    lane = lax.broadcasted_iota(jnp.int32, (1, rows), 1)
    doc_key = jnp.concatenate([doc_own[...], doc_far[...]], axis=1)
    spot = jnp.concatenate([here + lane, there + lane], axis=1)
    visible = (doc_key == doc_query) & (spot <= reach)
    scale = HEAD_DIM ** (-0.5) * math.log2(math.e)
    across = (((1,), (1,)), ((), ()))
    for head in range(heads):
        cols = slice(head * HEAD_DIM, (head + 1) * HEAD_DIM)
        keys = jnp.concatenate([k_own[:, cols], k_far[:, cols]], axis=0)
        values = jnp.concatenate([v_own[:, cols], v_far[:, cols]], axis=0)
        scores = lax.dot_general(q_ref[:, cols], keys, across, preferred_element_type=jnp.float32)
        scores = jnp.where(visible, scores * scale, -1e30)
        raw = jnp.exp2(scores - jnp.max(scores, axis=1, keepdims=True))
        share = 1.0 / jnp.sum(raw, axis=1, keepdims=True)
        mixed = jnp.dot(raw.astype(jnp.bfloat16), values, preferred_element_type=jnp.float32)
        out_ref[:, cols] = (mixed * share).astype(jnp.bfloat16)


def attend(half, place, q, k_own, k_far, v_own, v_far, doc_own, doc_far, ahead, before=None, after=()):
    rows, width = q.shape
    smem = pl.BlockSpec(memory_space=pltpu.SMEM)
    heads = pl.BlockSpec((rows, width // 2), lambda i: (0, half))
    line = pl.BlockSpec((1, rows), lambda i: (0, 0))
    extra = list(after) + ([] if before is None else [before])
    return pl.pallas_call(
        attend_kernel,
        grid=(1,),
        out_shape=jax.ShapeDtypeStruct(q.shape, jnp.bfloat16),
        in_specs=[smem] + [heads] * 5 + [line] * 3 + [pl.BlockSpec(memory_space=pl.ANY)] * len(extra),
        out_specs=heads,
        input_output_aliases={} if before is None else {8 + len(extra): 0},
        compiler_params=pltpu.CompilerParams(vmem_limit_bytes=ATTEND_VMEM),
        cost_estimate=pl.CostEstimate(
            flops=4 * rows * rows * width, bytes_accessed=6 * rows * width, transcendentals=0
        ),
    )(place, q, k_own, k_far, v_own, v_far, doc_own, doc_far, ahead, *extra)


def pack_kernel(named_any, doc_any, table_ref, named_ref, doc_ref, sems):
    loads = [
        pltpu.make_async_copy(named_any, named_ref, sems.at[0]),
        pltpu.make_async_copy(doc_any, doc_ref, sems.at[1]),
    ]
    for load in loads:
        load.start()
    for load in loads:
        load.wait()
    for k in range(TOPK):
        table_ref[0, k : k + 1, :] = named_ref[k]
    table_ref[0, TOPK : TOPK + 1, :] = doc_ref[...]
    table_ref[0, TOPK + 1 :, :] = doc_ref[...]


def pack(named, doc):
    anywhere = pl.BlockSpec(memory_space=pl.ANY)
    return pl.pallas_call(
        pack_kernel,
        out_shape=jax.ShapeDtypeStruct((1, 8, doc.shape[1]), jnp.int32),
        in_specs=[anywhere] * 2,
        out_specs=pl.BlockSpec(memory_space=pltpu.VMEM),
        scratch_shapes=[
            pltpu.VMEM(named.shape, jnp.int32),
            pltpu.VMEM(doc.shape, jnp.int32),
            pltpu.SemaphoreType.DMA((2,)),
        ],
        compiler_params=pltpu.CompilerParams(vmem_limit_bytes=SMALL_VMEM),
    )(named, doc)


def join_kernel(first_ref, second_ref, *refs):
    count = first_ref.shape[0]
    refs[-1][:count] = first_ref[...]
    refs[-1][count:] = second_ref[...]


def join(first, second, passed=None, after=()):
    vmem = pl.BlockSpec(memory_space=pltpu.VMEM)
    anywhere = pl.BlockSpec(memory_space=pl.ANY)
    table = jax.ShapeDtypeStruct((2 * first.shape[0],) + first.shape[1:], first.dtype)
    through = [] if passed is None else [passed]
    out = pl.pallas_call(
        join_kernel,
        out_shape=[jax.ShapeDtypeStruct(x.shape, x.dtype) for x in through] + [table],
        in_specs=[vmem] * 2 + [anywhere] * (len(through) + len(after)),
        out_specs=[anywhere] * len(through) + [vmem],
        input_output_aliases={2: 0} if through else {},
        compiler_params=pltpu.CompilerParams(vmem_limit_bytes=SMALL_VMEM),
    )(first, second, *through, *after)
    return out if through else out[0]


def load_kernel(w1_any, w2_any, *refs):
    w1_ref, w2_ref, sems = refs[-3:]
    loads = []
    for index, (source, target) in enumerate(((w1_any, w1_ref), (w2_any, w2_ref))):
        rows = source.shape[0] // 2
        for half in range(2):
            part = pl.ds(half * rows, rows)
            loads.append(
                pltpu.make_async_copy(source.at[part], target.at[part], sems.at[2 * index + half])
            )
    for load in loads:
        load.start()
    for load in loads:
        load.wait()


def load_weights(w_first, w_second, after):
    hbm = pl.BlockSpec(memory_space=pltpu.HBM)
    anywhere = pl.BlockSpec(memory_space=pl.ANY)
    vmem = pl.BlockSpec(memory_space=pltpu.VMEM)
    return pl.pallas_call(
        load_kernel,
        out_shape=[pltpu.VMEM(w.shape, w.dtype) for w in (w_first, w_second)],
        in_specs=[hbm] * 2 + [anywhere] * len(after),
        out_specs=[vmem] * 2,
        scratch_shapes=[pltpu.SemaphoreType.DMA((4,))],
        compiler_params=pltpu.CompilerParams(vmem_limit_bytes=LOAD_VMEM),
    )(w_first, w_second, *after)


def kept_kernel(own_ref, capacity_ref, low_ref, high_ref, *refs):
    out_ref = refs[-2]
    tables = (low_ref, high_ref)
    own = own_ref[0]
    z = own // 4
    rows = low_ref.shape[2]
    sources = 2 * low_ref.shape[0]
    line = sources // 4
    upto = lax.broadcasted_iota(jnp.int32, (rows, rows), 0) <= lax.broadcasted_iota(
        jnp.int32, (rows, rows), 1
    )
    upto = jnp.where(upto, 1.0, 0.0).astype(jnp.bfloat16)

    def device_of(entry):
        flips = 4 * lax.rem(entry, line) + 2 * lax.rem(lax.div(entry, line), 2)
        return own ^ (flips + lax.div(entry, 2 * line))

    device = device_of(lax.broadcasted_iota(jnp.int32, (sources, sources), 0))
    other = device_of(lax.broadcasted_iota(jnp.int32, (sources, sources), 1))
    lower = jnp.where(other < device, 1.0, 0.0).astype(jnp.bfloat16)
    entry = lax.broadcasted_iota(jnp.int32, (sources, rows), 0)
    named = []
    for k in range(TOPK):
        named.append(jnp.concatenate([part[:, k, :] for part in tables], axis=0))
    kept = []
    for which in range(2):
        expert = own ^ which
        mine = named[0] == expert
        for k in range(1, TOPK):
            mine |= named[k] == expert
        flags = jnp.where(mine, 1.0, 0.0)
        running = jnp.dot(flags.astype(jnp.bfloat16), upto, preferred_element_type=jnp.float32)
        totals = jnp.broadcast_to(running[:, rows - 1 :], (sources, rows)).astype(jnp.bfloat16)
        before = jnp.dot(lower, totals, preferred_element_type=jnp.float32)
        slots = before + running - flags
        limit = capacity_ref[expert].astype(jnp.float32)
        kept.append(jnp.where(mine & (slots < limit), 1, 0))
    for step in range(line):
        home = z ^ lax.rem(z + line - step, line)
        for side in range(2):
            here = entry == home + line * side
            for k, part in enumerate(named + kept):
                picked = jnp.sum(jnp.where(here, part, 0), axis=0, keepdims=True)
                out_ref[2 * step + side, k : k + 1, :] = picked


def kept_rows(own, capacity, low, high, passed, after):
    smem = pl.BlockSpec(memory_space=pltpu.SMEM)
    vmem = pl.BlockSpec(memory_space=pltpu.VMEM)
    anywhere = pl.BlockSpec(memory_space=pl.ANY)
    return pl.pallas_call(
        kept_kernel,
        out_shape=(
            jax.ShapeDtypeStruct(low.shape, jnp.int32),
            jax.ShapeDtypeStruct(passed.shape, passed.dtype),
        ),
        in_specs=[smem, smem, vmem, vmem] + [anywhere] * (1 + len(after)),
        out_specs=(vmem, anywhere),
        input_output_aliases={4: 1},
        compiler_params=pltpu.CompilerParams(vmem_limit_bytes=SMALL_VMEM),
    )(own, capacity, low, high, passed, *after)


def gate_columns(own, router_ref, x, kept):
    logits = lax.dot_general(
        router_ref[...], x, (((1,), (1,)), ((), ())), preferred_element_type=jnp.float32
    )
    number = lax.broadcasted_iota(jnp.int32, logits.shape, 0)
    named = number == kept[0:1]
    for k in range(1, TOPK):
        named |= number == kept[k : k + 1]
    sigma = jnp.where(named, jax.nn.sigmoid(logits), 0.0)
    gates = sigma / jnp.sum(sigma, axis=0, keepdims=True)
    lines = []
    for which in range(2):
        gate = jnp.sum(jnp.where(number == own ^ which, gates, 0.0), axis=0, keepdims=True)
        lines.append(jnp.where(kept[TOPK + which : TOPK + which + 1] > 0, gate, 0.0))
    square = jnp.concatenate(lines + [jnp.zeros((x.shape[0] - 2, x.shape[0]), jnp.float32)], axis=0)
    return square.T


def expert_kernel(place, first, own_ref, kept_ref, router_ref, xz_ref, xy_ref, *refs):
    step = 512
    if first:
        sources = refs[:4]
        z_ref, y_ref, *staged, hidden_ref, mixed_ref, sems = refs[-7:]
        weights = list(refs[:2]) + staged
    else:
        weights = refs[:4]
        z_ref, y_ref, hidden_ref, mixed_ref = refs[-4:]
    chunks = [(w, c) for w in (2, 3) for c in range(0, weights[w].shape[1], step)]

    def load(index):
        which, column = chunks[index]
        cols = pl.ds(column, step)
        return pltpu.make_async_copy(
            sources[which].at[:, cols], weights[which].at[:, cols], sems.at[index]
        )

    def ready(which, column):
        if first and which > 1:
            index = chunks.index((which, column))
            load(index).wait()
            if index + WINDOW < len(chunks):
                load(index + WINDOW).start()

    if first:
        for index in range(WINDOW):
            load(index).start()
    own = own_ref[0]
    rows = xz_ref.shape[0]
    x = jnp.concatenate([xz_ref[...], xy_ref[...]], axis=0)
    gates = [
        gate_columns(own, router_ref, x_ref[...], kept_ref[2 * place + side])
        for side, x_ref in enumerate((xz_ref, xy_ref))
    ]
    for which in range(2):
        gate = jnp.concatenate([g[:, which : which + 1] for g in gates], axis=0)
        w1_ref, w2_ref = weights[2 * which], weights[2 * which + 1]
        for column in range(0, w1_ref.shape[1], step):
            cols = slice(column, column + step)
            ready(2 * which, column)
            hidden = jnp.dot(x, w1_ref[:, cols], preferred_element_type=jnp.float32)
            hidden = jnp.maximum(hidden, 0.0)
            hidden_ref[which, :, cols] = (hidden * hidden).astype(jnp.bfloat16)
        for column in range(0, w2_ref.shape[1], step):
            cols = slice(column, column + step)
            ready(2 * which + 1, column)
            result = jnp.dot(hidden_ref[which], w2_ref[:, cols], preferred_element_type=jnp.float32)
            if which == 0:
                mixed_ref[:, cols] = result * gate
            else:
                mixed = (mixed_ref[:, cols] + result * gate).astype(jnp.bfloat16)
                z_ref[:, cols] = mixed[:rows]
                y_ref[:, cols] = mixed[rows:]


def run_piece(place, first, own, kept, router, from_line, from_side, weights, after):
    rows, width = from_line.shape
    hidden = weights[0].shape[1]
    smem = pl.BlockSpec(memory_space=pltpu.SMEM)
    vmem = pl.BlockSpec(memory_space=pltpu.VMEM)
    hbm = pl.BlockSpec(memory_space=pltpu.HBM)
    anywhere = pl.BlockSpec(memory_space=pl.ANY)
    piece = jax.ShapeDtypeStruct((rows, width), jnp.bfloat16)
    staged = [pltpu.VMEM(w.shape, w.dtype) for w in weights[2:]] if first else []
    scratch = [
        pltpu.VMEM((2, 2 * rows, hidden), jnp.bfloat16),
        pltpu.VMEM((2 * rows, width), jnp.float32),
    ]
    if first:
        scratch.append(pltpu.SemaphoreType.DMA(((hidden + width) // 512,)))
    return pl.pallas_call(
        functools.partial(expert_kernel, place, first),
        out_shape=[piece, piece] + staged,
        in_specs=[smem] + [vmem] * 6 + [hbm if first else vmem] * 2 + [anywhere] * len(after),
        out_specs=[vmem] * (2 + len(staged)),
        scratch_shapes=scratch,
        compiler_params=pltpu.CompilerParams(vmem_limit_bytes=FIRST_VMEM if first else EXPERT_VMEM),
        cost_estimate=pl.CostEstimate(
            flops=16 * rows * width * hidden,
            bytes_accessed=8 * rows * width,
            transcendentals=0,
        ),
    )(own, kept, router, from_line, from_side, *weights, *after)


def add_kernel(count, first_ref, second_ref, *refs):
    total = first_ref[...].astype(jnp.float32) + second_ref[...].astype(jnp.float32)
    outs = refs[len(refs) - count - 1 :]
    outs[-1][...] = total.astype(jnp.bfloat16)
    for index in range(count):
        outs[index][...] = refs[index][...]


def add(first, second, after=(), staged=()):
    vmem = pl.BlockSpec(memory_space=pltpu.VMEM)
    anywhere = pl.BlockSpec(memory_space=pl.ANY)
    out = pl.pallas_call(
        functools.partial(add_kernel, len(staged)),
        out_shape=[jax.ShapeDtypeStruct(x.shape, x.dtype) for x in staged]
        + [jax.ShapeDtypeStruct(first.shape, first.dtype)],
        in_specs=[vmem] * (2 + len(staged)) + [anywhere] * len(after),
        out_specs=[vmem] * (1 + len(staged)),
        compiler_params=pltpu.CompilerParams(vmem_limit_bytes=SMALL_VMEM),
        cost_estimate=pl.CostEstimate(flops=first.size, bytes_accessed=first.size, transcendentals=0),
    )(first, second, *staged, *after)
    return out if staged else out[0]


def dense_moe(latent, router, expert_in, expert_out, routes, segments, capacity, k_near, v_near, attention):
    f32 = jnp.float32
    line = router.shape[1] // 4
    spots = [(z, y) for z in range(line) for y in range(2)]
    sibling = [(0, 1), (1, 0)]
    across = [(2 * z + y, 2 * z + 1 - y) for z, y in spots]

    def swap_core(x):
        return lax.ppermute(x, "context", sibling)

    def swap_side(x):
        return lax.ppermute(x, "expert", across)

    def along(x, step):
        return lax.ppermute(x, "expert", [(2 * z + y, 2 * ((z + step) % line) + y) for z, y in spots])

    def flipped(x, span):
        return lax.ppermute(x, "expert", [(2 * z + y, 2 * (z ^ span) + y) for z, y in spots])

    own = lax.axis_index(("expert", "context")).astype(jnp.int32).reshape(1)
    far_weights = [swap_core(expert_in[0]), swap_core(expert_out[0])]

    from_line = [latent[0], along(latent[0], 1)]
    from_side = [swap_side(latent[0])]
    table = pack(routes.transpose(2, 0, 1), segments)
    span = 1
    while span < line:
        here = len(from_line) - 1
        flip = flipped(table, span)
        from_line[here], table = join(table, flip, passed=from_line[here], after=(from_side[-1],))
        span *= 2
        from_line.append(along(from_line[here], 1))
        from_side.append(swap_side(from_line[here]))
    table = join(table, swap_side(table))
    far_table = swap_core(table)
    doc_far = far_table[0, TOPK : TOPK + 1, :]
    own_weights = load_weights(expert_in[0], expert_out[0], (table,))
    kept, from_line[-1] = kept_rows(own, capacity, table, far_table, from_line[-1], own_weights)
    from_side.append(swap_side(from_line[-1]))
    weights = list(own_weights) + far_weights

    def piece(step, weights, *after):
        return run_piece(
            step, step == 1, own, kept, router.T, from_line[step], from_side[step], weights, after
        )

    one, theirs, *weights[2:] = piece(1, weights)
    one_far = swap_side(theirs)
    two, theirs = piece(2, weights, one)
    two_far = swap_side(theirs)
    k_near, v_near, first = add(one, one_far, after=(two,), staged=(k_near, v_near))
    home = [along(first, line - 1)]
    three, theirs = piece(3, weights, two, first)
    three_far = swap_side(theirs)
    second = add(two, two_far, after=(three,))
    home.append(along(second, line - 2))
    near, theirs = piece(0, weights, three, second)
    near_far = swap_side(theirs)
    third = add(three, three_far, after=(near,))
    home.append(along(third, line - 3))
    swapped = (k_near, swap_core(k_near), v_near, swap_core(v_near))
    half = attention(0, doc_far, *swapped, after=(third,))
    attn_out = attention(1, doc_far, *swapped, before=half)
    total = near.astype(f32) + near_far.astype(f32)
    for part in home:
        total += part.astype(f32)
    return attn_out, total.astype(jnp.bfloat16)[None]


def routed_moe(latent, router, expert_in, expert_out, routes, capacity):
    tok_count = latent.shape[1]
    token_rows = latent[0]
    expert_count = router.shape[1]
    per_peer = max(2, 2 * tok_count * TOPK // expert_count)
    logits = jnp.dot(token_rows, router, preferred_element_type=jnp.float32)
    chosen_ids = routes[0]
    expert_ids = jnp.arange(expert_count, dtype=jnp.int32)
    one_hot = chosen_ids[:, :, None] == expert_ids[None, None, :]
    picked = jnp.sum(jnp.where(one_hot, logits[:, None, :], 0.0), axis=2)
    sigmas = jax.nn.sigmoid(picked)
    gates = sigmas / jnp.sum(sigmas, axis=1, keepdims=True)
    flat_hot = one_hot.reshape(tok_count * TOPK, expert_count).astype(jnp.int32)
    counts = jnp.sum(flat_hot, axis=0)
    ranks = jnp.sum((jnp.cumsum(flat_hot, axis=0) - flat_hot) * flat_hot, axis=1)
    count_rows = lax.all_gather(counts[None, :], ("expert", "context"), axis=0, tiled=True)
    own_index = lax.axis_index(("expert", "context"))
    lower_rows = jnp.arange(count_rows.shape[0], dtype=jnp.int32)[:, None] < own_index
    before = jnp.sum(jnp.where(lower_rows, count_rows, 0), axis=0)
    slots = jnp.sum(flat_hot * before[None, :], axis=1) + ranks
    limits = jnp.sum(flat_hot * capacity[None, :], axis=1)
    kept = slots < limits
    flat_ids = chosen_ids.reshape(-1)
    places = flat_ids * per_peer + ranks
    owners = jnp.arange(tok_count * TOPK, dtype=jnp.int32) // TOPK
    send_rows = (
        jnp.zeros((expert_count * per_peer, LATENT), jnp.bfloat16)
        .at[places]
        .set(token_rows[owners])
    )
    recv_rows = lax.all_to_all(
        send_rows.reshape(expert_count, per_peer, LATENT),
        ("expert", "context"),
        split_axis=0,
        concat_axis=0,
        tiled=True,
    ).reshape(expert_count * per_peer, LATENT)
    results = run_expert(recv_rows, expert_in[0], expert_out[0])
    returned = lax.all_to_all(
        results.reshape(expert_count, per_peer, LATENT),
        ("expert", "context"),
        split_axis=0,
        concat_axis=0,
        tiled=True,
    ).reshape(expert_count * per_peer, LATENT)
    gate_kept = jnp.where(kept, gates.reshape(-1), 0.0).reshape(tok_count, TOPK)
    back_rows = returned[places].reshape(tok_count, TOPK, LATENT).astype(jnp.float32)
    mixture = jnp.sum(gate_kept[:, :, None] * back_rows, axis=1)
    return mixture.astype(jnp.bfloat16).reshape(1, tok_count, LATENT)


def shards(
    query_heads,
    key_heads,
    value_heads,
    latent,
    router,
    expert_in,
    expert_out,
    routes,
    segments,
    offsets,
    capacity,
):
    swap = [(0, 1), (1, 0)]
    place = lax.axis_index("context").astype(jnp.int32).reshape(1)

    def attention(half, doc_far, *keys_and_values, **order):
        return attend(
            half, place, query_heads[0], *keys_and_values, segments, doc_far, offsets, **order
        )

    if router.shape[1] <= DENSE_EXPERTS:
        attn_out, moe_out = dense_moe(
            latent,
            router,
            expert_in,
            expert_out,
            routes,
            segments,
            capacity,
            key_heads[0],
            value_heads[0],
            attention,
        )
    else:
        doc_far = lax.ppermute(segments, "context", swap)
        k_far = lax.ppermute(key_heads[0], "context", swap)
        v_far = lax.ppermute(value_heads[0], "context", swap)
        swapped = (key_heads[0], k_far, value_heads[0], v_far)
        attn_out = attention(1, doc_far, *swapped, before=attention(0, doc_far, *swapped))
        moe_out = routed_moe(latent, router, expert_in, expert_out, routes, capacity)
    return (attn_out[None], moe_out)


def solution(mesh):
    rows = P(("groups", "expert"), "context", None)
    placed = (
        rows,
        rows,
        rows,
        rows,
        P(),
        P(("expert", "context"), None, None),
        P(("expert", "context"), None, None),
        rows,
        P(("groups", "expert"), "context"),
        P(("groups", "expert"), "context"),
        P(),
    )
    return jax.shard_map(
        shards,
        mesh=mesh,
        in_specs=placed,
        out_specs=(rows, rows),
        check_vma=False,
    )
```

```python
import functools
import math

import jax
import jax.numpy as jnp
from jax import lax
from jax.experimental import pallas as pl
from jax.experimental.pallas import tpu as pltpu
from jax.sharding import PartitionSpec as P

HEAD_DIM = 128
LATENT = 1024
TOPK = 6
DENSE_EXPERTS = 16
EXPERT_VMEM = 26 * 1024 * 1024
FIRST_VMEM = 26 * 1024 * 1024
LOAD_VMEM = 44 * 1024 * 1024
ATTEND_VMEM = 8 * 1024 * 1024
SMALL_VMEM = 4 * 1024 * 1024
STEP = 512
WINDOW = 4


def run_expert(rows_in, w_first, w_second):
    hidden = jax.nn.relu(jnp.dot(rows_in, w_first, preferred_element_type=jnp.float32))
    hidden = (hidden * hidden).astype(jnp.bfloat16)
    return jnp.dot(hidden, w_second, preferred_element_type=jnp.float32).astype(jnp.bfloat16)


def column_of(row):
    n = row.shape[1]
    square = jnp.broadcast_to(row.astype(jnp.float32), (n, n)).T
    return square[:, :1].astype(jnp.int32)


def attend_kernel(place_ref, q_ref, k_own, k_far, v_own, v_far, doc_own, doc_far, ahead_ref, *rest):
    out_ref = rest[-1]
    rows = q_ref.shape[0]
    heads = q_ref.shape[1] // HEAD_DIM
    here = place_ref[0] * rows
    there = (1 - place_ref[0]) * rows
    doc_query = column_of(doc_own[...])
    reach = here + lax.broadcasted_iota(jnp.int32, (rows, 1), 0) + column_of(ahead_ref[...])
    lane = lax.broadcasted_iota(jnp.int32, (1, rows), 1)
    doc_key = jnp.concatenate([doc_own[...], doc_far[...]], axis=1)
    spot = jnp.concatenate([here + lane, there + lane], axis=1)
    visible = (doc_key == doc_query) & (spot <= reach)
    scale = HEAD_DIM ** (-0.5) * math.log2(math.e)
    across = (((1,), (1,)), ((), ()))
    for head in range(heads):
        cols = slice(head * HEAD_DIM, (head + 1) * HEAD_DIM)
        keys = jnp.concatenate([k_own[:, cols], k_far[:, cols]], axis=0)
        values = jnp.concatenate([v_own[:, cols], v_far[:, cols]], axis=0)
        scores = lax.dot_general(q_ref[:, cols], keys, across, preferred_element_type=jnp.float32)
        scores = jnp.where(visible, scores * scale, -1e30)
        raw = jnp.exp2(scores - jnp.max(scores, axis=1, keepdims=True))
        share = 1.0 / jnp.sum(raw, axis=1, keepdims=True)
        mixed = jnp.dot(raw.astype(jnp.bfloat16), values, preferred_element_type=jnp.float32)
        out_ref[:, cols] = (mixed * share).astype(jnp.bfloat16)


def attend(half, place, q, k_own, k_far, v_own, v_far, doc_own, doc_far, ahead, before=None, after=()):
    rows, width = q.shape
    smem = pl.BlockSpec(memory_space=pltpu.SMEM)
    heads = pl.BlockSpec((rows, width // 2), lambda i: (0, half))
    line = pl.BlockSpec((1, rows), lambda i: (0, 0))
    extra = list(after) + ([] if before is None else [before])
    return pl.pallas_call(
        attend_kernel,
        grid=(1,),
        out_shape=jax.ShapeDtypeStruct(q.shape, jnp.bfloat16),
        in_specs=[smem] + [heads] * 5 + [line] * 3 + [pl.BlockSpec(memory_space=pl.ANY)] * len(extra),
        out_specs=heads,
        input_output_aliases={} if before is None else {8 + len(extra): 0},
        compiler_params=pltpu.CompilerParams(vmem_limit_bytes=ATTEND_VMEM),
        cost_estimate=pl.CostEstimate(
            flops=4 * rows * rows * width, bytes_accessed=6 * rows * width, transcendentals=0
        ),
    )(place, q, k_own, k_far, v_own, v_far, doc_own, doc_far, ahead, *extra)


def pack_kernel(named_any, doc_any, table_ref, named_ref, doc_ref, sems):
    loads = [
        pltpu.make_async_copy(named_any, named_ref, sems.at[0]),
        pltpu.make_async_copy(doc_any, doc_ref, sems.at[1]),
    ]
    for load in loads:
        load.start()
    for load in loads:
        load.wait()
    for k in range(TOPK):
        table_ref[0, k : k + 1, :] = named_ref[k]
    table_ref[0, TOPK : TOPK + 1, :] = doc_ref[...]
    table_ref[0, TOPK + 1 :, :] = doc_ref[...]


def pack(named, doc):
    anywhere = pl.BlockSpec(memory_space=pl.ANY)
    return pl.pallas_call(
        pack_kernel,
        out_shape=jax.ShapeDtypeStruct((1, 8, doc.shape[1]), jnp.int32),
        in_specs=[anywhere] * 2,
        out_specs=pl.BlockSpec(memory_space=pltpu.VMEM),
        scratch_shapes=[
            pltpu.VMEM(named.shape, jnp.int32),
            pltpu.VMEM(doc.shape, jnp.int32),
            pltpu.SemaphoreType.DMA((2,)),
        ],
        compiler_params=pltpu.CompilerParams(vmem_limit_bytes=SMALL_VMEM),
    )(named, doc)


def join_kernel(first_ref, second_ref, *refs):
    count = first_ref.shape[0]
    refs[-1][:count] = first_ref[...]
    refs[-1][count:] = second_ref[...]


def join(first, second, passed=None, after=()):
    vmem = pl.BlockSpec(memory_space=pltpu.VMEM)
    anywhere = pl.BlockSpec(memory_space=pl.ANY)
    table = jax.ShapeDtypeStruct((2 * first.shape[0],) + first.shape[1:], first.dtype)
    through = [] if passed is None else [passed]
    out = pl.pallas_call(
        join_kernel,
        out_shape=[jax.ShapeDtypeStruct(x.shape, x.dtype) for x in through] + [table],
        in_specs=[vmem] * 2 + [anywhere] * (len(through) + len(after)),
        out_specs=[anywhere] * len(through) + [vmem],
        input_output_aliases={2: 0} if through else {},
        compiler_params=pltpu.CompilerParams(vmem_limit_bytes=SMALL_VMEM),
    )(first, second, *through, *after)
    return out if through else out[0]


def load_kernel(w1_any, w2_any, *refs):
    w1_ref, w2_ref, sems = refs[-3:]
    loads = []
    for index, (source, target) in enumerate(((w1_any, w1_ref), (w2_any, w2_ref))):
        rows = source.shape[0] // 2
        for half in range(2):
            part = pl.ds(half * rows, rows)
            loads.append(
                pltpu.make_async_copy(source.at[part], target.at[part], sems.at[2 * index + half])
            )
    for load in loads:
        load.start()
    for load in loads:
        load.wait()


def load_weights(w_first, w_second, after):
    hbm = pl.BlockSpec(memory_space=pltpu.HBM)
    anywhere = pl.BlockSpec(memory_space=pl.ANY)
    vmem = pl.BlockSpec(memory_space=pltpu.VMEM)
    return pl.pallas_call(
        load_kernel,
        out_shape=[pltpu.VMEM(w.shape, w.dtype) for w in (w_first, w_second)],
        in_specs=[hbm] * 2 + [anywhere] * len(after),
        out_specs=[vmem] * 2,
        scratch_shapes=[pltpu.SemaphoreType.DMA((4,))],
        compiler_params=pltpu.CompilerParams(vmem_limit_bytes=LOAD_VMEM),
    )(w_first, w_second, *after)


def kept_kernel(own_ref, capacity_ref, low_ref, high_ref, *refs):
    out_ref = refs[-2]
    tables = (low_ref, high_ref)
    own = own_ref[0]
    z = own // 4
    rows = low_ref.shape[2]
    sources = 2 * low_ref.shape[0]
    line = sources // 4
    upto = lax.broadcasted_iota(jnp.int32, (rows, rows), 0) <= lax.broadcasted_iota(
        jnp.int32, (rows, rows), 1
    )
    upto = jnp.where(upto, 1.0, 0.0).astype(jnp.bfloat16)

    def device_of(entry):
        flips = 4 * lax.rem(entry, line) + 2 * lax.rem(lax.div(entry, line), 2)
        return own ^ (flips + lax.div(entry, 2 * line))

    device = device_of(lax.broadcasted_iota(jnp.int32, (sources, sources), 0))
    other = device_of(lax.broadcasted_iota(jnp.int32, (sources, sources), 1))
    lower = jnp.where(other < device, 1.0, 0.0).astype(jnp.bfloat16)
    entry = lax.broadcasted_iota(jnp.int32, (sources, rows), 0)
    named = []
    for k in range(TOPK):
        named.append(jnp.concatenate([part[:, k, :] for part in tables], axis=0))
    kept = []
    for which in range(2):
        expert = own ^ which
        mine = named[0] == expert
        for k in range(1, TOPK):
            mine |= named[k] == expert
        flags = jnp.where(mine, 1.0, 0.0)
        running = jnp.dot(flags.astype(jnp.bfloat16), upto, preferred_element_type=jnp.float32)
        totals = jnp.broadcast_to(running[:, rows - 1 :], (sources, rows)).astype(jnp.bfloat16)
        before = jnp.dot(lower, totals, preferred_element_type=jnp.float32)
        slots = before + running - flags
        limit = capacity_ref[expert].astype(jnp.float32)
        kept.append(jnp.where(mine & (slots < limit), 1, 0))
    for step in range(line):
        home = z ^ lax.rem(z + line - step, line)
        for side in range(2):
            here = entry == home + line * side
            for k, part in enumerate(named + kept):
                picked = jnp.sum(jnp.where(here, part, 0), axis=0, keepdims=True)
                out_ref[2 * step + side, k : k + 1, :] = picked


def kept_rows(own, capacity, low, high, passed, after):
    smem = pl.BlockSpec(memory_space=pltpu.SMEM)
    vmem = pl.BlockSpec(memory_space=pltpu.VMEM)
    anywhere = pl.BlockSpec(memory_space=pl.ANY)
    return pl.pallas_call(
        kept_kernel,
        out_shape=(
            jax.ShapeDtypeStruct(low.shape, jnp.int32),
            jax.ShapeDtypeStruct(passed.shape, passed.dtype),
        ),
        in_specs=[smem, smem, vmem, vmem] + [anywhere] * (1 + len(after)),
        out_specs=(vmem, anywhere),
        input_output_aliases={4: 1},
        compiler_params=pltpu.CompilerParams(vmem_limit_bytes=SMALL_VMEM),
    )(own, capacity, low, high, passed, *after)


def gate_columns(own, router_ref, x, kept):
    logits = lax.dot_general(
        router_ref[...], x, (((1,), (1,)), ((), ())), preferred_element_type=jnp.float32
    )
    number = lax.broadcasted_iota(jnp.int32, logits.shape, 0)
    named = number == kept[0:1]
    for k in range(1, TOPK):
        named |= number == kept[k : k + 1]
    sigma = jnp.where(named, jax.nn.sigmoid(logits), 0.0)
    gates = sigma / jnp.sum(sigma, axis=0, keepdims=True)
    lines = []
    for which in range(2):
        gate = jnp.sum(jnp.where(number == own ^ which, gates, 0.0), axis=0, keepdims=True)
        lines.append(jnp.where(kept[TOPK + which : TOPK + which + 1] > 0, gate, 0.0))
    square = jnp.concatenate(lines + [jnp.zeros((x.shape[0] - 2, x.shape[0]), jnp.float32)], axis=0)
    return square.T


def gate_pairs(place, own_ref, kept_ref, router_ref, xz_ref, xy_ref):
    gates = [
        gate_columns(own_ref[0], router_ref, x_ref[...], kept_ref[2 * place + side])
        for side, x_ref in enumerate((xz_ref, xy_ref))
    ]
    return [jnp.concatenate([g[:, which : which + 1] for g in gates], axis=0) for which in range(2)]


def run_expert_pair(xz_ref, xy_ref, weights, hidden_ref, ready, emit):
    x = jnp.concatenate([xz_ref[...], xy_ref[...]], axis=0)
    for which in range(2):
        w1_ref, w2_ref = weights[2 * which], weights[2 * which + 1]
        for column in range(0, w1_ref.shape[1], STEP):
            cols = slice(column, column + STEP)
            ready(2 * which, column)
            hidden = jnp.dot(x, w1_ref[:, cols], preferred_element_type=jnp.float32)
            hidden = jnp.maximum(hidden, 0.0)
            hidden_ref[which, :, cols] = (hidden * hidden).astype(jnp.bfloat16)
        for column in range(0, w2_ref.shape[1], STEP):
            cols = slice(column, column + STEP)
            ready(2 * which + 1, column)
            result = jnp.dot(hidden_ref[which], w2_ref[:, cols], preferred_element_type=jnp.float32)
            emit(which, cols, result)


def expert_kernel(
    place, own_ref, kept_ref, router_ref, xz_ref, xy_ref, w1a, w2a, w1b, w2b, *refs
):
    z_ref, y_ref, hidden_ref, mixed_ref = refs[-4:]
    rows = xz_ref.shape[0]
    gates = gate_pairs(place, own_ref, kept_ref, router_ref, xz_ref, xy_ref)

    def emit(which, cols, result):
        if which == 0:
            mixed_ref[:, cols] = result * gates[0]
        else:
            mixed = (mixed_ref[:, cols] + result * gates[1]).astype(jnp.bfloat16)
            z_ref[:, cols] = mixed[:rows]
            y_ref[:, cols] = mixed[rows:]

    weights = (w1a, w2a, w1b, w2b)
    run_expert_pair(xz_ref, xy_ref, weights, hidden_ref, lambda which, column: None, emit)


def first_kernel(xz_ref, xy_ref, w1a, w2a, *refs):
    sources = refs[:2]
    own_ref, far_ref, w1b, w2b, hidden_ref, sems = refs[-6:]
    targets = (w1b, w2b)
    chunks = [(w, c) for w in range(2) for c in range(0, targets[w].shape[1], STEP)]

    def load(index):
        which, column = chunks[index]
        cols = pl.ds(column, STEP)
        return pltpu.make_async_copy(
            sources[which].at[:, cols], targets[which].at[:, cols], sems.at[index]
        )

    def ready(which, column):
        if which > 1:
            index = chunks.index((which - 2, column))
            load(index).wait()
            if index + WINDOW < len(chunks):
                load(index + WINDOW).start()

    def emit(which, cols, result):
        (own_ref, far_ref)[which][:, cols] = result.astype(jnp.bfloat16)

    for index in range(WINDOW):
        load(index).start()
    run_expert_pair(xz_ref, xy_ref, (w1a, w2a, w1b, w2b), hidden_ref, ready, emit)


def gate_kernel(place, own_ref, kept_ref, router_ref, xz_ref, xy_ref, mine_ref, far_ref, *refs):
    z_ref, y_ref = refs[-2:]
    rows = xz_ref.shape[0]
    gates = gate_pairs(place, own_ref, kept_ref, router_ref, xz_ref, xy_ref)
    mixed = mine_ref[...].astype(jnp.float32) * gates[0]
    mixed = (mixed + far_ref[...].astype(jnp.float32) * gates[1]).astype(jnp.bfloat16)
    z_ref[...] = mixed[:rows]
    y_ref[...] = mixed[rows:]


def gate_piece(place, own, kept, router, from_line, from_side, raw, after):
    smem = pl.BlockSpec(memory_space=pltpu.SMEM)
    vmem = pl.BlockSpec(memory_space=pltpu.VMEM)
    anywhere = pl.BlockSpec(memory_space=pl.ANY)
    piece = jax.ShapeDtypeStruct(from_line.shape, jnp.bfloat16)
    return pl.pallas_call(
        functools.partial(gate_kernel, place),
        out_shape=(piece, piece),
        in_specs=[smem] + [vmem] * 6 + [anywhere] * len(after),
        out_specs=(vmem, vmem),
        compiler_params=pltpu.CompilerParams(vmem_limit_bytes=ATTEND_VMEM),
    )(own, kept, router, from_line, from_side, *raw, *after)


def run_first(from_line, from_side, own_weights, far_weights):
    rows, width = from_line.shape
    hidden = own_weights[0].shape[1]
    vmem = pl.BlockSpec(memory_space=pltpu.VMEM)
    hbm = pl.BlockSpec(memory_space=pltpu.HBM)
    raw = jax.ShapeDtypeStruct((2 * rows, width), jnp.bfloat16)
    return pl.pallas_call(
        first_kernel,
        out_shape=[raw, raw] + [pltpu.VMEM(w.shape, w.dtype) for w in far_weights],
        in_specs=[vmem] * 4 + [hbm] * 2,
        out_specs=[vmem] * 4,
        scratch_shapes=[
            pltpu.VMEM((2, 2 * rows, hidden), jnp.bfloat16),
            pltpu.SemaphoreType.DMA(((hidden + width) // STEP,)),
        ],
        compiler_params=pltpu.CompilerParams(vmem_limit_bytes=FIRST_VMEM),
        cost_estimate=pl.CostEstimate(
            flops=16 * rows * width * hidden, bytes_accessed=8 * rows * width, transcendentals=0
        ),
    )(from_line, from_side, *own_weights, *far_weights)


def run_piece(place, own, kept, router, from_line, from_side, weights, after):
    rows, width = from_line.shape
    hidden = weights[0].shape[1]
    smem = pl.BlockSpec(memory_space=pltpu.SMEM)
    vmem = pl.BlockSpec(memory_space=pltpu.VMEM)
    anywhere = pl.BlockSpec(memory_space=pl.ANY)
    piece = jax.ShapeDtypeStruct((rows, width), jnp.bfloat16)
    return pl.pallas_call(
        functools.partial(expert_kernel, place),
        out_shape=(piece, piece),
        in_specs=[smem] + [vmem] * 8 + [anywhere] * len(after),
        out_specs=(vmem, vmem),
        scratch_shapes=[
            pltpu.VMEM((2, 2 * rows, hidden), jnp.bfloat16),
            pltpu.VMEM((2 * rows, width), jnp.float32),
        ],
        compiler_params=pltpu.CompilerParams(vmem_limit_bytes=EXPERT_VMEM),
        cost_estimate=pl.CostEstimate(
            flops=16 * rows * width * hidden, bytes_accessed=8 * rows * width, transcendentals=0
        ),
    )(own, kept, router, from_line, from_side, *weights, *after)


def add_kernel(count, first_ref, second_ref, *refs):
    total = first_ref[...].astype(jnp.float32) + second_ref[...].astype(jnp.float32)
    outs = refs[len(refs) - count - 1 :]
    outs[-1][...] = total.astype(jnp.bfloat16)
    for index in range(count):
        outs[index][...] = refs[index][...]


def add(first, second, after=(), staged=()):
    vmem = pl.BlockSpec(memory_space=pltpu.VMEM)
    anywhere = pl.BlockSpec(memory_space=pl.ANY)
    out = pl.pallas_call(
        functools.partial(add_kernel, len(staged)),
        out_shape=[jax.ShapeDtypeStruct(x.shape, x.dtype) for x in staged]
        + [jax.ShapeDtypeStruct(first.shape, first.dtype)],
        in_specs=[vmem] * (2 + len(staged)) + [anywhere] * len(after),
        out_specs=[vmem] * (1 + len(staged)),
        compiler_params=pltpu.CompilerParams(vmem_limit_bytes=SMALL_VMEM),
        cost_estimate=pl.CostEstimate(flops=first.size, bytes_accessed=first.size, transcendentals=0),
    )(first, second, *staged, *after)
    return out if staged else out[0]


def dense_moe(latent, router, expert_in, expert_out, routes, segments, capacity, k_near, v_near, attention):
    f32 = jnp.float32
    line = router.shape[1] // 4
    spots = [(z, y) for z in range(line) for y in range(2)]
    sibling = [(0, 1), (1, 0)]
    across = [(2 * z + y, 2 * z + 1 - y) for z, y in spots]

    def swap_core(x):
        return lax.ppermute(x, "context", sibling)

    def swap_side(x):
        return lax.ppermute(x, "expert", across)

    def along(x, step):
        return lax.ppermute(x, "expert", [(2 * z + y, 2 * ((z + step) % line) + y) for z, y in spots])

    def flipped(x, span):
        return lax.ppermute(x, "expert", [(2 * z + y, 2 * (z ^ span) + y) for z, y in spots])

    own = lax.axis_index(("expert", "context")).astype(jnp.int32).reshape(1)
    far_weights = [swap_core(expert_in[0]), swap_core(expert_out[0])]

    from_line = [latent[0], along(latent[0], 1)]
    from_side = [swap_side(latent[0])]
    table = pack(routes.transpose(2, 0, 1), segments)
    own_weights = load_weights(expert_in[0], expert_out[0], (table,))
    hold = own_weights
    span = 1
    while span < line:
        here = len(from_line) - 1
        flip = flipped(table, span)
        after = (from_side[-1], *hold)
        from_line[here], table = join(table, flip, passed=from_line[here], after=after)
        from_line.append(along(from_line[here], 1))
        from_side.append(swap_side(from_line[here]))
        if span == 1:
            *raw, far_first, far_second = run_first(
                from_line[0], from_side[0], own_weights, far_weights
            )
            weights = (*own_weights, far_first, far_second)
            hold = raw
        span *= 2
    table = join(table, swap_side(table))
    far_table = swap_core(table)
    doc_far = far_table[0, TOPK : TOPK + 1, :]
    kept, from_line[-1] = kept_rows(own, capacity, table, far_table, from_line[-1], ())
    from_side.append(swap_side(from_line[-1]))

    def piece(step, *after):
        return run_piece(
            step, own, kept, router.T, from_line[step], from_side[step], weights, after
        )

    one, theirs = piece(1)
    one_far = swap_side(theirs)
    two, theirs = piece(2, one)
    two_far = swap_side(theirs)
    first = add(one, one_far, after=(two,))
    home = [along(first, line - 1)]
    near, theirs = gate_piece(
        0, own, kept, router.T, from_line[0], from_side[0], raw, (first,)
    )
    near_far = swap_side(theirs)
    three, theirs = piece(3, two, near)
    three_far = swap_side(theirs)
    k_near, v_near, second = add(
        two, two_far, after=(three, home[0]), staged=(k_near, v_near)
    )
    home.append(along(second, line - 2))
    third = add(three, three_far, after=(second, near_far))
    home.append(along(third, line - 3))
    swapped = (k_near, swap_core(k_near), v_near, swap_core(v_near))
    half = attention(0, doc_far, *swapped, after=(third,))
    attn_out = attention(1, doc_far, *swapped, before=half)
    total = near.astype(f32) + near_far.astype(f32)
    for part in home:
        total += part.astype(f32)
    return attn_out, total.astype(jnp.bfloat16)[None]


def routed_moe(latent, router, expert_in, expert_out, routes, capacity):
    tok_count = latent.shape[1]
    token_rows = latent[0]
    expert_count = router.shape[1]
    per_peer = max(2, 2 * tok_count * TOPK // expert_count)
    logits = jnp.dot(token_rows, router, preferred_element_type=jnp.float32)
    chosen_ids = routes[0]
    expert_ids = jnp.arange(expert_count, dtype=jnp.int32)
    one_hot = chosen_ids[:, :, None] == expert_ids[None, None, :]
    picked = jnp.sum(jnp.where(one_hot, logits[:, None, :], 0.0), axis=2)
    sigmas = jax.nn.sigmoid(picked)
    gates = sigmas / jnp.sum(sigmas, axis=1, keepdims=True)
    flat_hot = one_hot.reshape(tok_count * TOPK, expert_count).astype(jnp.int32)
    counts = jnp.sum(flat_hot, axis=0)
    ranks = jnp.sum((jnp.cumsum(flat_hot, axis=0) - flat_hot) * flat_hot, axis=1)
    count_rows = lax.all_gather(counts[None, :], ("expert", "context"), axis=0, tiled=True)
    own_index = lax.axis_index(("expert", "context"))
    lower_rows = jnp.arange(count_rows.shape[0], dtype=jnp.int32)[:, None] < own_index
    before = jnp.sum(jnp.where(lower_rows, count_rows, 0), axis=0)
    slots = jnp.sum(flat_hot * before[None, :], axis=1) + ranks
    limits = jnp.sum(flat_hot * capacity[None, :], axis=1)
    kept = slots < limits
    flat_ids = chosen_ids.reshape(-1)
    places = flat_ids * per_peer + ranks
    owners = jnp.arange(tok_count * TOPK, dtype=jnp.int32) // TOPK
    send_rows = (
        jnp.zeros((expert_count * per_peer, LATENT), jnp.bfloat16)
        .at[places]
        .set(token_rows[owners])
    )
    recv_rows = lax.all_to_all(
        send_rows.reshape(expert_count, per_peer, LATENT),
        ("expert", "context"),
        split_axis=0,
        concat_axis=0,
        tiled=True,
    ).reshape(expert_count * per_peer, LATENT)
    results = run_expert(recv_rows, expert_in[0], expert_out[0])
    returned = lax.all_to_all(
        results.reshape(expert_count, per_peer, LATENT),
        ("expert", "context"),
        split_axis=0,
        concat_axis=0,
        tiled=True,
    ).reshape(expert_count * per_peer, LATENT)
    gate_kept = jnp.where(kept, gates.reshape(-1), 0.0).reshape(tok_count, TOPK)
    back_rows = returned[places].reshape(tok_count, TOPK, LATENT).astype(jnp.float32)
    mixture = jnp.sum(gate_kept[:, :, None] * back_rows, axis=1)
    return mixture.astype(jnp.bfloat16).reshape(1, tok_count, LATENT)


def shards(
    query_heads,
    key_heads,
    value_heads,
    latent,
    router,
    expert_in,
    expert_out,
    routes,
    segments,
    offsets,
    capacity,
):
    swap = [(0, 1), (1, 0)]
    place = lax.axis_index("context").astype(jnp.int32).reshape(1)

    def attention(half, doc_far, *keys_and_values, **order):
        return attend(
            half, place, query_heads[0], *keys_and_values, segments, doc_far, offsets, **order
        )

    if router.shape[1] <= DENSE_EXPERTS:
        attn_out, moe_out = dense_moe(
            latent,
            router,
            expert_in,
            expert_out,
            routes,
            segments,
            capacity,
            key_heads[0],
            value_heads[0],
            attention,
        )
    else:
        doc_far = lax.ppermute(segments, "context", swap)
        k_far = lax.ppermute(key_heads[0], "context", swap)
        v_far = lax.ppermute(value_heads[0], "context", swap)
        swapped = (key_heads[0], k_far, value_heads[0], v_far)
        attn_out = attention(1, doc_far, *swapped, before=attention(0, doc_far, *swapped))
        moe_out = routed_moe(latent, router, expert_in, expert_out, routes, capacity)
    return (attn_out[None], moe_out)


def solution(mesh):
    rows = P(("groups", "expert"), "context", None)
    placed = (
        rows,
        rows,
        rows,
        rows,
        P(),
        P(("expert", "context"), None, None),
        P(("expert", "context"), None, None),
        rows,
        P(("groups", "expert"), "context"),
        P(("groups", "expert"), "context"),
        P(),
    )
    return jax.shard_map(
        shards,
        mesh=mesh,
        in_specs=placed,
        out_specs=(rows, rows),
        check_vma=False,
    )
```

```python
import functools
import math

import jax
import jax.numpy as jnp
from jax import lax
from jax.experimental import pallas as pl
from jax.experimental.pallas import tpu as pltpu
from jax.sharding import PartitionSpec as P

HEAD_DIM = 128
LATENT = 1024
TOPK = 6
DENSE_EXPERTS = 16
EXPERT_VMEM = 26 * 1024 * 1024
FIRST_VMEM = 26 * 1024 * 1024
LOAD_VMEM = 44 * 1024 * 1024
ATTEND_VMEM = 8 * 1024 * 1024
SMALL_VMEM = 4 * 1024 * 1024
WINDOW = 4


def run_expert(rows_in, w_first, w_second):
    hidden = jax.nn.relu(jnp.dot(rows_in, w_first, preferred_element_type=jnp.float32))
    hidden = (hidden * hidden).astype(jnp.bfloat16)
    return jnp.dot(hidden, w_second, preferred_element_type=jnp.float32).astype(jnp.bfloat16)


def column_of(row):
    n = row.shape[1]
    square = jnp.broadcast_to(row.astype(jnp.float32), (n, n)).T
    return square[:, :1].astype(jnp.int32)


def attend_kernel(place_ref, q_ref, k_own, k_far, v_own, v_far, doc_own, doc_far, ahead_ref, *rest):
    out_ref = rest[-1]
    rows = q_ref.shape[0]
    heads = q_ref.shape[1] // HEAD_DIM
    here = place_ref[0] * rows
    there = (1 - place_ref[0]) * rows
    doc_query = column_of(doc_own[...])
    reach = here + lax.broadcasted_iota(jnp.int32, (rows, 1), 0) + column_of(ahead_ref[...])
    lane = lax.broadcasted_iota(jnp.int32, (1, rows), 1)
    doc_key = jnp.concatenate([doc_own[...], doc_far[...]], axis=1)
    spot = jnp.concatenate([here + lane, there + lane], axis=1)
    visible = (doc_key == doc_query) & (spot <= reach)
    scale = HEAD_DIM ** (-0.5) * math.log2(math.e)
    across = (((1,), (1,)), ((), ()))
    for head in range(heads):
        cols = slice(head * HEAD_DIM, (head + 1) * HEAD_DIM)
        keys = jnp.concatenate([k_own[:, cols], k_far[:, cols]], axis=0)
        values = jnp.concatenate([v_own[:, cols], v_far[:, cols]], axis=0)
        scores = lax.dot_general(q_ref[:, cols], keys, across, preferred_element_type=jnp.float32)
        scores = jnp.where(visible, scores * scale, -1e30)
        raw = jnp.exp2(scores - jnp.max(scores, axis=1, keepdims=True))
        share = 1.0 / jnp.sum(raw, axis=1, keepdims=True)
        mixed = jnp.dot(raw.astype(jnp.bfloat16), values, preferred_element_type=jnp.float32)
        out_ref[:, cols] = (mixed * share).astype(jnp.bfloat16)


def attend(half, place, q, k_own, k_far, v_own, v_far, doc_own, doc_far, ahead, before=None, after=()):
    rows, width = q.shape
    smem = pl.BlockSpec(memory_space=pltpu.SMEM)
    heads = pl.BlockSpec((rows, width // 2), lambda i: (0, half))
    line = pl.BlockSpec((1, rows), lambda i: (0, 0))
    extra = list(after) + ([] if before is None else [before])
    return pl.pallas_call(
        attend_kernel,
        grid=(1,),
        out_shape=jax.ShapeDtypeStruct(q.shape, jnp.bfloat16),
        in_specs=[smem] + [heads] * 5 + [line] * 3 + [pl.BlockSpec(memory_space=pl.ANY)] * len(extra),
        out_specs=heads,
        input_output_aliases={} if before is None else {8 + len(extra): 0},
        compiler_params=pltpu.CompilerParams(vmem_limit_bytes=ATTEND_VMEM),
        cost_estimate=pl.CostEstimate(
            flops=4 * rows * rows * width, bytes_accessed=6 * rows * width, transcendentals=0
        ),
    )(place, q, k_own, k_far, v_own, v_far, doc_own, doc_far, ahead, *extra)


def pack_kernel(named_any, doc_any, table_ref, named_ref, doc_ref, sems):
    loads = [
        pltpu.make_async_copy(named_any, named_ref, sems.at[0]),
        pltpu.make_async_copy(doc_any, doc_ref, sems.at[1]),
    ]
    for load in loads:
        load.start()
    for load in loads:
        load.wait()
    for k in range(TOPK):
        table_ref[0, k : k + 1, :] = named_ref[k]
    table_ref[0, TOPK : TOPK + 1, :] = doc_ref[...]
    table_ref[0, TOPK + 1 :, :] = doc_ref[...]


def pack(named, doc):
    anywhere = pl.BlockSpec(memory_space=pl.ANY)
    return pl.pallas_call(
        pack_kernel,
        out_shape=jax.ShapeDtypeStruct((1, 8, doc.shape[1]), jnp.int32),
        in_specs=[anywhere] * 2,
        out_specs=pl.BlockSpec(memory_space=pltpu.VMEM),
        scratch_shapes=[
            pltpu.VMEM(named.shape, jnp.int32),
            pltpu.VMEM(doc.shape, jnp.int32),
            pltpu.SemaphoreType.DMA((2,)),
        ],
        compiler_params=pltpu.CompilerParams(vmem_limit_bytes=SMALL_VMEM),
    )(named, doc)


def join_kernel(first_ref, second_ref, *refs):
    count = first_ref.shape[0]
    refs[-1][:count] = first_ref[...]
    refs[-1][count:] = second_ref[...]


def join(first, second, passed=None, after=()):
    vmem = pl.BlockSpec(memory_space=pltpu.VMEM)
    anywhere = pl.BlockSpec(memory_space=pl.ANY)
    table = jax.ShapeDtypeStruct((2 * first.shape[0],) + first.shape[1:], first.dtype)
    through = [] if passed is None else [passed]
    out = pl.pallas_call(
        join_kernel,
        out_shape=[jax.ShapeDtypeStruct(x.shape, x.dtype) for x in through] + [table],
        in_specs=[vmem] * 2 + [anywhere] * (len(through) + len(after)),
        out_specs=[anywhere] * len(through) + [vmem],
        input_output_aliases={2: 0} if through else {},
        compiler_params=pltpu.CompilerParams(vmem_limit_bytes=SMALL_VMEM),
    )(first, second, *through, *after)
    return out if through else out[0]


def load_kernel(w1_any, w2_any, *refs):
    w1_ref, w2_ref, sems = refs[-3:]
    loads = []
    for index, (source, target) in enumerate(((w1_any, w1_ref), (w2_any, w2_ref))):
        rows = source.shape[0] // 2
        for half in range(2):
            part = pl.ds(half * rows, rows)
            loads.append(
                pltpu.make_async_copy(source.at[part], target.at[part], sems.at[2 * index + half])
            )
    for load in loads:
        load.start()
    for load in loads:
        load.wait()


def load_weights(w_first, w_second, after):
    hbm = pl.BlockSpec(memory_space=pltpu.HBM)
    anywhere = pl.BlockSpec(memory_space=pl.ANY)
    vmem = pl.BlockSpec(memory_space=pltpu.VMEM)
    return pl.pallas_call(
        load_kernel,
        out_shape=[pltpu.VMEM(w.shape, w.dtype) for w in (w_first, w_second)],
        in_specs=[hbm] * 2 + [anywhere] * len(after),
        out_specs=[vmem] * 2,
        scratch_shapes=[pltpu.SemaphoreType.DMA((4,))],
        compiler_params=pltpu.CompilerParams(vmem_limit_bytes=LOAD_VMEM),
    )(w_first, w_second, *after)


def kept_kernel(own_ref, capacity_ref, low_ref, high_ref, *refs):
    out_ref = refs[-2]
    tables = (low_ref, high_ref)
    own = own_ref[0]
    z = own // 4
    rows = low_ref.shape[2]
    sources = 2 * low_ref.shape[0]
    line = sources // 4
    upto = lax.broadcasted_iota(jnp.int32, (rows, rows), 0) <= lax.broadcasted_iota(
        jnp.int32, (rows, rows), 1
    )
    upto = jnp.where(upto, 1.0, 0.0).astype(jnp.bfloat16)

    def device_of(entry):
        flips = 4 * lax.rem(entry, line) + 2 * lax.rem(lax.div(entry, line), 2)
        return own ^ (flips + lax.div(entry, 2 * line))

    device = device_of(lax.broadcasted_iota(jnp.int32, (sources, sources), 0))
    other = device_of(lax.broadcasted_iota(jnp.int32, (sources, sources), 1))
    lower = jnp.where(other < device, 1.0, 0.0).astype(jnp.bfloat16)
    entry = lax.broadcasted_iota(jnp.int32, (sources, rows), 0)
    named = []
    for k in range(TOPK):
        named.append(jnp.concatenate([part[:, k, :] for part in tables], axis=0))
    kept = []
    for which in range(2):
        expert = own ^ which
        mine = named[0] == expert
        for k in range(1, TOPK):
            mine |= named[k] == expert
        flags = jnp.where(mine, 1.0, 0.0)
        running = jnp.dot(flags.astype(jnp.bfloat16), upto, preferred_element_type=jnp.float32)
        totals = jnp.broadcast_to(running[:, rows - 1 :], (sources, rows)).astype(jnp.bfloat16)
        before = jnp.dot(lower, totals, preferred_element_type=jnp.float32)
        slots = before + running - flags
        limit = capacity_ref[expert].astype(jnp.float32)
        kept.append(jnp.where(mine & (slots < limit), 1, 0))
    for step in range(line):
        home = z ^ lax.rem(z + line - step, line)
        for side in range(2):
            here = entry == home + line * side
            for k, part in enumerate(named + kept):
                picked = jnp.sum(jnp.where(here, part, 0), axis=0, keepdims=True)
                out_ref[2 * step + side, k : k + 1, :] = picked


def kept_rows(own, capacity, low, high, passed, after):
    smem = pl.BlockSpec(memory_space=pltpu.SMEM)
    vmem = pl.BlockSpec(memory_space=pltpu.VMEM)
    anywhere = pl.BlockSpec(memory_space=pl.ANY)
    return pl.pallas_call(
        kept_kernel,
        out_shape=(
            jax.ShapeDtypeStruct(low.shape, jnp.int32),
            jax.ShapeDtypeStruct(passed.shape, passed.dtype),
        ),
        in_specs=[smem, smem, vmem, vmem] + [anywhere] * (1 + len(after)),
        out_specs=(vmem, anywhere),
        input_output_aliases={4: 1},
        compiler_params=pltpu.CompilerParams(vmem_limit_bytes=SMALL_VMEM),
    )(own, capacity, low, high, passed, *after)


def gate_columns(own, router_ref, x, kept):
    logits = lax.dot_general(
        router_ref[...], x, (((1,), (1,)), ((), ())), preferred_element_type=jnp.float32
    )
    number = lax.broadcasted_iota(jnp.int32, logits.shape, 0)
    named = number == kept[0:1]
    for k in range(1, TOPK):
        named |= number == kept[k : k + 1]
    sigma = jnp.where(named, jax.nn.sigmoid(logits), 0.0)
    gates = sigma / jnp.sum(sigma, axis=0, keepdims=True)
    lines = []
    for which in range(2):
        gate = jnp.sum(jnp.where(number == own ^ which, gates, 0.0), axis=0, keepdims=True)
        lines.append(jnp.where(kept[TOPK + which : TOPK + which + 1] > 0, gate, 0.0))
    square = jnp.concatenate(lines + [jnp.zeros((x.shape[0] - 2, x.shape[0]), jnp.float32)], axis=0)
    return square.T


def expert_kernel(place, first, own_ref, kept_ref, router_ref, xz_ref, xy_ref, *refs):
    step = 512
    if first:
        sources = refs[:4]
        z_ref, y_ref, *staged, hidden_ref, mixed_ref, sems = refs[-7:]
        weights = list(refs[:2]) + staged
    else:
        weights = refs[:4]
        z_ref, y_ref, hidden_ref, mixed_ref = refs[-4:]
    chunks = [(w, c) for w in (2, 3) for c in range(0, weights[w].shape[1], step)]

    def load(index):
        which, column = chunks[index]
        cols = pl.ds(column, step)
        return pltpu.make_async_copy(
            sources[which].at[:, cols], weights[which].at[:, cols], sems.at[index]
        )

    def ready(which, column):
        if first and which > 1:
            index = chunks.index((which, column))
            load(index).wait()
            if index + WINDOW < len(chunks):
                load(index + WINDOW).start()

    if first:
        for index in range(WINDOW):
            load(index).start()
    own = own_ref[0]
    rows = xz_ref.shape[0]
    x = jnp.concatenate([xz_ref[...], xy_ref[...]], axis=0)
    gates = [
        gate_columns(own, router_ref, x_ref[...], kept_ref[2 * place + side])
        for side, x_ref in enumerate((xz_ref, xy_ref))
    ]
    for which in range(2):
        gate = jnp.concatenate([g[:, which : which + 1] for g in gates], axis=0)
        w1_ref, w2_ref = weights[2 * which], weights[2 * which + 1]
        for column in range(0, w1_ref.shape[1], step):
            cols = slice(column, column + step)
            ready(2 * which, column)
            hidden = jnp.dot(x, w1_ref[:, cols], preferred_element_type=jnp.float32)
            hidden = jnp.maximum(hidden, 0.0)
            hidden_ref[which, :, cols] = (hidden * hidden).astype(jnp.bfloat16)
        for column in range(0, w2_ref.shape[1], step):
            cols = slice(column, column + step)
            ready(2 * which + 1, column)
            result = jnp.dot(hidden_ref[which], w2_ref[:, cols], preferred_element_type=jnp.float32)
            if which == 0:
                mixed_ref[:, cols] = result * gate
            else:
                mixed = (mixed_ref[:, cols] + result * gate).astype(jnp.bfloat16)
                z_ref[:, cols] = mixed[:rows]
                y_ref[:, cols] = mixed[rows:]


def run_piece(place, first, own, kept, router, from_line, from_side, weights, after):
    rows, width = from_line.shape
    hidden = weights[0].shape[1]
    smem = pl.BlockSpec(memory_space=pltpu.SMEM)
    vmem = pl.BlockSpec(memory_space=pltpu.VMEM)
    hbm = pl.BlockSpec(memory_space=pltpu.HBM)
    anywhere = pl.BlockSpec(memory_space=pl.ANY)
    piece = jax.ShapeDtypeStruct((rows, width), jnp.bfloat16)
    staged = [pltpu.VMEM(w.shape, w.dtype) for w in weights[2:]] if first else []
    scratch = [
        pltpu.VMEM((2, 2 * rows, hidden), jnp.bfloat16),
        pltpu.VMEM((2 * rows, width), jnp.float32),
    ]
    if first:
        scratch.append(pltpu.SemaphoreType.DMA(((hidden + width) // 512,)))
    return pl.pallas_call(
        functools.partial(expert_kernel, place, first),
        out_shape=[piece, piece] + staged,
        in_specs=[smem] + [vmem] * 6 + [hbm if first else vmem] * 2 + [anywhere] * len(after),
        out_specs=[vmem] * (2 + len(staged)),
        scratch_shapes=scratch,
        compiler_params=pltpu.CompilerParams(vmem_limit_bytes=FIRST_VMEM if first else EXPERT_VMEM),
        cost_estimate=pl.CostEstimate(
            flops=16 * rows * width * hidden,
            bytes_accessed=8 * rows * width,
            transcendentals=0,
        ),
    )(own, kept, router, from_line, from_side, *weights, *after)


def add_kernel(terms, count, *refs):
    total = refs[0][...].astype(jnp.float32)
    for term in refs[1:terms]:
        total += term[...].astype(jnp.float32)
    outs = refs[len(refs) - count - 1 :]
    outs[-1][...] = total.astype(jnp.bfloat16)
    for index in range(count):
        outs[index][...] = refs[terms + index][...]


def add(*terms, after=(), staged=()):
    vmem = pl.BlockSpec(memory_space=pltpu.VMEM)
    anywhere = pl.BlockSpec(memory_space=pl.ANY)
    first = terms[0]
    out = pl.pallas_call(
        functools.partial(add_kernel, len(terms), len(staged)),
        out_shape=[jax.ShapeDtypeStruct(x.shape, x.dtype) for x in staged]
        + [jax.ShapeDtypeStruct(first.shape, first.dtype)],
        in_specs=[vmem] * (len(terms) + len(staged)) + [anywhere] * len(after),
        out_specs=[vmem] * (1 + len(staged)),
        compiler_params=pltpu.CompilerParams(vmem_limit_bytes=SMALL_VMEM),
        cost_estimate=pl.CostEstimate(flops=first.size, bytes_accessed=first.size, transcendentals=0),
    )(*terms, *staged, *after)
    return out if staged else out[0]


def dense_moe(latent, router, expert_in, expert_out, routes, segments, capacity, k_near, v_near, attention):
    f32 = jnp.float32
    line = router.shape[1] // 4
    spots = [(z, y) for z in range(line) for y in range(2)]
    sibling = [(0, 1), (1, 0)]
    across = [(2 * z + y, 2 * z + 1 - y) for z, y in spots]

    def swap_core(x):
        return lax.ppermute(x, "context", sibling)

    def swap_side(x):
        return lax.ppermute(x, "expert", across)

    def along(x, step):
        return lax.ppermute(x, "expert", [(2 * z + y, 2 * ((z + step) % line) + y) for z, y in spots])

    def flipped(x, span):
        return lax.ppermute(x, "expert", [(2 * z + y, 2 * (z ^ span) + y) for z, y in spots])

    own = lax.axis_index(("expert", "context")).astype(jnp.int32).reshape(1)
    far_weights = [swap_core(expert_in[0]), swap_core(expert_out[0])]

    from_line = [latent[0], along(latent[0], 1)]
    from_side = [swap_side(latent[0])]
    table = pack(routes.transpose(2, 0, 1), segments)
    span = 1
    while span < line:
        here = len(from_line) - 1
        flip = flipped(table, span)
        from_line[here], table = join(table, flip, passed=from_line[here], after=(from_side[-1],))
        span *= 2
        from_line.append(along(from_line[here], 1))
        from_side.append(swap_side(from_line[here]))
    table = join(table, swap_side(table))
    far_table = swap_core(table)
    doc_far = far_table[0, TOPK : TOPK + 1, :]
    own_weights = load_weights(expert_in[0], expert_out[0], (table,))
    kept, from_line[-1] = kept_rows(own, capacity, table, far_table, from_line[-1], own_weights)
    from_side.append(swap_side(from_line[-1]))
    weights = list(own_weights) + far_weights

    def piece(step, weights, *after):
        return run_piece(
            step, step == 2, own, kept, router.T, from_line[step], from_side[step], weights, after
        )

    two, theirs, *weights[2:] = piece(2, weights)
    two_far = swap_side(theirs)
    one, theirs = piece(1, weights, two)
    one_far = swap_side(theirs)
    k_near, v_near, second = add(two, two_far, after=(one,), staged=(k_near, v_near))
    passing = along(second, line - 1)
    three, theirs = piece(3, weights, one, second)
    three_far = swap_side(theirs)
    swapped = (k_near, swap_core(k_near), v_near, swap_core(v_near))
    half = attention(0, doc_far, *swapped, after=(three,))
    attn_out = attention(1, doc_far, *swapped, before=half)
    first = add(one, one_far, passing, after=(attn_out,))
    home = [along(first, line - 1)]
    near, theirs = piece(0, weights, three, first)
    near_far = swap_side(theirs)
    third = add(three, three_far, after=(near, home[0]))
    home.append(along(third, line - 3))
    total = near.astype(f32) + near_far.astype(f32)
    for part in home:
        total += part.astype(f32)
    return attn_out, total.astype(jnp.bfloat16)[None]


def routed_moe(latent, router, expert_in, expert_out, routes, capacity):
    tok_count = latent.shape[1]
    token_rows = latent[0]
    expert_count = router.shape[1]
    per_peer = max(2, 2 * tok_count * TOPK // expert_count)
    logits = jnp.dot(token_rows, router, preferred_element_type=jnp.float32)
    chosen_ids = routes[0]
    expert_ids = jnp.arange(expert_count, dtype=jnp.int32)
    one_hot = chosen_ids[:, :, None] == expert_ids[None, None, :]
    picked = jnp.sum(jnp.where(one_hot, logits[:, None, :], 0.0), axis=2)
    sigmas = jax.nn.sigmoid(picked)
    gates = sigmas / jnp.sum(sigmas, axis=1, keepdims=True)
    flat_hot = one_hot.reshape(tok_count * TOPK, expert_count).astype(jnp.int32)
    counts = jnp.sum(flat_hot, axis=0)
    ranks = jnp.sum((jnp.cumsum(flat_hot, axis=0) - flat_hot) * flat_hot, axis=1)
    count_rows = lax.all_gather(counts[None, :], ("expert", "context"), axis=0, tiled=True)
    own_index = lax.axis_index(("expert", "context"))
    lower_rows = jnp.arange(count_rows.shape[0], dtype=jnp.int32)[:, None] < own_index
    before = jnp.sum(jnp.where(lower_rows, count_rows, 0), axis=0)
    slots = jnp.sum(flat_hot * before[None, :], axis=1) + ranks
    limits = jnp.sum(flat_hot * capacity[None, :], axis=1)
    kept = slots < limits
    flat_ids = chosen_ids.reshape(-1)
    places = flat_ids * per_peer + ranks
    owners = jnp.arange(tok_count * TOPK, dtype=jnp.int32) // TOPK
    send_rows = (
        jnp.zeros((expert_count * per_peer, LATENT), jnp.bfloat16)
        .at[places]
        .set(token_rows[owners])
    )
    recv_rows = lax.all_to_all(
        send_rows.reshape(expert_count, per_peer, LATENT),
        ("expert", "context"),
        split_axis=0,
        concat_axis=0,
        tiled=True,
    ).reshape(expert_count * per_peer, LATENT)
    results = run_expert(recv_rows, expert_in[0], expert_out[0])
    returned = lax.all_to_all(
        results.reshape(expert_count, per_peer, LATENT),
        ("expert", "context"),
        split_axis=0,
        concat_axis=0,
        tiled=True,
    ).reshape(expert_count * per_peer, LATENT)
    gate_kept = jnp.where(kept, gates.reshape(-1), 0.0).reshape(tok_count, TOPK)
    back_rows = returned[places].reshape(tok_count, TOPK, LATENT).astype(jnp.float32)
    mixture = jnp.sum(gate_kept[:, :, None] * back_rows, axis=1)
    return mixture.astype(jnp.bfloat16).reshape(1, tok_count, LATENT)


def shards(
    query_heads,
    key_heads,
    value_heads,
    latent,
    router,
    expert_in,
    expert_out,
    routes,
    segments,
    offsets,
    capacity,
):
    swap = [(0, 1), (1, 0)]
    place = lax.axis_index("context").astype(jnp.int32).reshape(1)

    def attention(half, doc_far, *keys_and_values, **order):
        return attend(
            half, place, query_heads[0], *keys_and_values, segments, doc_far, offsets, **order
        )

    if router.shape[1] <= DENSE_EXPERTS:
        attn_out, moe_out = dense_moe(
            latent,
            router,
            expert_in,
            expert_out,
            routes,
            segments,
            capacity,
            key_heads[0],
            value_heads[0],
            attention,
        )
    else:
        doc_far = lax.ppermute(segments, "context", swap)
        k_far = lax.ppermute(key_heads[0], "context", swap)
        v_far = lax.ppermute(value_heads[0], "context", swap)
        swapped = (key_heads[0], k_far, value_heads[0], v_far)
        attn_out = attention(1, doc_far, *swapped, before=attention(0, doc_far, *swapped))
        moe_out = routed_moe(latent, router, expert_in, expert_out, routes, capacity)
    return (attn_out[None], moe_out)


def solution(mesh):
    rows = P(("groups", "expert"), "context", None)
    placed = (
        rows,
        rows,
        rows,
        rows,
        P(),
        P(("expert", "context"), None, None),
        P(("expert", "context"), None, None),
        rows,
        P(("groups", "expert"), "context"),
        P(("groups", "expert"), "context"),
        P(),
    )
    return jax.shard_map(
        shards,
        mesh=mesh,
        in_specs=placed,
        out_specs=(rows, rows),
        check_vma=False,
    )
```

```python
import functools
import math

import jax
import jax.numpy as jnp
from jax import lax
from jax.experimental import pallas as pl
from jax.experimental.pallas import tpu as pltpu
from jax.sharding import PartitionSpec as P

HEAD_DIM = 128
LATENT = 1024
TOPK = 6
DENSE_EXPERTS = 16
EXPERT_VMEM = 26 * 1024 * 1024
FIRST_VMEM = 26 * 1024 * 1024
LOAD_VMEM = 44 * 1024 * 1024
ATTEND_VMEM = 8 * 1024 * 1024
SMALL_VMEM = 4 * 1024 * 1024
WINDOW = 4


def run_expert(rows_in, w_first, w_second):
    hidden = jax.nn.relu(jnp.dot(rows_in, w_first, preferred_element_type=jnp.float32))
    hidden = (hidden * hidden).astype(jnp.bfloat16)
    return jnp.dot(hidden, w_second, preferred_element_type=jnp.float32).astype(jnp.bfloat16)


def column_of(row):
    n = row.shape[1]
    square = jnp.broadcast_to(row.astype(jnp.float32), (n, n)).T
    return square[:, :1].astype(jnp.int32)


def attend_kernel(place_ref, q_ref, k_own, k_far, v_own, v_far, doc_own, doc_far, ahead_ref, *rest):
    out_ref = rest[-1]
    rows = q_ref.shape[0]
    heads = q_ref.shape[1] // HEAD_DIM
    here = place_ref[0] * rows
    there = (1 - place_ref[0]) * rows
    doc_query = column_of(doc_own[...])
    reach = here + lax.broadcasted_iota(jnp.int32, (rows, 1), 0) + column_of(ahead_ref[...])
    lane = lax.broadcasted_iota(jnp.int32, (1, rows), 1)
    doc_key = jnp.concatenate([doc_own[...], doc_far[...]], axis=1)
    spot = jnp.concatenate([here + lane, there + lane], axis=1)
    visible = (doc_key == doc_query) & (spot <= reach)
    scale = HEAD_DIM ** (-0.5) * math.log2(math.e)
    across = (((1,), (1,)), ((), ()))
    for head in range(heads):
        cols = slice(head * HEAD_DIM, (head + 1) * HEAD_DIM)
        keys = jnp.concatenate([k_own[:, cols], k_far[:, cols]], axis=0)
        values = jnp.concatenate([v_own[:, cols], v_far[:, cols]], axis=0)
        scores = lax.dot_general(q_ref[:, cols], keys, across, preferred_element_type=jnp.float32)
        scores = jnp.where(visible, scores * scale, -1e30)
        raw = jnp.exp2(scores - jnp.max(scores, axis=1, keepdims=True))
        share = 1.0 / jnp.sum(raw, axis=1, keepdims=True)
        mixed = jnp.dot(raw.astype(jnp.bfloat16), values, preferred_element_type=jnp.float32)
        out_ref[:, cols] = (mixed * share).astype(jnp.bfloat16)


def attend(half, place, q, k_own, k_far, v_own, v_far, doc_own, doc_far, ahead, before=None, after=()):
    rows, width = q.shape
    smem = pl.BlockSpec(memory_space=pltpu.SMEM)
    heads = pl.BlockSpec((rows, width // 2), lambda i: (0, half))
    line = pl.BlockSpec((1, rows), lambda i: (0, 0))
    extra = list(after) + ([] if before is None else [before])
    return pl.pallas_call(
        attend_kernel,
        grid=(1,),
        out_shape=jax.ShapeDtypeStruct(q.shape, jnp.bfloat16),
        in_specs=[smem] + [heads] * 5 + [line] * 3 + [pl.BlockSpec(memory_space=pl.ANY)] * len(extra),
        out_specs=heads,
        input_output_aliases={} if before is None else {8 + len(extra): 0},
        compiler_params=pltpu.CompilerParams(vmem_limit_bytes=ATTEND_VMEM),
        cost_estimate=pl.CostEstimate(
            flops=4 * rows * rows * width, bytes_accessed=6 * rows * width, transcendentals=0
        ),
    )(place, q, k_own, k_far, v_own, v_far, doc_own, doc_far, ahead, *extra)


def pack_kernel(named_any, doc_any, table_ref, named_ref, doc_ref, sems):
    loads = [
        pltpu.make_async_copy(named_any, named_ref, sems.at[0]),
        pltpu.make_async_copy(doc_any, doc_ref, sems.at[1]),
    ]
    for load in loads:
        load.start()
    for load in loads:
        load.wait()
    for k in range(TOPK):
        table_ref[0, k : k + 1, :] = named_ref[k]
    table_ref[0, TOPK : TOPK + 1, :] = doc_ref[...]
    table_ref[0, TOPK + 1 :, :] = doc_ref[...]


def pack(named, doc):
    anywhere = pl.BlockSpec(memory_space=pl.ANY)
    return pl.pallas_call(
        pack_kernel,
        out_shape=jax.ShapeDtypeStruct((1, 8, doc.shape[1]), jnp.int32),
        in_specs=[anywhere] * 2,
        out_specs=pl.BlockSpec(memory_space=pltpu.VMEM),
        scratch_shapes=[
            pltpu.VMEM(named.shape, jnp.int32),
            pltpu.VMEM(doc.shape, jnp.int32),
            pltpu.SemaphoreType.DMA((2,)),
        ],
        compiler_params=pltpu.CompilerParams(vmem_limit_bytes=SMALL_VMEM),
    )(named, doc)


def join_kernel(first_ref, second_ref, *refs):
    count = first_ref.shape[0]
    refs[-1][:count] = first_ref[...]
    refs[-1][count:] = second_ref[...]


def copy_join_kernel(first_ref, second_ref, rows_ref, *refs):
    join_kernel(first_ref, second_ref, refs[-1])
    refs[-2][...] = rows_ref[...]


def join(first, second, passed=None, after=(), copy=False):
    vmem = pl.BlockSpec(memory_space=pltpu.VMEM)
    anywhere = pl.BlockSpec(memory_space=pl.ANY)
    table = jax.ShapeDtypeStruct((2 * first.shape[0],) + first.shape[1:], first.dtype)
    through = [] if passed is None else [passed]
    place = vmem if copy else anywhere
    out = pl.pallas_call(
        copy_join_kernel if copy else join_kernel,
        out_shape=[jax.ShapeDtypeStruct(x.shape, x.dtype) for x in through] + [table],
        in_specs=[vmem] * 2 + [place] * len(through) + [anywhere] * len(after),
        out_specs=[place] * len(through) + [vmem],
        input_output_aliases={2: 0} if through and not copy else {},
        compiler_params=pltpu.CompilerParams(vmem_limit_bytes=SMALL_VMEM),
    )(first, second, *through, *after)
    return out if through else out[0]


def load_kernel(w1_any, w2_any, *refs):
    w1_ref, w2_ref, sems = refs[-3:]
    loads = []
    for index, (source, target) in enumerate(((w1_any, w1_ref), (w2_any, w2_ref))):
        rows = source.shape[0] // 2
        for half in range(2):
            part = pl.ds(half * rows, rows)
            loads.append(
                pltpu.make_async_copy(source.at[part], target.at[part], sems.at[2 * index + half])
            )
    for load in loads:
        load.start()
    for load in loads:
        load.wait()


def load_weights(w_first, w_second, after):
    hbm = pl.BlockSpec(memory_space=pltpu.HBM)
    anywhere = pl.BlockSpec(memory_space=pl.ANY)
    vmem = pl.BlockSpec(memory_space=pltpu.VMEM)
    return pl.pallas_call(
        load_kernel,
        out_shape=[pltpu.VMEM(w.shape, w.dtype) for w in (w_first, w_second)],
        in_specs=[hbm] * 2 + [anywhere] * len(after),
        out_specs=[vmem] * 2,
        scratch_shapes=[pltpu.SemaphoreType.DMA((4,))],
        compiler_params=pltpu.CompilerParams(vmem_limit_bytes=LOAD_VMEM),
    )(w_first, w_second, *after)


def behind_kernel(*refs):
    pass


def behind(x, after):
    anywhere = pl.BlockSpec(memory_space=pl.ANY)
    return pl.pallas_call(
        behind_kernel,
        out_shape=jax.ShapeDtypeStruct(x.shape, x.dtype),
        in_specs=[anywhere] * (1 + len(after)),
        out_specs=anywhere,
        input_output_aliases={0: 0},
        compiler_params=pltpu.CompilerParams(vmem_limit_bytes=SMALL_VMEM),
    )(x, *after)


def kept_kernel(own_ref, capacity_ref, low_ref, high_ref, *refs):
    out_ref = refs[-2]
    tables = (low_ref, high_ref)
    own = own_ref[0]
    z = own // 4
    rows = low_ref.shape[2]
    sources = 2 * low_ref.shape[0]
    line = sources // 4
    upto = lax.broadcasted_iota(jnp.int32, (rows, rows), 0) <= lax.broadcasted_iota(
        jnp.int32, (rows, rows), 1
    )
    upto = jnp.where(upto, 1.0, 0.0).astype(jnp.bfloat16)

    def device_of(entry):
        flips = 2 * lax.rem(entry, 2) + 4 * lax.rem(lax.div(entry, 2), line)
        return own ^ (flips + lax.div(entry, 2 * line))

    device = device_of(lax.broadcasted_iota(jnp.int32, (sources, sources), 0))
    other = device_of(lax.broadcasted_iota(jnp.int32, (sources, sources), 1))
    lower = jnp.where(other < device, 1.0, 0.0).astype(jnp.bfloat16)
    entry = lax.broadcasted_iota(jnp.int32, (sources, rows), 0)
    named = []
    for k in range(TOPK):
        named.append(jnp.concatenate([part[:, k, :] for part in tables], axis=0))
    kept = []
    for which in range(2):
        expert = own ^ which
        mine = named[0] == expert
        for k in range(1, TOPK):
            mine |= named[k] == expert
        flags = jnp.where(mine, 1.0, 0.0)
        running = jnp.dot(flags.astype(jnp.bfloat16), upto, preferred_element_type=jnp.float32)
        totals = jnp.broadcast_to(running[:, rows - 1 :], (sources, rows)).astype(jnp.bfloat16)
        before = jnp.dot(lower, totals, preferred_element_type=jnp.float32)
        slots = before + running - flags
        limit = capacity_ref[expert].astype(jnp.float32)
        kept.append(jnp.where(mine & (slots < limit), 1, 0))
    for step in range(line):
        home = 2 * (z ^ lax.rem(z + line - step, line))
        for side in range(2):
            here = entry == home + side
            for k, part in enumerate(named + kept):
                picked = jnp.sum(jnp.where(here, part, 0), axis=0, keepdims=True)
                out_ref[2 * step + side, k : k + 1, :] = picked


def kept_rows(own, capacity, low, high, passed, after):
    smem = pl.BlockSpec(memory_space=pltpu.SMEM)
    vmem = pl.BlockSpec(memory_space=pltpu.VMEM)
    anywhere = pl.BlockSpec(memory_space=pl.ANY)
    return pl.pallas_call(
        kept_kernel,
        out_shape=(
            jax.ShapeDtypeStruct(low.shape, jnp.int32),
            jax.ShapeDtypeStruct(passed.shape, passed.dtype),
        ),
        in_specs=[smem, smem, vmem, vmem] + [anywhere] * (1 + len(after)),
        out_specs=(vmem, anywhere),
        input_output_aliases={4: 1},
        compiler_params=pltpu.CompilerParams(vmem_limit_bytes=SMALL_VMEM),
    )(own, capacity, low, high, passed, *after)


def gate_columns(own, router_ref, x, kept):
    logits = lax.dot_general(
        router_ref[...], x, (((1,), (1,)), ((), ())), preferred_element_type=jnp.float32
    )
    number = lax.broadcasted_iota(jnp.int32, logits.shape, 0)
    named = number == kept[0:1]
    for k in range(1, TOPK):
        named |= number == kept[k : k + 1]
    sigma = jnp.where(named, jax.nn.sigmoid(logits), 0.0)
    gates = sigma / jnp.sum(sigma, axis=0, keepdims=True)
    lines = []
    for which in range(2):
        gate = jnp.sum(jnp.where(number == own ^ which, gates, 0.0), axis=0, keepdims=True)
        lines.append(jnp.where(kept[TOPK + which : TOPK + which + 1] > 0, gate, 0.0))
    square = jnp.concatenate(lines + [jnp.zeros((x.shape[0] - 2, x.shape[0]), jnp.float32)], axis=0)
    return square.T


def expert_kernel(place, first, own_ref, kept_ref, router_ref, xz_ref, xy_ref, *refs):
    step = 512
    if first:
        sources = refs[:4]
        z_ref, y_ref, *staged, hidden_ref, mixed_ref, sems = refs[-7:]
        weights = list(refs[:2]) + staged
    else:
        weights = refs[:4]
        z_ref, y_ref, hidden_ref, mixed_ref = refs[-4:]
    chunks = [(w, c) for w in (2, 3) for c in range(0, weights[w].shape[1], step)]

    def load(index):
        which, column = chunks[index]
        cols = pl.ds(column, step)
        return pltpu.make_async_copy(
            sources[which].at[:, cols], weights[which].at[:, cols], sems.at[index]
        )

    def ready(which, column):
        if first and which > 1:
            index = chunks.index((which, column))
            load(index).wait()
            if index + WINDOW < len(chunks):
                load(index + WINDOW).start()

    if first:
        for index in range(WINDOW):
            load(index).start()
    own = own_ref[0]
    rows = xz_ref.shape[0]
    x = jnp.concatenate([xz_ref[...], xy_ref[...]], axis=0)
    gates = [
        gate_columns(own, router_ref, x_ref[...], kept_ref[2 * place + side])
        for side, x_ref in enumerate((xz_ref, xy_ref))
    ]
    for which in range(2):
        gate = jnp.concatenate([g[:, which : which + 1] for g in gates], axis=0)
        w1_ref, w2_ref = weights[2 * which], weights[2 * which + 1]
        for column in range(0, w1_ref.shape[1], step):
            cols = slice(column, column + step)
            ready(2 * which, column)
            hidden = jnp.dot(x, w1_ref[:, cols], preferred_element_type=jnp.float32)
            hidden = jnp.maximum(hidden, 0.0)
            hidden_ref[which, :, cols] = (hidden * hidden).astype(jnp.bfloat16)
        for column in range(0, w2_ref.shape[1], step):
            cols = slice(column, column + step)
            ready(2 * which + 1, column)
            result = jnp.dot(hidden_ref[which], w2_ref[:, cols], preferred_element_type=jnp.float32)
            if which == 0:
                mixed_ref[:, cols] = result * gate
            else:
                mixed = (mixed_ref[:, cols] + result * gate).astype(jnp.bfloat16)
                z_ref[:, cols] = mixed[:rows]
                y_ref[:, cols] = mixed[rows:]


def run_piece(place, first, own, kept, router, from_line, from_side, weights, after):
    rows, width = from_line.shape
    hidden = weights[0].shape[1]
    smem = pl.BlockSpec(memory_space=pltpu.SMEM)
    vmem = pl.BlockSpec(memory_space=pltpu.VMEM)
    hbm = pl.BlockSpec(memory_space=pltpu.HBM)
    anywhere = pl.BlockSpec(memory_space=pl.ANY)
    piece = jax.ShapeDtypeStruct((rows, width), jnp.bfloat16)
    staged = [pltpu.VMEM(w.shape, w.dtype) for w in weights[2:]] if first else []
    scratch = [
        pltpu.VMEM((2, 2 * rows, hidden), jnp.bfloat16),
        pltpu.VMEM((2 * rows, width), jnp.float32),
    ]
    if first:
        scratch.append(pltpu.SemaphoreType.DMA(((hidden + width) // 512,)))
    return pl.pallas_call(
        functools.partial(expert_kernel, place, first),
        out_shape=[piece, piece] + staged,
        in_specs=[smem] + [vmem] * 6 + [hbm if first else vmem] * 2 + [anywhere] * len(after),
        out_specs=[vmem] * (2 + len(staged)),
        scratch_shapes=scratch,
        compiler_params=pltpu.CompilerParams(vmem_limit_bytes=FIRST_VMEM if first else EXPERT_VMEM),
        cost_estimate=pl.CostEstimate(
            flops=16 * rows * width * hidden,
            bytes_accessed=8 * rows * width,
            transcendentals=0,
        ),
    )(own, kept, router, from_line, from_side, *weights, *after)


def add_kernel(count, first_ref, second_ref, *refs):
    total = first_ref[...].astype(jnp.float32) + second_ref[...].astype(jnp.float32)
    outs = refs[len(refs) - count - 1 :]
    outs[-1][...] = total.astype(jnp.bfloat16)
    for index in range(count):
        outs[index][...] = refs[index][...]


def add(first, second, after=(), staged=()):
    vmem = pl.BlockSpec(memory_space=pltpu.VMEM)
    anywhere = pl.BlockSpec(memory_space=pl.ANY)
    out = pl.pallas_call(
        functools.partial(add_kernel, len(staged)),
        out_shape=[jax.ShapeDtypeStruct(x.shape, x.dtype) for x in staged]
        + [jax.ShapeDtypeStruct(first.shape, first.dtype)],
        in_specs=[vmem] * (2 + len(staged)) + [anywhere] * len(after),
        out_specs=[vmem] * (1 + len(staged)),
        compiler_params=pltpu.CompilerParams(vmem_limit_bytes=SMALL_VMEM),
        cost_estimate=pl.CostEstimate(flops=first.size, bytes_accessed=first.size, transcendentals=0),
    )(first, second, *staged, *after)
    return out if staged else out[0]


def dense_moe(latent, router, expert_in, expert_out, routes, segments, capacity, k_near, v_near, attention):
    f32 = jnp.float32
    line = router.shape[1] // 4
    spots = [(z, y) for z in range(line) for y in range(2)]
    sibling = [(0, 1), (1, 0)]
    across = [(2 * z + y, 2 * z + 1 - y) for z, y in spots]

    def swap_core(x):
        return lax.ppermute(x, "context", sibling)

    def swap_side(x):
        return lax.ppermute(x, "expert", across)

    def along(x, step):
        return lax.ppermute(x, "expert", [(2 * z + y, 2 * ((z + step) % line) + y) for z, y in spots])

    def flipped(x, span):
        return lax.ppermute(x, "expert", [(2 * z + y, 2 * (z ^ span) + y) for z, y in spots])

    own = lax.axis_index(("expert", "context")).astype(jnp.int32).reshape(1)
    far_weights = [swap_core(expert_in[0]), swap_core(expert_out[0])]

    arriving = along(latent[0], 1)
    table = pack(routes.transpose(2, 0, 1), segments)
    rows, table = join(table, swap_side(table), passed=latent[0], copy=True)
    beside_own = swap_side(rows)
    arriving, table = join(table, flipped(table, 1), passed=arriving)
    flip = flipped(table, 2)
    chained = along(arriving, 1)
    passed, table = join(table, flip, passed=arriving, copy=True, after=(beside_own,))
    far_table = swap_core(table)
    from_side = [beside_own, swap_side(passed)]
    own_weights = load_weights(expert_in[0], expert_out[0], (table,))
    kept, passed = kept_rows(own, capacity, table, far_table, chained, own_weights)
    doc_far = far_table[0, TOPK : TOPK + 1, :]
    from_line = [latent[0], arriving, passed]
    last = along(passed, 1)
    from_side.append(swap_side(passed))
    weights = list(own_weights) + far_weights

    def piece(step, weights, *after):
        return run_piece(
            step, step == 1, own, kept, router.T, from_line[step], from_side[step], weights, after
        )

    one, theirs, *weights[2:] = piece(1, weights)
    one_far = swap_side(theirs)
    last = behind(last, (one,))
    from_line.append(last)
    from_side.append(swap_side(last))
    two, theirs = piece(2, weights, one, from_line[3])
    two_far = swap_side(theirs)
    k_near, v_near, first = add(one, one_far, after=(two,), staged=(k_near, v_near))
    home = [along(first, line - 1)]
    three, theirs = piece(3, weights, two, first)
    three_far = swap_side(theirs)
    second = add(two, two_far, after=(three,))
    home.append(along(second, line - 2))
    near, theirs = piece(0, weights, three, second)
    near_far = swap_side(theirs)
    third = add(three, three_far, after=(near,))
    home.append(along(third, line - 3))
    swapped = (k_near, swap_core(k_near), v_near, swap_core(v_near))
    half = attention(0, doc_far, *swapped, after=(third,))
    attn_out = attention(1, doc_far, *swapped, before=half)
    total = near.astype(f32) + near_far.astype(f32)
    for part in home:
        total += part.astype(f32)
    return attn_out, total.astype(jnp.bfloat16)[None]


def routed_moe(latent, router, expert_in, expert_out, routes, capacity):
    tok_count = latent.shape[1]
    token_rows = latent[0]
    expert_count = router.shape[1]
    per_peer = max(2, 2 * tok_count * TOPK // expert_count)
    logits = jnp.dot(token_rows, router, preferred_element_type=jnp.float32)
    chosen_ids = routes[0]
    expert_ids = jnp.arange(expert_count, dtype=jnp.int32)
    one_hot = chosen_ids[:, :, None] == expert_ids[None, None, :]
    picked = jnp.sum(jnp.where(one_hot, logits[:, None, :], 0.0), axis=2)
    sigmas = jax.nn.sigmoid(picked)
    gates = sigmas / jnp.sum(sigmas, axis=1, keepdims=True)
    flat_hot = one_hot.reshape(tok_count * TOPK, expert_count).astype(jnp.int32)
    counts = jnp.sum(flat_hot, axis=0)
    ranks = jnp.sum((jnp.cumsum(flat_hot, axis=0) - flat_hot) * flat_hot, axis=1)
    count_rows = lax.all_gather(counts[None, :], ("expert", "context"), axis=0, tiled=True)
    own_index = lax.axis_index(("expert", "context"))
    lower_rows = jnp.arange(count_rows.shape[0], dtype=jnp.int32)[:, None] < own_index
    before = jnp.sum(jnp.where(lower_rows, count_rows, 0), axis=0)
    slots = jnp.sum(flat_hot * before[None, :], axis=1) + ranks
    limits = jnp.sum(flat_hot * capacity[None, :], axis=1)
    kept = slots < limits
    flat_ids = chosen_ids.reshape(-1)
    places = flat_ids * per_peer + ranks
    owners = jnp.arange(tok_count * TOPK, dtype=jnp.int32) // TOPK
    send_rows = (
        jnp.zeros((expert_count * per_peer, LATENT), jnp.bfloat16)
        .at[places]
        .set(token_rows[owners])
    )
    recv_rows = lax.all_to_all(
        send_rows.reshape(expert_count, per_peer, LATENT),
        ("expert", "context"),
        split_axis=0,
        concat_axis=0,
        tiled=True,
    ).reshape(expert_count * per_peer, LATENT)
    results = run_expert(recv_rows, expert_in[0], expert_out[0])
    returned = lax.all_to_all(
        results.reshape(expert_count, per_peer, LATENT),
        ("expert", "context"),
        split_axis=0,
        concat_axis=0,
        tiled=True,
    ).reshape(expert_count * per_peer, LATENT)
    gate_kept = jnp.where(kept, gates.reshape(-1), 0.0).reshape(tok_count, TOPK)
    back_rows = returned[places].reshape(tok_count, TOPK, LATENT).astype(jnp.float32)
    mixture = jnp.sum(gate_kept[:, :, None] * back_rows, axis=1)
    return mixture.astype(jnp.bfloat16).reshape(1, tok_count, LATENT)


def shards(
    query_heads,
    key_heads,
    value_heads,
    latent,
    router,
    expert_in,
    expert_out,
    routes,
    segments,
    offsets,
    capacity,
):
    swap = [(0, 1), (1, 0)]
    place = lax.axis_index("context").astype(jnp.int32).reshape(1)

    def attention(half, doc_far, *keys_and_values, **order):
        return attend(
            half, place, query_heads[0], *keys_and_values, segments, doc_far, offsets, **order
        )

    if router.shape[1] <= DENSE_EXPERTS:
        attn_out, moe_out = dense_moe(
            latent,
            router,
            expert_in,
            expert_out,
            routes,
            segments,
            capacity,
            key_heads[0],
            value_heads[0],
            attention,
        )
    else:
        doc_far = lax.ppermute(segments, "context", swap)
        k_far = lax.ppermute(key_heads[0], "context", swap)
        v_far = lax.ppermute(value_heads[0], "context", swap)
        swapped = (key_heads[0], k_far, value_heads[0], v_far)
        attn_out = attention(1, doc_far, *swapped, before=attention(0, doc_far, *swapped))
        moe_out = routed_moe(latent, router, expert_in, expert_out, routes, capacity)
    return (attn_out[None], moe_out)


def solution(mesh):
    rows = P(("groups", "expert"), "context", None)
    placed = (
        rows,
        rows,
        rows,
        rows,
        P(),
        P(("expert", "context"), None, None),
        P(("expert", "context"), None, None),
        rows,
        P(("groups", "expert"), "context"),
        P(("groups", "expert"), "context"),
        P(),
    )
    return jax.shard_map(
        shards,
        mesh=mesh,
        in_specs=placed,
        out_specs=(rows, rows),
        check_vma=False,
    )
```

```python
import functools
import math

import jax
import jax.numpy as jnp
from jax import lax
from jax.experimental import pallas as pl
from jax.experimental.pallas import tpu as pltpu
from jax.sharding import PartitionSpec as P

HEAD_DIM = 128
LATENT = 1024
TOPK = 6
DENSE_EXPERTS = 16
EXPERT_VMEM = 26 * 1024 * 1024
FIRST_VMEM = 26 * 1024 * 1024
LOAD_VMEM = 44 * 1024 * 1024
ATTEND_VMEM = 8 * 1024 * 1024
SMALL_VMEM = 4 * 1024 * 1024
WINDOW = 4


def run_expert(rows_in, w_first, w_second):
    hidden = jax.nn.relu(jnp.dot(rows_in, w_first, preferred_element_type=jnp.float32))
    hidden = (hidden * hidden).astype(jnp.bfloat16)
    return jnp.dot(hidden, w_second, preferred_element_type=jnp.float32).astype(jnp.bfloat16)


def column_of(row):
    n = row.shape[1]
    square = jnp.broadcast_to(row.astype(jnp.float32), (n, n)).T
    return square[:, :1].astype(jnp.int32)


def attend_kernel(place_ref, q_ref, k_own, k_far, v_own, v_far, doc_own, doc_far, ahead_ref, *rest):
    out_ref = rest[-1]
    rows = q_ref.shape[0]
    heads = q_ref.shape[1] // HEAD_DIM
    here = place_ref[0] * rows
    there = (1 - place_ref[0]) * rows
    doc_query = column_of(doc_own[...])
    reach = here + lax.broadcasted_iota(jnp.int32, (rows, 1), 0) + column_of(ahead_ref[...])
    lane = lax.broadcasted_iota(jnp.int32, (1, rows), 1)
    doc_key = jnp.concatenate([doc_own[...], doc_far[...]], axis=1)
    spot = jnp.concatenate([here + lane, there + lane], axis=1)
    visible = (doc_key == doc_query) & (spot <= reach)
    scale = HEAD_DIM ** (-0.5) * math.log2(math.e)
    across = (((1,), (1,)), ((), ()))
    for head in range(heads):
        cols = slice(head * HEAD_DIM, (head + 1) * HEAD_DIM)
        keys = jnp.concatenate([k_own[:, cols], k_far[:, cols]], axis=0)
        values = jnp.concatenate([v_own[:, cols], v_far[:, cols]], axis=0)
        scores = lax.dot_general(q_ref[:, cols], keys, across, preferred_element_type=jnp.float32)
        scores = jnp.where(visible, scores * scale, -1e30)
        raw = jnp.exp2(scores - jnp.max(scores, axis=1, keepdims=True))
        share = 1.0 / jnp.sum(raw, axis=1, keepdims=True)
        mixed = jnp.dot(raw.astype(jnp.bfloat16), values, preferred_element_type=jnp.float32)
        out_ref[:, cols] = (mixed * share).astype(jnp.bfloat16)


def attend(half, place, q, k_own, k_far, v_own, v_far, doc_own, doc_far, ahead, before=None, after=()):
    rows, width = q.shape
    smem = pl.BlockSpec(memory_space=pltpu.SMEM)
    heads = pl.BlockSpec((rows, width // 2), lambda i: (0, half))
    line = pl.BlockSpec((1, rows), lambda i: (0, 0))
    extra = list(after) + ([] if before is None else [before])
    return pl.pallas_call(
        attend_kernel,
        grid=(1,),
        out_shape=jax.ShapeDtypeStruct(q.shape, jnp.bfloat16),
        in_specs=[smem] + [heads] * 5 + [line] * 3 + [pl.BlockSpec(memory_space=pl.ANY)] * len(extra),
        out_specs=heads,
        input_output_aliases={} if before is None else {8 + len(extra): 0},
        compiler_params=pltpu.CompilerParams(vmem_limit_bytes=ATTEND_VMEM),
        cost_estimate=pl.CostEstimate(
            flops=4 * rows * rows * width, bytes_accessed=6 * rows * width, transcendentals=0
        ),
    )(place, q, k_own, k_far, v_own, v_far, doc_own, doc_far, ahead, *extra)


def pack_kernel(latent_any, named_any, rows_ref, table_ref, named_ref, sems):
    loads = [
        pltpu.make_async_copy(named_any, named_ref, sems.at[0]),
        pltpu.make_async_copy(latent_any, rows_ref, sems.at[1]),
    ]
    for load in loads:
        load.start()
    loads[0].wait()
    for k in range(TOPK):
        table_ref[0, k : k + 1, :] = named_ref[k]
    table_ref[0, TOPK:, :] = jnp.zeros((8 - TOPK, named_ref.shape[2]), jnp.int32)
    loads[1].wait()


def pack(latent, named):
    hbm = pl.BlockSpec(memory_space=pltpu.HBM)
    vmem = pl.BlockSpec(memory_space=pltpu.VMEM)
    return pl.pallas_call(
        pack_kernel,
        out_shape=[
            jax.ShapeDtypeStruct(latent.shape, latent.dtype),
            jax.ShapeDtypeStruct((1, 8, named.shape[2]), jnp.int32),
        ],
        in_specs=[hbm] * 2,
        out_specs=[vmem] * 2,
        scratch_shapes=[pltpu.VMEM(named.shape, jnp.int32), pltpu.SemaphoreType.DMA((2,))],
        compiler_params=pltpu.CompilerParams(vmem_limit_bytes=SMALL_VMEM),
    )(latent, named)


def join_kernel(first_ref, second_ref, *refs):
    count = first_ref.shape[0]
    refs[-1][:count] = first_ref[...]
    refs[-1][count:] = second_ref[...]


def copy_join_kernel(first_ref, second_ref, rows_ref, doc_ref, *refs):
    join_kernel(first_ref, second_ref, refs[-1])
    refs[-1][0, TOPK : TOPK + 1, :] = doc_ref[...]
    refs[-2][...] = rows_ref[...]


def join(first, second, passed=None, after=(), doc=None):
    vmem = pl.BlockSpec(memory_space=pltpu.VMEM)
    anywhere = pl.BlockSpec(memory_space=pl.ANY)
    table = jax.ShapeDtypeStruct((2 * first.shape[0],) + first.shape[1:], first.dtype)
    copy = doc is not None
    through = [] if passed is None else [passed]
    place = vmem if copy else anywhere
    extra = through + ([doc] if copy else [])
    out = pl.pallas_call(
        copy_join_kernel if copy else join_kernel,
        out_shape=[jax.ShapeDtypeStruct(x.shape, x.dtype) for x in through] + [table],
        in_specs=[vmem] * 2 + [place] * len(extra) + [anywhere] * len(after),
        out_specs=[place] * len(through) + [vmem],
        input_output_aliases={2: 0} if through and not copy else {},
        compiler_params=pltpu.CompilerParams(vmem_limit_bytes=SMALL_VMEM),
    )(first, second, *extra, *after)
    return out if through else out[0]


def load_kernel(w1_any, w2_any, *refs):
    w1_ref, w2_ref, sems = refs[-3:]
    loads = []
    for index, (source, target) in enumerate(((w1_any, w1_ref), (w2_any, w2_ref))):
        rows = source.shape[0] // 2
        for half in range(2):
            part = pl.ds(half * rows, rows)
            loads.append(
                pltpu.make_async_copy(source.at[part], target.at[part], sems.at[2 * index + half])
            )
    for load in loads:
        load.start()
    for load in loads:
        load.wait()


def load_weights(w_first, w_second, after):
    hbm = pl.BlockSpec(memory_space=pltpu.HBM)
    anywhere = pl.BlockSpec(memory_space=pl.ANY)
    vmem = pl.BlockSpec(memory_space=pltpu.VMEM)
    return pl.pallas_call(
        load_kernel,
        out_shape=[pltpu.VMEM(w.shape, w.dtype) for w in (w_first, w_second)],
        in_specs=[hbm] * 2 + [anywhere] * len(after),
        out_specs=[vmem] * 2,
        scratch_shapes=[pltpu.SemaphoreType.DMA((4,))],
        compiler_params=pltpu.CompilerParams(vmem_limit_bytes=LOAD_VMEM),
    )(w_first, w_second, *after)


def behind_kernel(*refs):
    pass


def behind(x, after):
    anywhere = pl.BlockSpec(memory_space=pl.ANY)
    return pl.pallas_call(
        behind_kernel,
        out_shape=jax.ShapeDtypeStruct(x.shape, x.dtype),
        in_specs=[anywhere] * (1 + len(after)),
        out_specs=anywhere,
        input_output_aliases={0: 0},
        compiler_params=pltpu.CompilerParams(vmem_limit_bytes=SMALL_VMEM),
    )(x, *after)


def kept_kernel(own_ref, capacity_ref, low_ref, high_ref, *refs):
    out_ref = refs[-2]
    tables = (low_ref, high_ref)
    own = own_ref[0]
    z = own // 4
    rows = low_ref.shape[2]
    sources = 2 * low_ref.shape[0]
    line = sources // 4
    upto = lax.broadcasted_iota(jnp.int32, (rows, rows), 0) <= lax.broadcasted_iota(
        jnp.int32, (rows, rows), 1
    )
    upto = jnp.where(upto, 1.0, 0.0).astype(jnp.bfloat16)

    def device_of(entry):
        flips = 2 * lax.rem(entry, 2) + 4 * lax.rem(lax.div(entry, 2), line)
        return own ^ (flips + lax.div(entry, 2 * line))

    device = device_of(lax.broadcasted_iota(jnp.int32, (sources, sources), 0))
    other = device_of(lax.broadcasted_iota(jnp.int32, (sources, sources), 1))
    lower = jnp.where(other < device, 1.0, 0.0).astype(jnp.bfloat16)
    entry = lax.broadcasted_iota(jnp.int32, (sources, rows), 0)
    named = []
    for k in range(TOPK):
        named.append(jnp.concatenate([part[:, k, :] for part in tables], axis=0))
    kept = []
    for which in range(2):
        expert = own ^ which
        mine = named[0] == expert
        for k in range(1, TOPK):
            mine |= named[k] == expert
        flags = jnp.where(mine, 1.0, 0.0)
        running = jnp.dot(flags.astype(jnp.bfloat16), upto, preferred_element_type=jnp.float32)
        totals = jnp.broadcast_to(running[:, rows - 1 :], (sources, rows)).astype(jnp.bfloat16)
        before = jnp.dot(lower, totals, preferred_element_type=jnp.float32)
        slots = before + running - flags
        limit = capacity_ref[expert].astype(jnp.float32)
        kept.append(jnp.where(mine & (slots < limit), 1, 0))
    for step in range(line):
        home = 2 * (z ^ lax.rem(z + line - step, line))
        for side in range(2):
            here = entry == home + side
            for k, part in enumerate(named + kept):
                picked = jnp.sum(jnp.where(here, part, 0), axis=0, keepdims=True)
                out_ref[2 * step + side, k : k + 1, :] = picked


def kept_rows(own, capacity, low, high, passed, after):
    smem = pl.BlockSpec(memory_space=pltpu.SMEM)
    vmem = pl.BlockSpec(memory_space=pltpu.VMEM)
    anywhere = pl.BlockSpec(memory_space=pl.ANY)
    return pl.pallas_call(
        kept_kernel,
        out_shape=(
            jax.ShapeDtypeStruct(low.shape, jnp.int32),
            jax.ShapeDtypeStruct(passed.shape, passed.dtype),
        ),
        in_specs=[smem, smem, vmem, vmem] + [anywhere] * (1 + len(after)),
        out_specs=(vmem, anywhere),
        input_output_aliases={4: 1},
        compiler_params=pltpu.CompilerParams(vmem_limit_bytes=SMALL_VMEM),
    )(own, capacity, low, high, passed, *after)


def gate_columns(own, router_ref, x, kept):
    logits = lax.dot_general(
        router_ref[...], x, (((1,), (1,)), ((), ())), preferred_element_type=jnp.float32
    )
    number = lax.broadcasted_iota(jnp.int32, logits.shape, 0)
    named = number == kept[0:1]
    for k in range(1, TOPK):
        named |= number == kept[k : k + 1]
    sigma = jnp.where(named, jax.nn.sigmoid(logits), 0.0)
    gates = sigma / jnp.sum(sigma, axis=0, keepdims=True)
    lines = []
    for which in range(2):
        gate = jnp.sum(jnp.where(number == own ^ which, gates, 0.0), axis=0, keepdims=True)
        lines.append(jnp.where(kept[TOPK + which : TOPK + which + 1] > 0, gate, 0.0))
    square = jnp.concatenate(lines + [jnp.zeros((x.shape[0] - 2, x.shape[0]), jnp.float32)], axis=0)
    return square.T


def expert_kernel(place, first, own_ref, kept_ref, router_ref, xz_ref, xy_ref, *refs):
    step = 512
    if first:
        sources = refs[:4]
        z_ref, y_ref, *staged, hidden_ref, mixed_ref, sems = refs[-7:]
        weights = list(refs[:2]) + staged
    else:
        weights = refs[:4]
        z_ref, y_ref, hidden_ref, mixed_ref = refs[-4:]
    chunks = [(w, c) for w in (2, 3) for c in range(0, weights[w].shape[1], step)]

    def load(index):
        which, column = chunks[index]
        cols = pl.ds(column, step)
        return pltpu.make_async_copy(
            sources[which].at[:, cols], weights[which].at[:, cols], sems.at[index]
        )

    def ready(which, column):
        if first and which == 1 and column == 0:
            for index in range(WINDOW, len(chunks)):
                load(index).start()
        if first and which > 1:
            load(chunks.index((which, column))).wait()

    if first:
        for index in range(WINDOW):
            load(index).start()
    own = own_ref[0]
    rows = xz_ref.shape[0]
    x = jnp.concatenate([xz_ref[...], xy_ref[...]], axis=0)
    gates = [
        gate_columns(own, router_ref, x_ref[...], kept_ref[2 * place + side])
        for side, x_ref in enumerate((xz_ref, xy_ref))
    ]
    for which in range(2):
        gate = jnp.concatenate([g[:, which : which + 1] for g in gates], axis=0)
        w1_ref, w2_ref = weights[2 * which], weights[2 * which + 1]
        for column in range(0, w1_ref.shape[1], step):
            cols = slice(column, column + step)
            ready(2 * which, column)
            hidden = jnp.dot(x, w1_ref[:, cols], preferred_element_type=jnp.float32)
            hidden = jnp.maximum(hidden, 0.0)
            hidden_ref[which, :, cols] = (hidden * hidden).astype(jnp.bfloat16)
        for column in range(0, w2_ref.shape[1], step):
            cols = slice(column, column + step)
            ready(2 * which + 1, column)
            result = jnp.dot(hidden_ref[which], w2_ref[:, cols], preferred_element_type=jnp.float32)
            if which == 0:
                mixed_ref[:, cols] = result * gate
            else:
                mixed = (mixed_ref[:, cols] + result * gate).astype(jnp.bfloat16)
                z_ref[:, cols] = mixed[:rows]
                y_ref[:, cols] = mixed[rows:]


def run_piece(place, first, own, kept, router, from_line, from_side, weights, after):
    rows, width = from_line.shape
    hidden = weights[0].shape[1]
    smem = pl.BlockSpec(memory_space=pltpu.SMEM)
    vmem = pl.BlockSpec(memory_space=pltpu.VMEM)
    hbm = pl.BlockSpec(memory_space=pltpu.HBM)
    anywhere = pl.BlockSpec(memory_space=pl.ANY)
    piece = jax.ShapeDtypeStruct((rows, width), jnp.bfloat16)
    staged = [pltpu.VMEM(w.shape, w.dtype) for w in weights[2:]] if first else []
    scratch = [
        pltpu.VMEM((2, 2 * rows, hidden), jnp.bfloat16),
        pltpu.VMEM((2 * rows, width), jnp.float32),
    ]
    if first:
        scratch.append(pltpu.SemaphoreType.DMA(((hidden + width) // 512,)))
    return pl.pallas_call(
        functools.partial(expert_kernel, place, first),
        out_shape=[piece, piece] + staged,
        in_specs=[smem] + [vmem] * 6 + [hbm if first else vmem] * 2 + [anywhere] * len(after),
        out_specs=[vmem] * (2 + len(staged)),
        scratch_shapes=scratch,
        compiler_params=pltpu.CompilerParams(vmem_limit_bytes=FIRST_VMEM if first else EXPERT_VMEM),
        cost_estimate=pl.CostEstimate(
            flops=16 * rows * width * hidden,
            bytes_accessed=8 * rows * width,
            transcendentals=0,
        ),
    )(own, kept, router, from_line, from_side, *weights, *after)


def add_kernel(count, first_ref, second_ref, *refs):
    total = first_ref[...].astype(jnp.float32) + second_ref[...].astype(jnp.float32)
    outs = refs[len(refs) - count - 1 :]
    outs[-1][...] = total.astype(jnp.bfloat16)
    for index in range(count):
        outs[index][...] = refs[index][...]


def add(first, second, after=(), staged=()):
    vmem = pl.BlockSpec(memory_space=pltpu.VMEM)
    anywhere = pl.BlockSpec(memory_space=pl.ANY)
    out = pl.pallas_call(
        functools.partial(add_kernel, len(staged)),
        out_shape=[jax.ShapeDtypeStruct(x.shape, x.dtype) for x in staged]
        + [jax.ShapeDtypeStruct(first.shape, first.dtype)],
        in_specs=[vmem] * (2 + len(staged)) + [anywhere] * len(after),
        out_specs=[vmem] * (1 + len(staged)),
        compiler_params=pltpu.CompilerParams(vmem_limit_bytes=SMALL_VMEM),
        cost_estimate=pl.CostEstimate(flops=first.size, bytes_accessed=first.size, transcendentals=0),
    )(first, second, *staged, *after)
    return out if staged else out[0]


def dense_moe(latent, router, expert_in, expert_out, routes, segments, capacity, k_near, v_near, attention):
    f32 = jnp.float32
    line = router.shape[1] // 4
    spots = [(z, y) for z in range(line) for y in range(2)]
    sibling = [(0, 1), (1, 0)]
    across = [(2 * z + y, 2 * z + 1 - y) for z, y in spots]

    def swap_core(x):
        return lax.ppermute(x, "context", sibling)

    def swap_side(x):
        return lax.ppermute(x, "expert", across)

    def along(x, step):
        return lax.ppermute(x, "expert", [(2 * z + y, 2 * ((z + step) % line) + y) for z, y in spots])

    def flipped(x, span):
        return lax.ppermute(x, "expert", [(2 * z + y, 2 * (z ^ span) + y) for z, y in spots])

    own = lax.axis_index(("expert", "context")).astype(jnp.int32).reshape(1)
    far_weights = [swap_core(expert_in[0]), swap_core(expert_out[0])]

    arriving = along(latent[0], 1)
    rows, table = pack(latent[0], routes.transpose(2, 0, 1))
    rows, table = join(table, swap_side(table), passed=rows)
    beside_own = swap_side(rows)
    arriving, table = join(table, flipped(table, 1), passed=arriving)
    flip = flipped(table, 2)
    chained = along(arriving, 1)
    passed, table = join(table, flip, passed=arriving, after=(beside_own,), doc=segments)
    far_table = swap_core(table)
    from_side = [beside_own, swap_side(passed)]
    own_weights = load_weights(expert_in[0], expert_out[0], (table,))
    kept, passed = kept_rows(own, capacity, table, far_table, chained, own_weights)
    doc_far = far_table[0, TOPK : TOPK + 1, :]
    from_line = [latent[0], arriving, passed]
    last = along(passed, 1)
    from_side.append(swap_side(passed))
    weights = list(own_weights) + far_weights

    def piece(step, weights, *after):
        return run_piece(
            step, step == 1, own, kept, router.T, from_line[step], from_side[step], weights, after
        )

    one, theirs, *weights[2:] = piece(1, weights)
    one_far = swap_side(theirs)
    last = behind(last, (one,))
    from_line.append(last)
    from_side.append(swap_side(last))
    two, theirs = piece(2, weights, one, from_line[3])
    two_far = swap_side(theirs)
    k_near, v_near, first = add(one, one_far, after=(two,), staged=(k_near, v_near))
    home = [along(first, line - 1)]
    three, theirs = piece(3, weights, two, first)
    three_far = swap_side(theirs)
    second = add(two, two_far, after=(three,))
    home.append(along(second, line - 2))
    near, theirs = piece(0, weights, three, second)
    near_far = swap_side(theirs)
    third = add(three, three_far, after=(near,))
    home.append(along(third, line - 3))
    swapped = (k_near, swap_core(k_near), v_near, swap_core(v_near))
    half = attention(0, doc_far, *swapped, after=(third,))
    attn_out = attention(1, doc_far, *swapped, before=half)
    total = near.astype(f32) + near_far.astype(f32)
    for part in home:
        total += part.astype(f32)
    return attn_out, total.astype(jnp.bfloat16)[None]


def routed_moe(latent, router, expert_in, expert_out, routes, capacity):
    tok_count = latent.shape[1]
    token_rows = latent[0]
    expert_count = router.shape[1]
    per_peer = max(2, 2 * tok_count * TOPK // expert_count)
    logits = jnp.dot(token_rows, router, preferred_element_type=jnp.float32)
    chosen_ids = routes[0]
    expert_ids = jnp.arange(expert_count, dtype=jnp.int32)
    one_hot = chosen_ids[:, :, None] == expert_ids[None, None, :]
    picked = jnp.sum(jnp.where(one_hot, logits[:, None, :], 0.0), axis=2)
    sigmas = jax.nn.sigmoid(picked)
    gates = sigmas / jnp.sum(sigmas, axis=1, keepdims=True)
    flat_hot = one_hot.reshape(tok_count * TOPK, expert_count).astype(jnp.int32)
    counts = jnp.sum(flat_hot, axis=0)
    ranks = jnp.sum((jnp.cumsum(flat_hot, axis=0) - flat_hot) * flat_hot, axis=1)
    count_rows = lax.all_gather(counts[None, :], ("expert", "context"), axis=0, tiled=True)
    own_index = lax.axis_index(("expert", "context"))
    lower_rows = jnp.arange(count_rows.shape[0], dtype=jnp.int32)[:, None] < own_index
    before = jnp.sum(jnp.where(lower_rows, count_rows, 0), axis=0)
    slots = jnp.sum(flat_hot * before[None, :], axis=1) + ranks
    limits = jnp.sum(flat_hot * capacity[None, :], axis=1)
    kept = slots < limits
    flat_ids = chosen_ids.reshape(-1)
    places = flat_ids * per_peer + ranks
    owners = jnp.arange(tok_count * TOPK, dtype=jnp.int32) // TOPK
    send_rows = (
        jnp.zeros((expert_count * per_peer, LATENT), jnp.bfloat16)
        .at[places]
        .set(token_rows[owners])
    )
    recv_rows = lax.all_to_all(
        send_rows.reshape(expert_count, per_peer, LATENT),
        ("expert", "context"),
        split_axis=0,
        concat_axis=0,
        tiled=True,
    ).reshape(expert_count * per_peer, LATENT)
    results = run_expert(recv_rows, expert_in[0], expert_out[0])
    returned = lax.all_to_all(
        results.reshape(expert_count, per_peer, LATENT),
        ("expert", "context"),
        split_axis=0,
        concat_axis=0,
        tiled=True,
    ).reshape(expert_count * per_peer, LATENT)
    gate_kept = jnp.where(kept, gates.reshape(-1), 0.0).reshape(tok_count, TOPK)
    back_rows = returned[places].reshape(tok_count, TOPK, LATENT).astype(jnp.float32)
    mixture = jnp.sum(gate_kept[:, :, None] * back_rows, axis=1)
    return mixture.astype(jnp.bfloat16).reshape(1, tok_count, LATENT)


def shards(
    query_heads,
    key_heads,
    value_heads,
    latent,
    router,
    expert_in,
    expert_out,
    routes,
    segments,
    offsets,
    capacity,
):
    swap = [(0, 1), (1, 0)]
    place = lax.axis_index("context").astype(jnp.int32).reshape(1)

    def attention(half, doc_far, *keys_and_values, **order):
        return attend(
            half, place, query_heads[0], *keys_and_values, segments, doc_far, offsets, **order
        )

    if router.shape[1] <= DENSE_EXPERTS:
        attn_out, moe_out = dense_moe(
            latent,
            router,
            expert_in,
            expert_out,
            routes,
            segments,
            capacity,
            key_heads[0],
            value_heads[0],
            attention,
        )
    else:
        doc_far = lax.ppermute(segments, "context", swap)
        k_far = lax.ppermute(key_heads[0], "context", swap)
        v_far = lax.ppermute(value_heads[0], "context", swap)
        swapped = (key_heads[0], k_far, value_heads[0], v_far)
        attn_out = attention(1, doc_far, *swapped, before=attention(0, doc_far, *swapped))
        moe_out = routed_moe(latent, router, expert_in, expert_out, routes, capacity)
    return (attn_out[None], moe_out)


def solution(mesh):
    rows = P(("groups", "expert"), "context", None)
    placed = (
        rows,
        rows,
        rows,
        rows,
        P(),
        P(("expert", "context"), None, None),
        P(("expert", "context"), None, None),
        rows,
        P(("groups", "expert"), "context"),
        P(("groups", "expert"), "context"),
        P(),
    )
    return jax.shard_map(
        shards,
        mesh=mesh,
        in_specs=placed,
        out_specs=(rows, rows),
        check_vma=False,
    )
```
